256 devices in a mesh: passage: 32 (over x_lo, z, core), span: 4 (over y), radial: 2 (over x_hi).
Axes of the slice: x: 4 (x_hi: 2, x_lo: 2; x = x_hi * 2 + x_lo), y: 4, z: 8, core: 2. Of those that a mesh axis runs over, the one named last changes fastest.
Arguments:
- right_side: float32 [1024, 320], P(('passage', 'span', 'radial'))
- mass: float32 [1024, 320], P(('passage', 'span', 'radial')), may hold values from 1 to 4
- volume_jac: float32 [1024, 3, 5, 5], P(('passage', 'span', 'radial')), may hold values from -0.6 to 0.6
- face_flux: float32 [1024, 6, 5, 5], P(('passage', 'span', 'radial')), may hold values from -1.2 to 1.2
- face_visc: float32 [1024, 6, 5, 5], P(('passage', 'span', 'radial')), may hold values from -0.3 to 0.3
- block_inverse: bfloat16 [1024, 320, 320], P(('passage', 'span', 'radial'))
- coarse_inverse: float32 [32, 2, 160, 160], P('passage', 'radial')
- neighbours: int32 [1024, 6], P(('passage', 'span', 'radial')), may hold values from 0 to 1023, as said below
- orientation: int32 [1024, 6], P(('passage', 'span', 'radial')), may hold values from 0 to 7
- bc_tags: int32 [1024, 6], P(('passage', 'span', 'radial')), may hold values from 0 to 2, as said below
- coarse_group: int32 [1024], P(('passage', 'span', 'radial')), may hold values from 0 to 3
Outputs:
- update: float32 [1024, 320], P(('passage', 'span', 'radial'))
- lin_residual: float32 [1024, 320], P(('passage', 'span', 'radial'))
The draws below stay inside these ranges and needn't reach their ends.
Inputs may be any that keep to these rules, and one draw needn't show every extreme that they name: `neighbours`: the elements form a structured grid of (1 * passage devices) x (1 * span devices) x (4 * radial devices), periodic along the passage direction; each device holds one 1 x 1 x 4 block of it, in an order of its own. The element across face f touches through its face f xor 1 and lies on the same device or on the next device along direction f // 2. Where bc_tags is not 0 the entry is the element itself. `bc_tags`: 0 on interior faces (periodic ones too), 1 for a slip wall, 2 for far field; not 0 exactly on the faces at the two ends of the span and radial directions of the grid.
All inputs are finite; a program needn't handle non-finite values.
Results may differ from the reference program's by a relative error of at most 0.0068.
Values sent between devices are 32-bit elements; how exact they have to be, the bound alone decides.
No kernel may reach another device: no remote copies, remote signals or barrier semaphores. Data moves between devices by JAX's collectives and lax.ppermute only.
A program may use at most 128 MiB of HBM per device.

```python
import math
import jax
import jax.numpy as jnp
import numpy as np
from jax import lax

QN = 4
VARS = 5
ITERS = 3
CG = 4
EX = 1
EY = 1
EZ = 4
ELEMS = 4
NE = 1024
ROWS = 320
KC = 160
N_PASSAGE = 32
N_SPAN = 4
N_RADIAL = 2
DEVICES = 256


def grid_layout(key):
    keys = jax.random.split(jax.random.fold_in(key, 90), DEVICES)
    return jax.vmap(lambda one_key: jax.random.permutation(one_key, ELEMS))(keys).astype(jnp.int32)


def grid_links(orders):
    device = jnp.arange(DEVICES, dtype=jnp.int32)[:, None]
    slots = jnp.arange(ELEMS, dtype=jnp.int32)[None, :]
    coords = [device // (N_SPAN * N_RADIAL) * EX + slots // (EY * EZ), device // N_RADIAL % N_SPAN * EY + slots // EZ % EY, device % N_RADIAL * EZ + slots % EZ]
    extents = (EX * N_PASSAGE, EY * N_SPAN, EZ * N_RADIAL)
    own_id = device * ELEMS + orders[device, slots]
    links = []
    edges = []
    for face_id in range(6):
        axis_pos = face_id // 2
        offset = -1 if face_id % 2 == 0 else 1
        moved = list(coords)
        target = coords[axis_pos] + offset
        if axis_pos == 0:
            edge = jnp.zeros(own_id.shape, jnp.bool_)
            target = target % extents[0]
        else:
            edge = (target < 0) | (target >= extents[axis_pos])
            target = jnp.clip(target, 0, extents[axis_pos] - 1)
        moved[axis_pos] = target
        owner = (moved[0] // EX * N_SPAN + moved[1] // EY) * N_RADIAL + moved[2] // EZ
        owner = owner + jnp.zeros_like(own_id)
        spot = (moved[0] % EX * EY + moved[1] % EY) * EZ + moved[2] % EZ
        spot = spot + jnp.zeros_like(own_id)
        links.append(jnp.where(edge, own_id, owner * ELEMS + orders[owner, spot]))
        edges.append(edge)
    return (jnp.stack(links, -1), jnp.stack(edges, -1))


def by_element(orders, values):
    inverse = jnp.argsort(orders, axis=1, stable=True)
    return jnp.take_along_axis(values, inverse[:, :, None], axis=1).reshape(NE, 6)


def draw_neighbours(key, part):
    orders = grid_layout(key)
    links, edges = grid_links(orders)
    return by_element(orders, links).astype(jnp.int32)


def draw_bc_tags(key, part):
    orders = grid_layout(key)
    key = jax.random.fold_in(key, 22)
    links, edges = grid_links(orders)
    kinds = jax.random.randint(key, (DEVICES, ELEMS, 6), 1, 3)
    return by_element(orders, jnp.where(edges, kinds, 0)).astype(jnp.int32)


def draw_right_side(key, part):
    key = jax.random.fold_in(key, 11)
    first_key, second_key = jax.random.split(key)
    rising = jnp.exp(math.log(3.0) * jnp.arange(NE, dtype=jnp.float32) / NE)[:, None]
    scales = jnp.exp(jax.random.uniform(second_key, (NE, 1), jnp.float32, 0.0, math.log(4.0))) * rising
    base = jax.random.normal(first_key, (NE, ROWS), jnp.float32)
    return base * scales


def draw_block_inverse(key, part):
    key = jax.random.fold_in(key, 12)
    first_key, second_key = jax.random.split(key)
    diagonal = jnp.exp(jax.random.uniform(first_key, (NE, ROWS), jnp.float32, math.log(0.12), math.log(0.5)))
    spread = jax.random.normal(second_key, (NE, ROWS, ROWS), jnp.float32)
    result = spread * (0.1 / math.sqrt(ROWS)) + diagonal[:, :, None] * jnp.eye(ROWS, dtype=jnp.float32)[None]
    return result.astype(jnp.bfloat16)


def draw_coarse_inverse(key, part):
    key = jax.random.fold_in(key, 13)
    first_key, second_key = jax.random.split(key)
    shape_lead = (N_PASSAGE, N_RADIAL, KC)
    diagonal = jnp.exp(jax.random.uniform(first_key, shape_lead, jnp.float32, math.log(0.005), math.log(0.02)))
    spread = jax.random.normal(second_key, (N_PASSAGE, N_RADIAL, KC, KC), jnp.float32)
    return spread * (0.004 / math.sqrt(KC)) + diagonal[..., None] * jnp.eye(KC, dtype=jnp.float32)


def touch_ends(entries, key, least, high):
    longest = entries.shape.index(max(entries.shape))
    spots = []
    for shift in (0, 1):
        where = [jax.random.randint(jax.random.fold_in(key, axis), (), 0, length) for axis, length in enumerate(entries.shape)]
        where[longest] = (where[longest] + shift) % entries.shape[longest]
        spots.append(tuple(where))
    return entries.at[spots[0]].set(least).at[spots[1]].set(high)


def level_of(own_key, extent, cuts, least, high):
    def one(dim, parts):
        draws = jax.random.uniform(jax.random.fold_in(jax.random.fold_in(own_key, 6), dim), (parts,), jnp.float32, least / len(cuts), high / len(cuts))
        return jnp.repeat(jnp.exp(draws), extent[dim] // parts).reshape((-1,) + (1,) * (len(extent) - dim - 1))

    factor_of = one(*cuts[0])
    for cut in cuts[1:]:
        factor_of = factor_of * one(*cut)
    return factor_of


def noise(rng, extent, deviation, reach, shards=(), held_as=jnp.bfloat16):
    values = deviation * jax.random.normal(rng, extent, jnp.float32)
    if shards:
        values = values * level_of(rng, extent, shards, -0.22, 0.18)
    return jnp.clip(values, -reach, reach).astype(held_as)


def setup_inputs(seed: int = 0) -> dict:
    key_of = jax.random.split(jax.random.key(seed), 12)
    return {
        "right_side": draw_right_side(jax.random.fold_in(key_of[11], 71), 0),
        "mass": jnp.clip(jnp.exp(math.log(4.0) - 1.3862944 * jax.random.uniform(key_of[1], (NE, ROWS), jnp.float32) ** level_of(key_of[1], (NE, ROWS), ((0, 256),), -0.2, 0.2)), 1.0, 4.0),
        "volume_jac": noise(key_of[2], (NE, 3, VARS, VARS), 0.1, 0.6, ((0, 256),), jnp.float32),
        "face_flux": noise(key_of[3], (NE, 6, VARS, VARS), 0.2, 1.2, ((0, 256),), jnp.float32),
        "face_visc": noise(key_of[4], (NE, 6, VARS, VARS), 0.05, 0.3, ((0, 256),), jnp.float32),
        "block_inverse": draw_block_inverse(jax.random.fold_in(key_of[11], 71), 0),
        "coarse_inverse": draw_coarse_inverse(jax.random.fold_in(key_of[11], 71), 0),
        "neighbours": draw_neighbours(jax.random.fold_in(key_of[11], 71), 0),
        "orientation": touch_ends(jax.random.randint(key_of[8], (NE, 6), 0, 8), jax.random.fold_in(key_of[8], 1), 0, 7).astype(jnp.int32),
        "bc_tags": draw_bc_tags(jax.random.fold_in(key_of[11], 71), 0),
        "coarse_group": touch_ends(jax.random.randint(key_of[10], (NE,), 0, CG), jax.random.fold_in(key_of[10], 1), 0, CG - 1).astype(jnp.int32),
    }


HIGHEST = lax.Precision.HIGHEST
FORMS = ('pq,nvqbc->nvpbc', 'pq,nvaqc->nvapc', 'pq,nvabq->nvabp')

def lobatto_nodes(node_count):
    if node_count == 2:
        return np.array([-1.0, 1.0])
    if node_count == 3:
        return np.array([-1.0, 0.0, 1.0])
    inner_node = 1.0 / math.sqrt(5.0)
    return np.array([-1.0, -inner_node, inner_node, 1.0])

def derivative_table(node_count):
    nodes = lobatto_nodes(node_count)
    weights = np.ones(node_count)
    for row_id in range(node_count):
        for col_id in range(node_count):
            if col_id != row_id:
                weights[row_id] = weights[row_id] / (nodes[row_id] - nodes[col_id])
    result = np.zeros((node_count, node_count))
    for row_id in range(node_count):
        for col_id in range(node_count):
            if col_id != row_id:
                result[row_id, col_id] = weights[col_id] / weights[row_id] / (nodes[row_id] - nodes[col_id])
        result[row_id, row_id] = -np.sum(result[row_id])
    return result

def vertex_table(node_count):
    nodes = lobatto_nodes(node_count)
    shapes = np.stack([(1.0 - nodes) / 2.0, (1.0 + nodes) / 2.0])
    first_part = shapes[:, None, None, :, None, None]
    second_part = shapes[None, :, None, None, :, None]
    third_part = shapes[None, None, :, None, None, :]
    return (first_part * second_part * third_part).reshape(8, node_count ** 3)

def face_values(state_block, face_id, deriv_table):
    axis_pos = face_id // 2
    layer_index = 0 if face_id % 2 == 0 else QN - 1
    moved = jnp.moveaxis(state_block, 2 + axis_pos, 2)
    row_weights = jnp.asarray(deriv_table[layer_index], jnp.float32)
    normal = jnp.einsum('q,nvqij->nvij', row_weights, moved, precision=HIGHEST)
    return (moved[:, :, layer_index], normal)

def orient(values, codes):
    result = jnp.zeros_like(values)
    for code_value in range(8):
        variant = values
        if code_value & 4:
            variant = jnp.swapaxes(variant, 2, 3)
        if code_value & 2:
            variant = jnp.flip(variant, 2)
        if code_value & 1:
            variant = jnp.flip(variant, 3)
        chosen = (codes == code_value)[:, None, None, None]
        result = result + jnp.where(chosen, variant, jnp.zeros_like(variant))
    return result

def face_input(near_trace, near_normal, own_trace, own_normal, tags, axis_pos):
    sign_table = np.ones((1, VARS, 1, 1))
    sign_table[0, 1 + axis_pos] = -1.0
    signs = jnp.asarray(sign_table, jnp.float32)
    interior = (tags == 0)[:, None, None, None]
    wall = (tags == 1)[:, None, None, None]
    zeros = jnp.zeros_like(own_trace)
    trace = jnp.where(interior, near_trace, jnp.where(wall, signs * own_trace, zeros))
    normal = jnp.where(interior, near_normal, jnp.where(wall, -signs * own_normal, zeros))
    return (trace, normal)

def face_contribution(trace, normal, flux, viscous, face_id):
    axis_pos = face_id // 2
    layer_index = 0 if face_id % 2 == 0 else QN - 1
    term = jnp.einsum('nuv,nvij->nuij', flux, trace, precision=HIGHEST)
    term = term + jnp.einsum('nuv,nvij->nuij', viscous, normal, precision=HIGHEST)
    onehot = (jnp.arange(QN, dtype=jnp.int32) == layer_index).astype(jnp.float32)
    placed = -term[:, :, None] * onehot[None, None, :, None, None]
    return jnp.moveaxis(placed, 2, 2 + axis_pos)

def volume_part(state_block, mass_block, volume_jac, dmat):
    result = 1.5 * mass_block * state_block
    for axis_pos in range(3):
        slope = jnp.einsum(FORMS[axis_pos], dmat, state_block, precision=HIGHEST)
        result = result + jnp.einsum('nuv,nvabc->nuabc', volume_jac[:, axis_pos], slope, precision=HIGHEST)
    return result

def least_squares(hess, beta):
    matrix = [list(row_vals) for row_vals in hess]
    target = [beta] + [jnp.zeros((), jnp.float32) for row_id in range(ITERS)]
    for column_id in range(ITERS):
        top_val = matrix[column_id][column_id]
        low_val = matrix[column_id + 1][column_id]
        radius = jnp.sqrt(top_val * top_val + low_val * low_val)
        cosine = top_val / radius
        sine_val = low_val / radius
        for later in range(column_id, ITERS):
            upper = matrix[column_id][later]
            lower = matrix[column_id + 1][later]
            matrix[column_id][later] = cosine * upper + sine_val * lower
            matrix[column_id + 1][later] = -sine_val * upper + cosine * lower
        upper = target[column_id]
        lower = target[column_id + 1]
        target[column_id] = cosine * upper + sine_val * lower
        target[column_id + 1] = -sine_val * upper + cosine * lower
    weights = [None] * ITERS
    for column_id in reversed(range(ITERS)):
        value = target[column_id]
        for later in range(column_id + 1, ITERS):
            value = value - matrix[column_id][later] * weights[later]
        weights[column_id] = value / matrix[column_id][column_id]
    return weights

def apply_operator(vector, mass, volume_jac, face_flux, face_visc, neighbours, orientation, bc_tags):
    elem_count = vector.shape[0]
    deriv_table = derivative_table(QN)
    dmat = jnp.asarray(deriv_table, jnp.float32)
    block_shape = (elem_count, VARS, QN, QN, QN)
    state_block = vector.reshape(block_shape)
    result = volume_part(state_block, mass.reshape(block_shape), volume_jac, dmat)
    for face_id in range(6):
        other_trace, other_normal = face_values(state_block, face_id ^ 1, deriv_table)
        picked = neighbours[:, face_id]
        near_trace = orient(other_trace[picked], orientation[:, face_id])
        near_normal = orient(other_normal[picked], orientation[:, face_id])
        own_trace, own_normal = face_values(state_block, face_id, deriv_table)
        trace, normal = face_input(near_trace, near_normal, own_trace, own_normal, bc_tags[:, face_id], face_id // 2)
        result = result + face_contribution(trace, normal, face_flux[:, face_id], face_visc[:, face_id], face_id)
    return result.reshape(elem_count, ROWS)

def apply_blocks(block_inverse, low):
    groups = low.shape[0] // ELEMS
    pairs = (block_inverse.reshape(groups, ELEMS, ROWS, ROWS), low.reshape(groups, ELEMS, ROWS))

    def one_group(pair):
        return jnp.einsum('nij,nj->ni', pair[0].astype(jnp.float32), pair[1].astype(jnp.float32), precision=HIGHEST)
    return lax.map(one_group, pairs).reshape(low.shape[0], ROWS)

def coarse_correct(vector, coarse_inverse, coarse_group):
    rtable = jnp.asarray(vertex_table(QN), jnp.float32)
    modes = jnp.einsum('mk,nvk->nvm', rtable, vector.reshape(NE, VARS, QN ** 3), precision=HIGHEST)
    modes = modes.reshape(NE, VARS * 8)
    device = jnp.arange(NE, dtype=jnp.int32) // ELEMS
    passage_idx = device // (N_SPAN * N_RADIAL)
    radial_idx = device % N_RADIAL
    segment = (passage_idx * N_RADIAL + radial_idx) * CG + coarse_group
    gathered = jax.ops.segment_sum(modes, segment, num_segments=N_PASSAGE * N_RADIAL * CG)
    coarse = gathered.reshape(N_PASSAGE, N_RADIAL, KC)
    solved = jnp.einsum('prij,prj->pri', coarse_inverse, coarse, precision=HIGHEST).reshape(N_PASSAGE * N_RADIAL * CG, VARS * 8)
    spread = solved[segment].reshape(NE, VARS, 8)
    return jnp.einsum('mk,nvm->nvk', rtable, spread, precision=HIGHEST).reshape(NE, ROWS)

def reference(right_side, mass, volume_jac, face_flux, face_visc, block_inverse, coarse_inverse, neighbours, orientation, bc_tags, coarse_group):

    def operate(vector):
        return apply_operator(vector, mass, volume_jac, face_flux, face_visc, neighbours, orientation, bc_tags)

    def precondition(vector):
        first = apply_blocks(block_inverse, vector.astype(jnp.bfloat16)) + coarse_correct(vector, coarse_inverse, coarse_group)
        defect = (vector - operate(first)).astype(jnp.bfloat16)
        return first + apply_blocks(block_inverse, defect)
    beta = jnp.sqrt(jnp.sum(right_side * right_side))
    basis = [right_side / beta]
    search = []
    hess = [[jnp.zeros((), jnp.float32) for column_id in range(ITERS)] for row_id in range(ITERS + 1)]
    for column_id in range(ITERS):
        direction = precondition(basis[column_id])
        search.append(direction)
        mapped = operate(direction)
        coeffs = [jnp.sum(mapped * basis[row_id]) for row_id in range(column_id + 1)]
        for row_id in range(column_id + 1):
            hess[row_id][column_id] = coeffs[row_id]
            mapped = mapped - coeffs[row_id] * basis[row_id]
        height = jnp.sqrt(jnp.sum(mapped * mapped))
        hess[column_id + 1][column_id] = height
        basis.append(mapped / height)
    weights = least_squares(hess, beta)
    update = weights[0] * search[0]
    for column_id in range(1, ITERS):
        update = update + weights[column_id] * search[column_id]
    return (update, right_side - operate(update))
```

```python
import math

import jax
import jax.numpy as jnp
import numpy as np
from jax import lax
from jax.experimental import pallas as pl
from jax.experimental.pallas import tpu as pltpu
from jax.sharding import PartitionSpec as P

QN = 4
VARS = 5
CG = 4
ELEMS = 4
NODES = QN**3
ROWS = 320
KC = 160
STRIDE = 8
RW = ELEMS * STRIDE
FACE = QN * QN
SOURCES = 9
WIDE = 256
SCALAR0 = KC
AXES = ("passage", "span", "radial")
HIGHEST = lax.Precision.HIGHEST
F32 = jnp.float32


def lobatto_nodes():
    inner_node = 1.0 / math.sqrt(5.0)
    return np.array([-1.0, -inner_node, inner_node, 1.0])


def derivative_table():
    nodes = lobatto_nodes()
    weights = np.ones(QN)
    for row_id in range(QN):
        for col_id in range(QN):
            if col_id != row_id:
                weights[row_id] = weights[row_id] / (nodes[row_id] - nodes[col_id])
    result = np.zeros((QN, QN))
    for row_id in range(QN):
        for col_id in range(QN):
            if col_id != row_id:
                result[row_id, col_id] = (
                    weights[col_id] / weights[row_id] / (nodes[row_id] - nodes[col_id])
                )
        result[row_id, row_id] = -np.sum(result[row_id])
    return result


def vertex_table():
    nodes = lobatto_nodes()
    shapes = np.stack([(1.0 - nodes) / 2.0, (1.0 + nodes) / 2.0])
    first_part = shapes[:, None, None, :, None, None]
    second_part = shapes[None, :, None, None, :, None]
    third_part = shapes[None, None, :, None, None, :]
    return (first_part * second_part * third_part).reshape(8, NODES)


def coords(node):
    return (node // 16, node // 4 % 4, node % 4)


def others(node, axis):
    picked = [c for i, c in enumerate(coords(node)) if i != axis]
    return picked[0] * QN + picked[1]


def layer_of(face):
    return 0 if face % 2 == 0 else QN - 1


def tables():
    dmat = derivative_table()
    de = np.zeros((NODES, 3 * NODES + 6 * 2 * FACE), np.float32)
    place = np.zeros((6, 8, FACE, NODES), np.float32)
    for node in range(NODES):
        for axis in range(3):
            for target in range(NODES):
                if others(node, axis) == others(target, axis):
                    de[node, axis * NODES + target] = dmat[
                        coords(target)[axis], coords(node)[axis]
                    ]
        for face in range(6):
            axis = face // 2
            spot = others(node, axis)
            base = 3 * NODES + face * 2 * FACE
            de[node, base + FACE + spot] = dmat[layer_of(face), coords(node)[axis]]
            if coords(node)[axis] == layer_of(face):
                de[node, base + spot] = 1.0
                place[face, :, spot, node] = 1.0
    turn = np.zeros((FACE, 8, FACE), np.float32)
    for code in range(8):
        for i in range(QN):
            for j in range(QN):
                a = QN - 1 - i if code & 2 else i
                b = QN - 1 - j if code & 1 else j
                if code & 4:
                    a, b = b, a
                turn[a * QN + b, code, i * QN + j] = 1.0
    rtab = vertex_table().astype(np.float32)
    restrict = np.zeros((NODES, WIDE), np.float32)
    restrict[:, :KC] = np.tile(rtab.T, (1, CG * VARS))
    spread = np.ascontiguousarray(restrict.T)
    own_lanes = np.zeros((RW, ROWS), np.float32)
    for row in range(RW):
        v = row % STRIDE
        if v < VARS:
            own_lanes[row, v * NODES : (v + 1) * NODES] = 1.0
    cols = SOURCES * 2 * RW
    tile = np.zeros((16, cols), np.float32)
    colcode = np.zeros((8, cols), np.float32)
    for col in range(cols):
        source, kind, n, v = col // (2 * RW), col // RW % 2, col // STRIDE % ELEMS, col % STRIDE
        if v < VARS:
            tile[kind * 8 + v, col] = 1.0
        colcode[0, col] = source * ELEMS + n
        for axis in range(3):
            colcode[1 + axis, col] = (-1.0 if v == 1 + axis else 1.0) * (-1.0 if kind else 1.0)
    vtile = np.zeros((24, 3 * RW), np.float32)
    vmask = np.zeros((RW, 3 * RW), np.float32)
    for col in range(3 * RW):
        axis, n, v = col // RW, col // STRIDE % ELEMS, col % STRIDE
        if v < VARS:
            vtile[axis * 8 + v, col] = 1.0
        vmask[n * STRIDE : (n + 1) * STRIDE, col] = 1.0
    return dict(
        de=de,
        place=place.reshape(6 * 8 * FACE, NODES),
        turn=turn.reshape(FACE, 8 * FACE),
        restrict=restrict,
        spread=spread,
        own_lanes=own_lanes,
        tile=tile,
        colcode=colcode,
        vtile=vtile,
        vmask=vmask,
    )


def exact_dot(a, b):
    return jnp.dot(a, b, precision=HIGHEST, preferred_element_type=F32)


def exact_dot_t(a, b):
    return lax.dot_general(
        a, b, (((1,), (1,)), ((), ())), precision=HIGHEST, preferred_element_type=F32
    )


def total(values):
    return jnp.sum(values, axis=(0, 1), keepdims=True)


def member_mask(group_ref):
    row = lax.broadcasted_iota(jnp.int32, (STRIDE, WIDE), 0)
    lane = lax.broadcasted_iota(jnp.int32, (STRIDE, WIDE), 1)
    pieces = []
    for e in range(ELEMS):
        hit = (lane // (VARS * 8) == group_ref[e]) & (lane // 8 % VARS == row)
        pieces.append(jnp.where(hit & (lane < KC), 1.0, 0.0))
    return jnp.concatenate(pieces, axis=0)


def message(member, restrict, vector, scalars):
    row = jnp.sum(member * exact_dot(vector, restrict), axis=0, keepdims=True)
    lane = lax.broadcasted_iota(jnp.int32, (1, WIDE), 1)
    for i, value in enumerate(scalars):
        row = jnp.where(lane == SCALAR0 + i, value, row)
    return row


def read_scalars(table_ref, count):
    sums = jnp.sum(table_ref[:, 128:256], axis=0, keepdims=True)
    return [sums[:, SCALAR0 - 128 + i : SCALAR0 - 128 + i + 1] for i in range(count)]


def read_coarse(table_ref, pos_ref):
    rows = table_ref[pl.ds(pl.multiple_of(pos_ref[0] * 8, 8), 8), :]
    row = lax.broadcasted_iota(jnp.int32, (8, WIDE), 0)
    return jnp.sum(jnp.where(row % 2 == pos_ref[2], rows, 0.0), axis=0, keepdims=True)


def coarse_values(coarse, cinv_ref, member_ref, spread_ref):
    solved = exact_dot_t(coarse[:, :KC], cinv_ref[0, 0])
    return exact_dot(member_ref[:, :KC] * solved, spread_ref[:KC, :])


def apply_blocks(blocks_ref, own_lanes, parts):
    stacked = []
    for part in parts:
        pair = jnp.concatenate([part, part], axis=1)
        stacked.append(jnp.concatenate([pair, pair, part], axis=1) * own_lanes)
    wide = jnp.concatenate(stacked, axis=0).astype(jnp.bfloat16)
    pieces = []
    for e in range(ELEMS):
        out = lax.dot_general(
            wide, blocks_ref[e], (((1,), (1,)), ((), ())), preferred_element_type=F32
        )
        mine = out[e * STRIDE : (e + 1) * STRIDE]
        for i in range(1, len(parts)):
            mine = mine + out[i * RW + e * STRIDE : i * RW + (e + 1) * STRIDE]
        pieces.append(jnp.broadcast_to(jnp.sum(mine, axis=0, keepdims=True), (STRIDE, ROWS)))
    full = jnp.concatenate(pieces, axis=0) * own_lanes
    half = full[:, :128] + full[:, 128:256]
    return half[:, :NODES] + half[:, NODES:] + full[:, 256:]


def rounded(values):
    return [values.astype(jnp.bfloat16).astype(F32)]


def two_parts(values):
    high = values.astype(jnp.bfloat16).astype(F32)
    return [high, values - high]


def face_of(grown, face):
    base = 3 * NODES + face * 2 * FACE
    return grown[:, base : base + 2 * FACE]


def write_sends(pos_ref, grown, send_refs):
    p_odd, s_odd, r = pos_ref[0] % 2, pos_ref[1] % 2, pos_ref[2]
    faces = [face_of(grown, f) for f in range(6)]
    send_refs[0][...] = jnp.where(p_odd == 0, faces[1], faces[0])
    send_refs[1][...] = jnp.where(p_odd == 0, faces[0], faces[1])
    send_refs[2][...] = jnp.where(s_odd == 0, faces[3], faces[2])
    send_refs[3][...] = jnp.where(s_odd == 0, faces[2], faces[3])
    send_refs[4][...] = jnp.where(r == 0, faces[5], faces[4])


def jacobian(vector, grown, recv, mass, amat, omask, vmat, turn, place):
    slopes = jnp.concatenate([grown[:, i * NODES : (i + 1) * NODES] for i in range(3)], axis=0)
    result = 1.5 * mass * vector + exact_dot(vmat, slopes)
    pieces = []
    for source in list(recv) + [face_of(grown, f) for f in range(2, 6)]:
        pieces += [source[:, :FACE], source[:, FACE : 2 * FACE]]
    terms = exact_dot(amat, jnp.concatenate(pieces, axis=0))
    laid = exact_dot(terms, turn) * omask
    laid = jnp.concatenate([laid[f * RW : (f + 1) * RW] for f in range(6)], axis=1)
    return result + exact_dot(laid, place)


def start_kernel(rs_ref, mass_ref, group_ref, restrict_ref, x_ref, massw_ref, member_ref, table_ref):
    x_ref[...] = jnp.zeros_like(x_ref)
    massw_ref[...] = jnp.zeros_like(massw_ref)
    for e in range(ELEMS):
        for v in range(VARS):
            lanes = slice(v * NODES, (v + 1) * NODES)
            row = e * STRIDE + v
            x_ref[row : row + 1, :] = rs_ref[e : e + 1, lanes]
            massw_ref[row : row + 1, :] = mass_ref[e : e + 1, lanes]
    member = member_mask(group_ref)
    member_ref[...] = member
    x = x_ref[...]
    row = message(member, restrict_ref[...], x, [total(x * x)])
    table_ref[...] = jnp.broadcast_to(row, table_ref.shape)


def setup_kernel(
    pos_ref,
    neigh_ref,
    orient_ref,
    tags_ref,
    vj_ref,
    flux_ref,
    visc_ref,
    tile_ref,
    colcode_ref,
    vtile_ref,
    vmask_ref,
    amat_ref,
    omask_ref,
    vmat_ref,
    coef_ref,
    vcoef_ref,
):
    p_odd, s_odd = pos_ref[0] % 2, pos_ref[1] % 2
    device = pos_ref[3]
    coef_ref[...] = jnp.zeros_like(coef_ref)
    vcoef_ref[...] = jnp.zeros_like(vcoef_ref)
    for e in range(ELEMS):
        for axis in range(3):
            vcoef_ref[e * STRIDE : e * STRIDE + VARS, axis * 8 : axis * 8 + VARS] = vj_ref[e, axis]
        for f in range(6):
            row = f * RW + e * STRIDE
            coef_ref[row : row + VARS, 0:VARS] = flux_ref[e, f]
            coef_ref[row : row + VARS, 8 : 8 + VARS] = visc_ref[e, f]
    vmat_ref[...] = exact_dot(vcoef_ref[...], vtile_ref[...]) * vmask_ref[...]
    cols = SOURCES * 2 * RW
    lane = lax.broadcasted_iota(jnp.int32, (STRIDE, 8 * FACE), 1)
    colcode = jnp.broadcast_to(colcode_ref[0:1, :], (STRIDE, cols))
    for f in range(6):
        axis = f // 2
        spread = exact_dot(coef_ref[f * RW : (f + 1) * RW, :], tile_ref[...])
        signs = jnp.broadcast_to(colcode_ref[1 + axis : 2 + axis, :], (STRIDE, cols))
        for e in range(ELEMS):
            near = neigh_ref[e, f]
            tag = tags_ref[e, f]
            spot = near % ELEMS
            crossing = near // ELEMS != device
            if f == 0:
                source = 1 - p_odd
            elif f == 1:
                source = p_odd
            elif f == 2:
                source = 3 - s_odd
            elif f == 3:
                source = 2 + s_odd
            else:
                source = jnp.where(crossing, 4, 8 if f == 4 else 7)
            code = source * ELEMS + spot
            turn_code = orient_ref[e, f]
            if f >= 2:
                wall_code = (5 + f - 2) * ELEMS + e
                code = jnp.where(tag == 0, code, jnp.where(tag == 1, wall_code, -1))
                turn_code = jnp.where(tag == 0, turn_code, 0)
            rows = slice(f * RW + e * STRIDE, f * RW + (e + 1) * STRIDE)
            values = spread[e * STRIDE : (e + 1) * STRIDE]
            values = jnp.where(tag == 1, values * signs, values)
            amat_ref[rows, :] = jnp.where(colcode == code.astype(F32), -values, 0.0)
            omask_ref[rows, :] = jnp.where(lane // FACE == turn_code, 1.0, 0.0)


def first_kernel(step, *refs):
    if step == 0:
        pos, table, x, blocks, cinv, member, spread, own, de = refs[:9]
        z_ref, coarse_ref, scal_ref, first_ref, grown_ref, *sends = refs[9:]
        beta = jnp.sqrt(read_scalars(table, 1)[0])
        z = x[...] / beta
        coarse = read_coarse(table, pos) / beta
        scal_ref[...] = jnp.broadcast_to(beta, scal_ref.shape)
        parts = rounded(z)
    elif step == 1:
        pos, table, x, b0, coarse0, blocks, cinv, member, spread, own, de = refs[:11]
        z_ref, scal_ref, first_ref, grown_ref, *sends = refs[11:]
        h00, square = read_scalars(table, 2)
        h10 = jnp.sqrt(jnp.maximum(square - h00 * h00, 1e-7 * square))
        z = (x[...] - h00 * b0[...]) / h10
        coarse = (read_coarse(table, pos) - h00 * coarse0[...]) / h10
        row = lax.broadcasted_iota(jnp.int32, scal_ref.shape, 0)
        scal_ref[...] = jnp.where(row == 0, h00, jnp.where(row == 1, h10, square))
        parts = rounded(z)
    else:
        pos, c0, c1, c2, c3, x, blocks, cinv, member, spread, own, de = refs[:12]
        first_ref, grown_ref, *sends = refs[12:]
        z_ref = None
        z = x[...]
        coarse = (c0[...] + c1[...]) + (c2[...] + c3[...])
        parts = two_parts(z)
    if z_ref is not None:
        z_ref[...] = z
    if step == 0:
        coarse_ref[...] = coarse
    first = apply_blocks(blocks, own[...], parts) + coarse_values(coarse, cinv, member, spread)
    first_ref[...] = first
    grown = exact_dot(first, de[...])
    grown_ref[...] = grown
    write_sends(pos, grown, sends)


def second_kernel(step, *refs):
    pos, z, first, grown = refs[:4]
    recv = [r[...] for r in refs[4:9]]
    mass, amat, omask, vmat, turn, place, blocks, own, de = refs[9:18]
    search_ref, grown2_ref, *sends = refs[18:]
    mapped = jacobian(
        first[...],
        grown[...],
        recv,
        mass[...],
        amat[...],
        omask[...],
        vmat[...],
        turn[...],
        place[...],
    )
    defect = z[...] - mapped
    parts = two_parts(defect) if step == 2 else rounded(defect)
    search = first[...] + apply_blocks(blocks, own[...], parts)
    search_ref[...] = search
    grown2 = exact_dot(search, de[...])
    grown2_ref[...] = grown2
    write_sends(pos, grown2, sends)


def third_kernel(step, *refs):
    search, grown = refs[:2]
    recv = [r[...] for r in refs[2:7]]
    mass, amat, omask, vmat, turn, place = refs[7:13]
    mapped = jacobian(
        search[...],
        grown[...],
        recv,
        mass[...],
        amat[...],
        omask[...],
        vmat[...],
        turn[...],
        place[...],
    )
    if step == 0:
        member, restrict, b0, w_ref, table_ref = refs[13:]
        scalars = [total(mapped * b0[...]), total(mapped * mapped)]
        row = message(member[...], restrict[...], mapped, scalars)
        table_ref[...] = jnp.broadcast_to(row, table_ref.shape)
    elif step == 1:
        member, restrict, w_ref, row_ref = refs[13:]
        row_ref[...] = message(member[...], restrict[...], mapped, [])
    else:
        b0, b1, w1, w_ref, table_ref = refs[13:]
        scalars = [total(w1[...] * b[...]) for b in (b0, b1, w1)]
        scalars += [total(mapped * b[...]) for b in (b0, b1, w1)]
        scalars += [total(mapped * mapped)]
        lane = lax.broadcasted_iota(jnp.int32, (1, 128), 1)
        row = jnp.zeros((1, 128), F32)
        for i, value in enumerate(scalars):
            row = jnp.where(lane == i, value, row)
        table_ref[...] = jnp.broadcast_to(row, table_ref.shape)
    w_ref[...] = mapped


def least_squares(matrix, beta):
    iters = len(matrix) - 1
    target = [beta] + [jnp.zeros_like(beta)] * iters
    for k in range(iters):
        top, low = matrix[k][k], matrix[k + 1][k]
        radius = jnp.sqrt(top * top + low * low)
        cosine, sine = top / radius, low / radius
        for later in range(k, iters):
            upper, lower = matrix[k][later], matrix[k + 1][later]
            matrix[k][later] = cosine * upper + sine * lower
            matrix[k + 1][later] = -sine * upper + cosine * lower
        upper, lower = target[k], target[k + 1]
        target[k] = cosine * upper + sine * lower
        target[k + 1] = -sine * upper + cosine * lower
    weights = [None] * iters
    for k in reversed(range(iters)):
        value = target[k]
        for later in range(k + 1, iters):
            value = value - matrix[k][later] * weights[later]
        weights[k] = value / matrix[k][k]
    return weights


def final_kernel(table, scal0, scal1, x, s0, s1, s2, w0, w1, w2, update_ref, residual_ref):
    sums = jnp.sum(table[...], axis=0, keepdims=True)
    g0, g1, g2, q0, q1, qw, qq = [sums[:, i : i + 1] for i in range(7)]
    beta = scal0[0:1, 0:1]
    h00, h10, square0 = [scal1[i : i + 1, 0:1] for i in range(3)]
    h01, h11 = g0, g1
    h21 = jnp.sqrt(jnp.maximum(g2 - h01 * h01 - h11 * h11, 1e-7 * g2))
    cross = h00 * h01 + h10 * h11
    h02 = (q0 - h01 * h00 - h11 * h01) / h21
    h12 = (q1 - h01 * h10 - h11 * h11) / h21
    with_w1 = (qw - h01 * cross - h11 * g2) / h21
    h22 = (with_w1 - h01 * h02 - h11 * h12) / h21
    with_w0 = h00 * q0 + h10 * q1
    square = qq + h01 * h01 * square0 + h11 * h11 * g2
    square = square - 2.0 * (h01 * with_w0 + h11 * qw - h01 * h11 * cross)
    square = square / (h21 * h21)
    h32 = jnp.sqrt(jnp.maximum(square - h02 * h02 - h12 * h12 - h22 * h22, 1e-7 * square))
    zero = jnp.zeros_like(beta)
    hess = [[h00, h01, h02], [h10, h11, h12], [zero, h21, h22], [zero, zero, h32]]
    y0, y1, y2 = least_squares(hess, beta)
    y2 = y2 / h21
    y0 = y0 - y2 * h01
    y1 = y1 - y2 * h11
    update = y0 * s0[...] + y1 * s1[...] + y2 * s2[...]
    residual = x[...] - (y0 * w0[...] + y1 * w1[...] + y2 * w2[...])
    for e in range(ELEMS):
        for v in range(VARS):
            lanes = slice(v * NODES, (v + 1) * NODES)
            row = e * STRIDE + v
            update_ref[e : e + 1, lanes] = update[row : row + 1, :]
            residual_ref[e : e + 1, lanes] = residual[row : row + 1, :]


VMEM = pltpu.VMEM
SMEM = pltpu.SMEM


def call(kernel, name, args, outs, smem=(), scratch=()):
    return pl.pallas_call(
        kernel,
        name=name,
        out_shape=[jax.ShapeDtypeStruct(shape, F32) for shape in outs],
        in_specs=[
            pl.BlockSpec(memory_space=SMEM if i in smem else VMEM) for i in range(len(args))
        ],
        out_specs=[pl.BlockSpec(memory_space=VMEM)] * len(outs),
        scratch_shapes=[VMEM(shape, F32) for shape in scratch],
        compiler_params=pltpu.CompilerParams(vmem_limit_bytes=32 * 1024 * 1024),
    )(*args)


def with_step(kernel, step):
    def run(*refs):
        kernel(step, *refs)

    return run


def body(
    right_side,
    mass,
    volume_jac,
    face_flux,
    face_visc,
    block_inverse,
    coarse_inverse,
    neighbours,
    orientation,
    bc_tags,
    coarse_group,
):
    t = {name: jnp.asarray(value) for name, value in tables().items()}
    n_pass, n_span = lax.axis_size("passage"), lax.axis_size("span")
    n_rad = lax.axis_size("radial")
    devices = n_pass * n_span * n_rad
    p, s, r = (lax.axis_index(a) for a in AXES)
    pos = jnp.stack([p, s, r, (p * n_span + s) * n_rad + r]).astype(jnp.int32)

    pass_a = [(i, i ^ 1) for i in range(n_pass)]
    pass_b = [(i, (i + 1 if i % 2 else i - 1) % n_pass) for i in range(n_pass)]
    span_a = [(i, i ^ 1) for i in range(n_span)]
    span_b = [(i, i + 1 if i % 2 else i - 1) for i in range(1, n_span - 1)]
    rad = [(0, 1), (1, 0)]

    def exchange(sends):
        got = [None] * 5
        got[4] = lax.ppermute(sends[4], "radial", rad)
        got[3] = lax.ppermute(sends[3], "span", span_b)
        got[2] = lax.ppermute(sends[2], "span", span_a)
        got[1] = lax.ppermute(sends[1], "passage", pass_b)
        got[0] = lax.ppermute(sends[0], "passage", pass_a)
        return got

    vec = (RW, NODES)
    grow = (RW, t["de"].shape[1])
    send = (RW, 2 * FACE)

    x, massw, member, table = call(
        start_kernel,
        "start",
        (right_side, mass, coarse_group, t["restrict"]),
        [vec, vec, (RW, WIDE), (devices, WIDE)],
        smem=(2,),
    )
    amat, omask, vmat = call(
        setup_kernel,
        "setup",
        (
            pos,
            neighbours,
            orientation,
            bc_tags,
            volume_jac,
            face_flux,
            face_visc,
            t["tile"],
            t["colcode"],
            t["vtile"],
            t["vmask"],
        ),
        [(6 * RW, SOURCES * 2 * RW), (6 * RW, 8 * FACE), (RW, 3 * RW)],
        smem=(0, 1, 2, 3),
        scratch=[(6 * RW, 16), (RW, 24)],
    )
    operator = (massw, amat, omask, vmat, t["turn"], t["place"])
    table = lax.all_to_all(table, AXES, 0, 0, tiled=True)

    basis, search, images, scalars = [], [], [], []
    coarse0 = row = None
    for step in range(3):
        tail = (block_inverse, coarse_inverse, member, t["spread"], t["own_lanes"], t["de"])
        outs = [vec, grow] + [send] * 5
        kernel = with_step(first_kernel, step)
        if step == 0:
            z, coarse0, scal, first, grown, *sends = call(
                kernel,
                "first0",
                (pos, table, x) + tail,
                [vec, (1, WIDE), (8, 128)] + outs,
                smem=(0,),
            )
            scalars.append(scal)
        elif step == 1:
            z, scal, first, grown, *sends = call(
                kernel,
                "first1",
                (pos, table, images[0], basis[0], coarse0) + tail,
                [vec, (8, 128)] + outs,
                smem=(0,),
            )
            scalars.append(scal)
        else:
            rows = [lax.ppermute(row, "span", [(i, i ^ k) for i in range(n_span)]) for k in (2, 3, 1)]
            z = images[1]
            first, grown, *sends = call(
                kernel, "first2", (pos, row, *rows, z) + tail, outs, smem=(0,)
            )
        basis.append(z)
        recv = exchange(sends)
        direction, grown, *sends = call(
            with_step(second_kernel, step),
            "second%d" % step,
            (pos, z, first, grown, *recv) + operator + (block_inverse, t["own_lanes"], t["de"]),
            outs,
            smem=(0,),
        )
        search.append(direction)
        recv = exchange(sends)
        kernel = with_step(third_kernel, step)
        head = (direction, grown, *recv) + operator
        if step == 0:
            image, table = call(
                kernel,
                "third0",
                head + (member, t["restrict"], basis[0]),
                [vec, (devices, WIDE)],
            )
            table = lax.all_to_all(table, AXES, 0, 0, tiled=True)
        elif step == 1:
            image, row = call(kernel, "third1", head + (member, t["restrict"]), [vec, (1, WIDE)])
        else:
            image, table = call(
                kernel,
                "third2",
                head + (basis[0], basis[1], basis[2]),
                [vec, (devices, 128)],
            )
            table = lax.all_to_all(table, AXES, 0, 0, tiled=True)
        images.append(image)

    update, residual = call(
        final_kernel,
        "final",
        (table, *scalars, x, *search, *images),
        [right_side.shape] * 2,
    )
    return (update, residual)


def solution(mesh):
    rows = P(AXES, None)
    blocks = P(AXES, None, None)
    jac = P(AXES, None, None, None)
    in_specs = (
        rows,
        rows,
        jac,
        jac,
        jac,
        blocks,
        P("passage", "radial", None, None),
        rows,
        rows,
        rows,
        P(AXES),
    )
    return jax.shard_map(body, mesh=mesh, in_specs=in_specs, out_specs=(rows, rows), check_vma=False)
```

```python
import math

import jax
import jax.numpy as jnp
import numpy as np
from jax import lax
from jax.experimental import pallas as pl
from jax.experimental.pallas import tpu as pltpu
from jax.sharding import PartitionSpec as P

QN = 4
VARS = 5
CG = 4
ELEMS = 4
NODES = QN**3
ROWS = 320
KC = 160
STRIDE = 8
RW = ELEMS * STRIDE
FACE = QN * QN
SOURCES = ((0, 1), (2, 3, 5, 6), (4, 7, 8))
WIDE = 256
AXES = ("passage", "span", "radial")
NEIGH, ORIENT, TAGS, GROUP, PLACE = 0, 6, 12, 18, 19
HIGHEST = lax.Precision.HIGHEST
F32 = jnp.float32


def lobatto_nodes():
    inner_node = 1.0 / math.sqrt(5.0)
    return np.array([-1.0, -inner_node, inner_node, 1.0])


def derivative_table():
    nodes = lobatto_nodes()
    weights = np.ones(QN)
    for row_id in range(QN):
        for col_id in range(QN):
            if col_id != row_id:
                weights[row_id] = weights[row_id] / (nodes[row_id] - nodes[col_id])
    result = np.zeros((QN, QN))
    for row_id in range(QN):
        for col_id in range(QN):
            if col_id != row_id:
                result[row_id, col_id] = (
                    weights[col_id] / weights[row_id] / (nodes[row_id] - nodes[col_id])
                )
        result[row_id, row_id] = -np.sum(result[row_id])
    return result


def vertex_table():
    nodes = lobatto_nodes()
    shapes = np.stack([(1.0 - nodes) / 2.0, (1.0 + nodes) / 2.0])
    first_part = shapes[:, None, None, :, None, None]
    second_part = shapes[None, :, None, None, :, None]
    third_part = shapes[None, None, :, None, None, :]
    return (first_part * second_part * third_part).reshape(8, NODES)


def coords(node):
    return (node // 16, node // 4 % 4, node % 4)


def others(node, axis):
    picked = [c for i, c in enumerate(coords(node)) if i != axis]
    return picked[0] * QN + picked[1]


def layer_of(face):
    return 0 if face % 2 == 0 else QN - 1


def stacked(values):
    high = values.astype(jnp.bfloat16)
    low = (values - high.astype(np.float32)).astype(jnp.bfloat16)
    return np.concatenate([high, high, low], axis=0)


def tables():
    dmat = derivative_table()
    de = np.zeros((NODES, 3 * NODES + 6 * 2 * FACE), np.float32)
    place = np.zeros((6, 1, FACE, NODES), np.float32)
    for node in range(NODES):
        for axis in range(3):
            for target in range(NODES):
                if others(node, axis) == others(target, axis):
                    de[node, axis * NODES + target] = dmat[
                        coords(target)[axis], coords(node)[axis]
                    ]
        for face in range(6):
            axis = face // 2
            spot = others(node, axis)
            base = 3 * NODES + face * 2 * FACE
            de[node, base + FACE + spot] = dmat[layer_of(face), coords(node)[axis]]
            if coords(node)[axis] == layer_of(face):
                de[node, base + spot] = 1.0
                place[face, :, spot, node] = 1.0
    turn = np.zeros((FACE, 8, FACE), np.float32)
    for code in range(8):
        for i in range(QN):
            for j in range(QN):
                a = QN - 1 - i if code & 2 else i
                b = QN - 1 - j if code & 1 else j
                if code & 4:
                    a, b = b, a
                turn[a * QN + b, code, i * QN + j] = 1.0
    rtab = vertex_table().astype(np.float32)
    restrict = np.zeros((NODES, WIDE), np.float32)
    restrict[:, :KC] = np.tile(rtab.T, (1, CG * VARS))
    lay = np.einsum("aob,fbk->foak", turn, place[:, 0]).reshape(6 * 8 * FACE, NODES)
    own_lanes = np.zeros((RW, ROWS), np.float32)
    for row in range(RW):
        v = row % STRIDE
        if v < VARS:
            own_lanes[row, v * NODES : (v + 1) * NODES] = 1.0
    tile = np.zeros((80, 6 * 256), np.float32)
    colcode = np.full((8, 6 * 256), -100.0, np.float32)
    for face in range(6):
        axis = face // 2
        for place_id, source in enumerate(SOURCES[axis]):
            for col in range(2 * RW):
                kind, n, v = col // RW, col // STRIDE % ELEMS, col % STRIDE
                lane = face * 256 + place_id * 2 * RW + col
                if v < VARS:
                    tile[kind * 40 + v * 8 + face, lane] = 1.0
                colcode[0, lane] = source * ELEMS + n
                colcode[1, lane] = (-1.0 if v == 1 + axis else 1.0) * (-1.0 if kind else 1.0)
    rows = np.zeros((RW, 24), np.float32)
    for e in range(ELEMS):
        for u in range(VARS):
            rows[e * STRIDE + u, u * ELEMS + e] = 1.0
    vtile = np.zeros((24, 3 * RW), np.float32)
    vmask = np.zeros((RW, 3 * RW), np.float32)
    for col in range(3 * RW):
        axis, n, v = col // RW, col // STRIDE % ELEMS, col % STRIDE
        if v < VARS:
            vtile[axis * 8 + v, col] = 1.0
        vmask[n * STRIDE : (n + 1) * STRIDE, col] = 1.0
    return dict(
        de=stacked(de),
        lay=lay.astype(jnp.bfloat16),
        restrict=stacked(restrict),
        spread=stacked(np.ascontiguousarray(restrict.T)),
        own_lanes=own_lanes,
        tile=tile,
        colcode=colcode,
        rows=rows,
        vtile=vtile,
        vmask=vmask,
    )


def exact_dot(a, b):
    return jnp.dot(a, b, precision=HIGHEST, preferred_element_type=F32)


def halves(values):
    high = values.astype(jnp.bfloat16)
    return high, (values - high.astype(F32)).astype(jnp.bfloat16)


def left_stack(values):
    high = values.astype(jnp.bfloat16).astype(F32)
    return jnp.concatenate([high, values - high, high], axis=1).astype(jnp.bfloat16)


def right_stack(values):
    high, low = halves(values)
    return jnp.concatenate([high, low, high], axis=0)


def dot(a, b):
    return jnp.dot(a, b, preferred_element_type=F32)


def total(values):
    return jnp.sum(values, axis=(0, 1), keepdims=True)


def member_mask(ints_ref):
    row = lax.broadcasted_iota(jnp.int32, (STRIDE, WIDE), 0)
    lane = lax.broadcasted_iota(jnp.int32, (STRIDE, WIDE), 1)
    pieces = []
    for e in range(ELEMS):
        hit = (lane // (VARS * 8) == ints_ref[e, GROUP]) & (lane // 8 % VARS == row)
        pieces.append(jnp.where(hit & (lane < KC), 1.0, 0.0))
    return jnp.concatenate(pieces, axis=0)


def coarse_row(member, restrict, vector):
    return jnp.sum(member * dot(left_stack(vector), restrict), axis=0, keepdims=True)


def scalar_row(scalars):
    lane = lax.broadcasted_iota(jnp.int32, (1, 128), 1)
    row = jnp.zeros((1, 128), F32)
    for i, value in enumerate(scalars):
        row = jnp.where(lane == i, value, row)
    return row


def read_scalars(table_ref, count):
    sums = jnp.sum(table_ref[...], axis=0, keepdims=True)
    return [sums[:, i : i + 1] for i in range(count)]


def coarse_values(coarse, cinv_ref, member_ref, spread_ref):
    solved = lax.dot_general(
        left_stack(coarse[:, :KC]),
        cinv_ref[...],
        (((1,), (1,)), ((), ())),
        preferred_element_type=F32,
    )
    solved = jnp.concatenate([solved, jnp.zeros((1, WIDE - KC), F32)], axis=1)
    return dot(left_stack(member_ref[...] * solved), spread_ref[...])


def apply_blocks(turned_ref, own_lanes, parts):
    stacked = []
    for part in parts:
        pair = jnp.concatenate([part, part], axis=1)
        stacked.append(jnp.concatenate([pair, pair, part], axis=1) * own_lanes)
    pieces = []
    for e in range(ELEMS):
        rows = [part[e * STRIDE : (e + 1) * STRIDE] for part in stacked]
        rows = jnp.concatenate(rows, axis=0) if len(rows) > 1 else rows[0]
        out = dot(rows.astype(jnp.bfloat16), turned_ref[e])
        pieces.append(jnp.broadcast_to(jnp.sum(out, axis=0, keepdims=True), (STRIDE, ROWS)))
    full = jnp.concatenate(pieces, axis=0) * own_lanes
    half = full[:, :128] + full[:, 128:256]
    return half[:, :NODES] + half[:, NODES:] + full[:, 256:]


def rounded(values):
    return [values.astype(jnp.bfloat16).astype(F32)]


def two_parts(values):
    high = values.astype(jnp.bfloat16).astype(F32)
    return [high, values - high]


def face_of(grown, face):
    base = 3 * NODES + face * 2 * FACE
    return grown[:, base : base + 2 * FACE]


def pack(grown, face):
    values = face_of(grown, face)
    rows = [values[e * STRIDE : (e + 1) * STRIDE] for e in range(ELEMS)]
    return jnp.concatenate(rows, axis=1)


def copies(tile, slot):
    lane = lax.broadcasted_iota(jnp.int32, tile.shape, 1)
    values = jnp.where(lane // FACE == slot, tile, 0.0)
    for shift in (FACE, 2 * FACE, 4 * FACE):
        values = values + pltpu.roll(values, shift, 1)
    return values


def unpack(tile):
    return [copies(tile, e * 2 + kind) for kind in range(2) for e in range(ELEMS)]


def write_sends(ints_ref, grown, send_refs):
    p_odd, s_odd, r = ints_ref[0, PLACE] % 2, ints_ref[1, PLACE] % 2, ints_ref[2, PLACE]
    faces = [pack(grown, f) for f in range(6)]
    send_refs[0][...] = jnp.where(r == 0, faces[5], faces[4])
    send_refs[1][...] = jnp.where(p_odd == 0, faces[0], faces[1])
    send_refs[2][...] = jnp.where(s_odd == 0, faces[3], faces[2])
    send_refs[3][...] = jnp.where(s_odd == 0, faces[2], faces[3])
    send_refs[4][...] = jnp.where(p_odd == 0, faces[1], faces[0])


def place_terms(groups, omask_ref, lay_ref, first_face):
    laid = []
    for i, terms in enumerate(groups):
        base = (first_face + 2 * i) * RW
        terms = terms * omask_ref[base : base + 2 * RW, :]
        laid += [terms[:RW], terms[RW:]]
    laid = jnp.concatenate(laid, axis=1)
    high, low = halves(laid)
    out = dot(jnp.concatenate([high, low], axis=0), lay_ref[first_face * 8 * FACE :, :])
    return out[:RW] + out[RW:]


def halo_part(recv, rem, omask_ref, lay_ref):
    rad, pass_b, span_a, span_b, pass_a = [unpack(r[...]) for r in recv]
    groups = []
    for pieces, mat in ((pass_a + pass_b, rem[0]), (span_a + span_b, rem[1]), (rad, rem[2])):
        groups.append(dot(mat[...], right_stack(jnp.concatenate(pieces, axis=0))))
    return place_terms(groups, omask_ref, lay_ref, 0)


def start_kernel(rs_ref, table_ref):
    rs = rs_ref[...]
    table_ref[...] = jnp.broadcast_to(scalar_row([total(rs * rs)]), table_ref.shape)


def prepare_kernel(rs_ref, mass_ref, ints_ref, restrict_ref, x_ref, massw_ref, member_ref, row_ref):
    x_ref[...] = jnp.zeros_like(x_ref)
    massw_ref[...] = jnp.zeros_like(massw_ref)
    for e in range(ELEMS):
        for v in range(VARS):
            lanes = slice(v * NODES, (v + 1) * NODES)
            row = e * STRIDE + v
            x_ref[row : row + 1, :] = rs_ref[e : e + 1, lanes]
            massw_ref[row : row + 1, :] = mass_ref[e : e + 1, lanes]
    member = member_mask(ints_ref)
    member_ref[...] = member
    row_ref[...] = coarse_row(member, restrict_ref[...], x_ref[...])


def setup_kernel(
    ints_ref,
    volume_ref,
    flux_ref,
    visc_ref,
    blocks_ref,
    rows_ref,
    tile_ref,
    colcode_ref,
    vtile_ref,
    vmask_ref,
    cinv_ref,
    rem0_ref,
    rem1_ref,
    rem2_ref,
    loc1_ref,
    loc2_ref,
    omask_ref,
    vmat_ref,
    cinv3_ref,
    turned_ref,
    coef_ref,
    amat_ref,
):
    p_odd, s_odd = ints_ref[0, PLACE] % 2, ints_ref[1, PLACE] % 2
    device = ints_ref[3, PLACE]
    coef_ref[...] = jnp.zeros_like(coef_ref)
    for u in range(VARS):
        here = slice(u * ELEMS, (u + 1) * ELEMS)
        for axis in range(3):
            coef_ref[here, 80 + axis * 8 : 80 + axis * 8 + VARS] = volume_ref[axis, u]
        for v in range(VARS):
            coef_ref[here, v * 8 : v * 8 + 6] = flux_ref[u, v]
            coef_ref[here, 40 + v * 8 : 40 + v * 8 + 6] = visc_ref[u, v]
    coef = exact_dot(rows_ref[...], coef_ref[...])
    vmat_ref[...] = right_factor(exact_dot(coef[:, 80:104], vtile_ref[...]) * vmask_ref[...])
    cinv3_ref[...] = right_factor(cinv_ref[0, 0])
    for e in range(ELEMS):
        turned_ref[e] = blocks_ref[e].T
    spread = exact_dot(coef[:, :80], tile_ref[...])
    lane = lax.broadcasted_iota(jnp.int32, (STRIDE, 8 * FACE), 1)
    for f in range(6):
        cols = slice(f * 256, (f + 1) * 256)
        colcode = jnp.broadcast_to(colcode_ref[0:1, cols], (STRIDE, 256))
        signs = jnp.broadcast_to(colcode_ref[1:2, cols], (STRIDE, 256))
        for e in range(ELEMS):
            near = ints_ref[e, NEIGH + f]
            tag = ints_ref[e, TAGS + f]
            spot = near % ELEMS
            crossing = near // ELEMS != device
            if f == 0:
                source = 1 - p_odd
            elif f == 1:
                source = p_odd
            elif f == 2:
                source = 3 - s_odd
            elif f == 3:
                source = 2 + s_odd
            else:
                source = jnp.where(crossing, 4, 8 if f == 4 else 7)
            code = source * ELEMS + spot
            turn_code = ints_ref[e, ORIENT + f]
            if f >= 2:
                wall_code = (5 + f - 2) * ELEMS + e
                code = jnp.where(tag == 0, code, jnp.where(tag == 1, wall_code, -1))
                turn_code = jnp.where(tag == 0, turn_code, 0)
            rows = slice(f * RW + e * STRIDE, f * RW + (e + 1) * STRIDE)
            values = spread[e * STRIDE : (e + 1) * STRIDE, cols]
            values = jnp.where(tag == 1, values * signs, values)
            amat_ref[rows, :] = jnp.where(colcode == code.astype(F32), -values, 0.0)
            omask_ref[rows, :] = jnp.where(lane // FACE == turn_code, 1.0, 0.0)
    one = 2 * RW
    rem0_ref[...] = right_factor(amat_ref[:one, : 2 * one])
    rem1_ref[...] = right_factor(amat_ref[one : 2 * one, : 2 * one])
    loc1_ref[...] = right_factor(amat_ref[one : 2 * one, 2 * one : 4 * one])
    rem2_ref[...] = right_factor(amat_ref[2 * one :, :one])
    loc2_ref[...] = right_factor(amat_ref[2 * one :, one : 3 * one])


def right_factor(values):
    high = values.astype(jnp.bfloat16).astype(F32)
    return jnp.concatenate([high, high, values - high], axis=1).astype(jnp.bfloat16)


def coarse_kernel(r0, r1, r2, r3, cinv, member, spread, coarse_ref):
    coarse = (r0[...] + r1[...]) + (r2[...] + r3[...])
    coarse_ref[...] = coarse_values(coarse, cinv, member, spread)


def blocks_kernel(x, blocks, own, out_ref):
    out_ref[...] = apply_blocks(blocks, own[...], two_parts(x[...]))


def finish_first(ints, first, de, first_ref, grown_ref, sends):
    first_ref[...] = first
    grown = dot(left_stack(first), de[...])
    grown_ref[...] = grown
    write_sends(ints, grown, sends)


def first0_kernel(ints, table, x, coarse, blocks, own, de, *outs):
    z_ref, coarse_ref, scal_ref, first_ref, grown_ref, *sends = outs
    beta = jnp.sqrt(read_scalars(table, 1)[0])
    z = x[...] / beta
    z_ref[...] = z
    scal_ref[...] = jnp.broadcast_to(beta, scal_ref.shape)
    scaled = coarse[...] / beta
    coarse_ref[...] = scaled
    first = apply_blocks(blocks, own[...], rounded(z)) + scaled
    finish_first(ints, first, de, first_ref, grown_ref, sends)


def first1_kernel(ints, table, x, coarse, b0, coarse0, blocks, own, de, *outs):
    z_ref, scal_ref, first_ref, grown_ref, *sends = outs
    h00, square = read_scalars(table, 2)
    h10 = jnp.sqrt(jnp.maximum(square - h00 * h00, 1e-7 * square))
    z = (x[...] - h00 * b0[...]) / h10
    z_ref[...] = z
    row = lax.broadcasted_iota(jnp.int32, scal_ref.shape, 0)
    scal_ref[...] = jnp.where(row == 0, h00, jnp.where(row == 1, h10, square))
    scaled = (coarse[...] - h00 * coarse0[...]) / h10
    first = apply_blocks(blocks, own[...], rounded(z)) + scaled
    finish_first(ints, first, de, first_ref, grown_ref, sends)


def first2_kernel(ints, r0, r1, r2, r3, fine, cinv, member, spread, de, *outs):
    first_ref, grown_ref, *sends = outs
    coarse = (r0[...] + r1[...]) + (r2[...] + r3[...])
    first = fine[...] + coarse_values(coarse, cinv, member, spread)
    finish_first(ints, first, de, first_ref, grown_ref, sends)


def local_kernel(x, grown_ref, mass, vmat, loc1, loc2, omask, lay, out_ref):
    grown = grown_ref[...]
    slopes = jnp.concatenate([grown[:, i * NODES : (i + 1) * NODES] for i in range(3)], axis=0)
    result = 1.5 * mass[...] * x[...] + dot(vmat[...], right_stack(slopes))
    groups = []
    for faces, mat in (((2, 3), loc1), ((4, 5), loc2)):
        pieces = []
        for f in faces:
            base = 3 * NODES + f * 2 * FACE
            tile = grown[:, base // 128 * 128 : base // 128 * 128 + 128]
            slot = base % 128 // FACE
            pieces += [copies(tile, slot), copies(tile, slot + 1)]
        groups.append(dot(mat[...], right_stack(jnp.concatenate(pieces, axis=0))))
    out_ref[...] = result + place_terms(groups, omask, lay, 2)


def second_kernel(step, *refs):
    ints, z, first, local = refs[:4]
    recv = refs[4:9]
    rem, omask, lay, blocks, own, de = refs[9:12], *refs[12:17]
    search_ref, grown_ref, *sends = refs[17:]
    defect = z[...] - (local[...] + halo_part(recv, rem, omask, lay))
    parts = two_parts(defect) if step == 2 else rounded(defect)
    search = first[...] + apply_blocks(blocks, own[...], parts)
    search_ref[...] = search
    grown = dot(left_stack(search), de[...])
    grown_ref[...] = grown
    write_sends(ints, grown, sends)


def third_kernel(step, *refs):
    local = refs[0]
    recv = refs[1:6]
    rem, omask, lay = refs[6:9], refs[9], refs[10]
    mapped = local[...] + halo_part(recv, rem, omask, lay)
    if step == 0:
        member, restrict, b0, w_ref, table_ref, row_ref = refs[11:]
        scalars = [total(mapped * b0[...]), total(mapped * mapped)]
    elif step == 1:
        member, restrict, w_ref, row_ref = refs[11:]
    else:
        b0, b1, w1, w_ref, table_ref = refs[11:]
        scalars = [total(w1[...] * b[...]) for b in (b0, b1, w1)]
        scalars += [total(mapped * b[...]) for b in (b0, b1, w1)]
        scalars += [total(mapped * mapped)]
    w_ref[...] = mapped
    if step != 1:
        table_ref[...] = jnp.broadcast_to(scalar_row(scalars), table_ref.shape)
    if step != 2:
        row_ref[...] = coarse_row(member[...], restrict[...], mapped)


def inverse_sqrt(value):
    guess = lax.rsqrt(value)
    return guess * (1.5 - 0.5 * (value * guess) * guess)


def least_squares(matrix, beta):
    iters = len(matrix) - 1
    target = [beta] + [jnp.zeros_like(beta)] * iters
    inverse = []
    for k in range(iters):
        top, low = matrix[k][k], matrix[k + 1][k]
        scale = inverse_sqrt(top * top + low * low)
        inverse.append(scale)
        cosine, sine = top * scale, low * scale
        for later in range(k + 1, iters):
            upper, lower = matrix[k][later], matrix[k + 1][later]
            matrix[k][later] = cosine * upper + sine * lower
            matrix[k + 1][later] = -sine * upper + cosine * lower
        upper, lower = target[k], target[k + 1]
        target[k] = cosine * upper + sine * lower
        target[k + 1] = -sine * upper + cosine * lower
    weights = [None] * iters
    for k in reversed(range(iters)):
        value = target[k]
        for later in range(k + 1, iters):
            value = value - matrix[k][later] * weights[later]
        weights[k] = value * inverse[k]
    return weights


def final_kernel(table, scal0, scal1, x, s0, s1, s2, w0, w1, w2, update_ref, residual_ref):
    sums = jnp.sum(table[...], axis=0, keepdims=True)
    g0, g1, g2, q0, q1, qw, qq = [sums[:, i : i + 1] for i in range(7)]
    beta = scal0[0:1, 0:1]
    h00, h10, square0 = [scal1[i : i + 1, 0:1] for i in range(3)]
    h01, h11 = g0, g1
    squared = jnp.maximum(g2 - h01 * h01 - h11 * h11, 1e-7 * g2)
    inv21 = inverse_sqrt(squared)
    h21 = squared * inv21
    cross = h00 * h01 + h10 * h11
    h02 = (q0 - h01 * h00 - h11 * h01) * inv21
    h12 = (q1 - h01 * h10 - h11 * h11) * inv21
    with_w1 = (qw - h01 * cross - h11 * g2) * inv21
    h22 = (with_w1 - h01 * h02 - h11 * h12) * inv21
    with_w0 = h00 * q0 + h10 * q1
    square = qq + h01 * h01 * square0 + h11 * h11 * g2
    square = square - 2.0 * (h01 * with_w0 + h11 * qw - h01 * h11 * cross)
    square = square * inv21 * inv21
    h32 = jnp.sqrt(jnp.maximum(square - h02 * h02 - h12 * h12 - h22 * h22, 1e-7 * square))
    zero = jnp.zeros_like(beta)
    hess = [[h00, h01, h02], [h10, h11, h12], [zero, h21, h22], [zero, zero, h32]]
    y0, y1, y2 = least_squares(hess, beta)
    y2 = y2 * inv21
    y0 = y0 - y2 * h01
    y1 = y1 - y2 * h11
    update = y0 * s0[...] + y1 * s1[...] + y2 * s2[...]
    residual = x[...] - (y0 * w0[...] + y1 * w1[...] + y2 * w2[...])
    for e in range(ELEMS):
        for v in range(VARS):
            lanes = slice(v * NODES, (v + 1) * NODES)
            row = e * STRIDE + v
            update_ref[e : e + 1, lanes] = update[row : row + 1, :]
            residual_ref[e : e + 1, lanes] = residual[row : row + 1, :]


VMEM = pltpu.VMEM
SMEM = pltpu.SMEM


def shape_of(out):
    return out if isinstance(out, jax.ShapeDtypeStruct) else jax.ShapeDtypeStruct(out, F32)


def call(kernel, name, args, outs, smem=(), scratch=(), raw=()):
    return pl.pallas_call(
        kernel,
        name=name,
        out_shape=[shape_of(out) for out in outs],
        in_specs=[
            pl.BlockSpec()
            if i in raw
            else pl.BlockSpec(memory_space=SMEM if i in smem else VMEM)
            for i in range(len(args))
        ],
        out_specs=[pl.BlockSpec(memory_space=VMEM)] * len(outs),
        scratch_shapes=[VMEM(shape, F32) for shape in scratch],
        compiler_params=pltpu.CompilerParams(vmem_limit_bytes=32 * 1024 * 1024),
    )(*args)


def with_step(kernel, step):
    def run(*refs):
        kernel(step, *refs)

    return run


def body(
    right_side,
    mass,
    volume_jac,
    face_flux,
    face_visc,
    block_inverse,
    coarse_inverse,
    neighbours,
    orientation,
    bc_tags,
    coarse_group,
):
    t = {name: jnp.asarray(value) for name, value in tables().items()}
    n_pass, n_span = lax.axis_size("passage"), lax.axis_size("span")
    n_rad = lax.axis_size("radial")
    devices = n_pass * n_span * n_rad
    p, s, r = (lax.axis_index(a) for a in AXES)
    place = jnp.stack([p, s, r, (p * n_span + s) * n_rad + r]).astype(jnp.int32)
    ints = [neighbours, orientation, bc_tags, coarse_group[:, None], place[:, None]]
    ints = jnp.concatenate(ints, axis=1)
    volume_t = jnp.transpose(volume_jac, (1, 2, 0, 3))
    flux_t, visc_t = (jnp.transpose(a, (2, 3, 0, 1)) for a in (face_flux, face_visc))

    pass_a = [(i, i ^ 1) for i in range(n_pass)]
    pass_b = [(i, (i + 1 if i % 2 else i - 1) % n_pass) for i in range(n_pass)]
    span_a = [(i, i ^ 1) for i in range(n_span)]
    span_b = [(i, (i + 1 if i % 2 else i - 1) % n_span) for i in range(n_span)]
    rad = [(0, 1), (1, 0)]

    def exchange(sends):
        ways = (
            ("radial", rad),
            ("passage", pass_b),
            ("span", span_a),
            ("span", span_b),
            ("passage", pass_a),
        )
        return [lax.ppermute(x, axis, way) for x, (axis, way) in zip(sends, ways)]

    def span_rows(row):
        return [row] + [
            lax.ppermute(row, "span", [(i, i ^ k) for i in range(n_span)]) for k in (2, 3, 1)
        ]

    vec = (RW, NODES)
    grow = (RW, t["de"].shape[1])
    send = (STRIDE, 128)
    table_shape = (devices, 128)

    def half_floats(*shape):
        return jax.ShapeDtypeStruct(shape, jnp.bfloat16)

    (table,) = call(start_kernel, "start", (right_side,), [table_shape], raw=(0,))
    table = lax.all_to_all(table, AXES, 0, 0, tiled=True)
    x, massw, member, row = call(
        prepare_kernel,
        "prepare",
        (right_side, mass, ints, t["restrict"]),
        [vec, vec, (RW, WIDE), (1, WIDE)],
        smem=(2,),
        raw=(0, 1, 3),
    )
    rows = span_rows(row)
    pair = half_floats(2 * RW, 3 * 4 * RW)
    rem0, rem1, rem2, loc1, loc2, omask, vmat, cinv3, turned = call(
        setup_kernel,
        "setup",
        (
            ints,
            volume_t,
            flux_t,
            visc_t,
            block_inverse,
            t["rows"],
            t["tile"],
            t["colcode"],
            t["vtile"],
            t["vmask"],
            coarse_inverse,
        ),
        [
            pair,
            pair,
            half_floats(2 * RW, 3 * 2 * RW),
            pair,
            pair,
            (6 * RW, 8 * FACE),
            half_floats(RW, 9 * RW),
            half_floats(KC, 3 * KC),
            half_floats(*block_inverse.shape),
        ],
        smem=(0,),
        raw=tuple(range(1, 11)),
        scratch=[(24, 104), (6 * RW, 256)],
    )
    remote = (rem0, rem1, rem2, omask, t["lay"])
    near = (massw, vmat, loc1, loc2, omask, t["lay"])

    def local_part(vector, grown, step):
        return call(local_kernel, "local%d" % step, (vector, grown) + near, [vec])[0]

    coarse_tables = (cinv3, member, t["spread"])
    tail = (turned, t["own_lanes"], t["de"])
    basis, search, images, scalars = [], [], [], []
    coarse0 = None
    outs = [vec, grow] + [send] * 5
    for step in range(3):
        if step < 2:
            (coarse,) = call(coarse_kernel, "coarse%d" % step, (*rows, *coarse_tables), [vec])
        if step == 0:
            z, coarse0, scal, first, grown, *sends = call(
                first0_kernel,
                "first0",
                (ints, table, x, coarse) + tail,
                [vec, vec, (8, 128)] + outs,
                smem=(0,),
            )
            scalars.append(scal)
        elif step == 1:
            z, scal, first, grown, *sends = call(
                first1_kernel,
                "first1",
                (ints, table, images[0], coarse, basis[0], coarse0) + tail,
                [vec, (8, 128)] + outs,
                smem=(0,),
            )
            scalars.append(scal)
        else:
            z = images[1]
            (fine,) = call(blocks_kernel, "fine", (z, turned, t["own_lanes"]), [vec])
            first, grown, *sends = call(
                first2_kernel,
                "first2",
                (ints, *rows, fine, *coarse_tables, t["de"]),
                outs,
                smem=(0,),
            )
        basis.append(z)
        recv = exchange(sends)
        local = local_part(first, grown, step)
        direction, grown, *sends = call(
            with_step(second_kernel, step),
            "second%d" % step,
            (ints, z, first, local, *recv) + remote + tail,
            outs,
            smem=(0,),
        )
        search.append(direction)
        recv = exchange(sends)
        local = local_part(direction, grown, step)
        kernel = with_step(third_kernel, step)
        args = (local, *recv) + remote
        if step == 0:
            image, table, row = call(
                kernel,
                "third0",
                args + (member, t["restrict"], basis[0]),
                [vec, table_shape, (1, WIDE)],
            )
            table = lax.all_to_all(table, AXES, 0, 0, tiled=True)
            rows = span_rows(row)
        elif step == 1:
            image, row = call(kernel, "third1", args + (member, t["restrict"]), [vec, (1, WIDE)])
            rows = span_rows(row)
        else:
            image, table = call(kernel, "third2", args + tuple(basis), [vec, table_shape])
            table = lax.all_to_all(table, AXES, 0, 0, tiled=True)
        images.append(image)

    update, residual = call(
        final_kernel,
        "final",
        (table, *scalars, x, *search, *images),
        [right_side.shape] * 2,
    )
    return (update, residual)


def solution(mesh):
    rows = P(AXES, None)
    blocks = P(AXES, None, None)
    jac = P(AXES, None, None, None)
    in_specs = (
        rows,
        rows,
        jac,
        jac,
        jac,
        blocks,
        P("passage", "radial", None, None),
        rows,
        rows,
        rows,
        P(AXES),
    )
    return jax.shard_map(body, mesh=mesh, in_specs=in_specs, out_specs=(rows, rows), check_vma=False)
```

```python
import math

import jax
import jax.numpy as jnp
import numpy as np
from jax import lax
from jax.experimental import pallas as pl
from jax.experimental.pallas import tpu as pltpu
from jax.sharding import PartitionSpec as P

QN = 4
VARS = 5
CG = 4
ELEMS = 4
NODES = QN**3
ROWS = 320
KC = 160
STRIDE = 8
RW = ELEMS * STRIDE
FACE = QN * QN
SOURCES = ((0, 1), (2, 3, 5, 6), (4, 7, 8))
WIDE = 256
AXES = ("passage", "span", "radial")
NEIGH, ORIENT, TAGS, GROUP, PLACE = 0, 6, 12, 18, 19
HIGHEST = lax.Precision.HIGHEST
GROWN = 3 * NODES + 6 * 2 * FACE
LAID = 6 * 8 * FACE
CONSTS = ((0, 80, 256), (80, 8, 256), (88, 8, 256), (96, 24, 96), (120, 32, 96), (152, 32, 24))
F32 = jnp.float32


def lobatto_nodes():
    inner_node = 1.0 / math.sqrt(5.0)
    return np.array([-1.0, -inner_node, inner_node, 1.0])


def derivative_table():
    nodes = lobatto_nodes()
    weights = np.ones(QN)
    for row_id in range(QN):
        for col_id in range(QN):
            if col_id != row_id:
                weights[row_id] = weights[row_id] / (nodes[row_id] - nodes[col_id])
    result = np.zeros((QN, QN))
    for row_id in range(QN):
        for col_id in range(QN):
            if col_id != row_id:
                result[row_id, col_id] = (
                    weights[col_id] / weights[row_id] / (nodes[row_id] - nodes[col_id])
                )
        result[row_id, row_id] = -np.sum(result[row_id])
    return result


def vertex_table():
    nodes = lobatto_nodes()
    shapes = np.stack([(1.0 - nodes) / 2.0, (1.0 + nodes) / 2.0])
    first_part = shapes[:, None, None, :, None, None]
    second_part = shapes[None, :, None, None, :, None]
    third_part = shapes[None, None, :, None, None, :]
    return (first_part * second_part * third_part).reshape(8, NODES)


def coords(node):
    return (node // 16, node // 4 % 4, node % 4)


def others(node, axis):
    picked = [c for i, c in enumerate(coords(node)) if i != axis]
    return picked[0] * QN + picked[1]


def layer_of(face):
    return 0 if face % 2 == 0 else QN - 1


def stacked(values):
    high = values.astype(jnp.bfloat16)
    low = (values - high.astype(np.float32)).astype(jnp.bfloat16)
    return np.concatenate([high, high, low], axis=0)


def tables():
    dmat = derivative_table()
    de = np.zeros((NODES, 3 * NODES + 6 * 2 * FACE), np.float32)
    place = np.zeros((6, 1, FACE, NODES), np.float32)
    for node in range(NODES):
        for axis in range(3):
            for target in range(NODES):
                if others(node, axis) == others(target, axis):
                    de[node, axis * NODES + target] = dmat[
                        coords(target)[axis], coords(node)[axis]
                    ]
        for face in range(6):
            axis = face // 2
            spot = others(node, axis)
            base = 3 * NODES + face * 2 * FACE
            de[node, base + FACE + spot] = dmat[layer_of(face), coords(node)[axis]]
            if coords(node)[axis] == layer_of(face):
                de[node, base + spot] = 1.0
                place[face, :, spot, node] = 1.0
    turn = np.zeros((FACE, 8, FACE), np.float32)
    for code in range(8):
        for i in range(QN):
            for j in range(QN):
                a = QN - 1 - i if code & 2 else i
                b = QN - 1 - j if code & 1 else j
                if code & 4:
                    a, b = b, a
                turn[a * QN + b, code, i * QN + j] = 1.0
    rtab = vertex_table().astype(np.float32)
    restrict = np.zeros((NODES, WIDE), np.float32)
    restrict[:, :KC] = np.tile(rtab.T, (1, CG * VARS))
    lay = np.einsum("aob,fbk->foak", turn, place[:, 0]).reshape(6 * 8 * FACE, NODES)
    tile = np.zeros((80, 256), np.float32)
    for col in range(256):
        kind, v = col // RW % 2, col % STRIDE
        if v < VARS:
            tile[kind * 40 + v * 8 : kind * 40 + v * 8 + 6, col] = 1.0
    code = np.full((8, 256), -100.0, np.float32)
    sign = np.ones((8, 256), np.float32)
    for face in range(6):
        axis = face // 2
        for place_id, source in enumerate(SOURCES[axis]):
            for col in range(2 * RW):
                kind, n, v = col // RW, col // STRIDE % ELEMS, col % STRIDE
                lane = place_id * 2 * RW + col
                code[face, lane] = source * ELEMS + n
                sign[face, lane] = (-1.0 if v == 1 + axis else 1.0) * (-1.0 if kind else 1.0)
    rows = np.zeros((RW, 24), np.float32)
    for e in range(ELEMS):
        for u in range(VARS):
            rows[e * STRIDE + u, u * ELEMS + e] = 1.0
    vtile = np.zeros((24, 3 * RW), np.float32)
    vmask = np.zeros((RW, 3 * RW), np.float32)
    for col in range(3 * RW):
        axis, n, v = col // RW, col // STRIDE % ELEMS, col % STRIDE
        if v < VARS:
            vtile[axis * 8 + v, col] = 1.0
        vmask[n * STRIDE : (n + 1) * STRIDE, col] = 1.0
    consts = np.zeros((184, 256), np.float32)
    for (row, count, lanes), part in zip(CONSTS, (tile, code, sign, vtile, vmask, rows)):
        consts[row : row + count, :lanes] = part
    return dict(
        consts=consts,
        rise=np.concatenate([stacked(de), stacked(restrict)], axis=1),
        lay=np.concatenate(
            [lay.astype(jnp.bfloat16), stacked(np.ascontiguousarray(restrict.T))], axis=0
        ),
    )


def exact_dot(a, b):
    return jnp.dot(a, b, precision=HIGHEST, preferred_element_type=F32)


def halves(values):
    high = values.astype(jnp.bfloat16)
    return high, (values - high.astype(F32)).astype(jnp.bfloat16)


def left_stack(values):
    high = values.astype(jnp.bfloat16).astype(F32)
    return jnp.concatenate([high, values - high, high], axis=1).astype(jnp.bfloat16)


def right_stack(values):
    high, low = halves(values)
    return jnp.concatenate([high, low, high], axis=0)


def dot(a, b):
    return jnp.dot(a, b, preferred_element_type=F32)


def total(values):
    return jnp.sum(values, axis=(0, 1), keepdims=True)


def member_mask(ints_ref):
    row = lax.broadcasted_iota(jnp.int32, (STRIDE, WIDE), 0)
    lane = lax.broadcasted_iota(jnp.int32, (STRIDE, WIDE), 1)
    pieces = []
    for e in range(ELEMS):
        hit = (lane // (VARS * 8) == ints_ref[e, GROUP]) & (lane // 8 % VARS == row)
        pieces.append(jnp.where(hit & (lane < KC), 1.0, 0.0))
    return jnp.concatenate(pieces, axis=0)


def coarse_row(member, rise_ref, vector):
    return jnp.sum(member * dot(left_stack(vector), rise_ref[:, GROWN:]), axis=0, keepdims=True)


def scalar_row(scalars):
    lane = lax.broadcasted_iota(jnp.int32, (1, 128), 1)
    row = jnp.zeros((1, 128), F32)
    for i, value in enumerate(scalars):
        row = jnp.where(lane == i, value, row)
    return row


def read_scalars(table_ref, count):
    sums = jnp.sum(table_ref[...], axis=0, keepdims=True)
    return [sums[:, i : i + 1] for i in range(count)]


def coarse_values(coarse, cinv_ref, member_ref, lay_ref):
    solved = dot(left_stack(coarse[:, :KC]), cinv_ref[...])
    solved = jnp.concatenate([solved, jnp.zeros((1, WIDE - KC), F32)], axis=1)
    return dot(left_stack(member_ref[...] * solved), lay_ref[LAID:, :])


def apply_blocks(turned_ref, parts):
    row = lax.broadcasted_iota(jnp.int32, (RW, ROWS), 0) % STRIDE
    own_lanes = lax.broadcasted_iota(jnp.int32, (RW, ROWS), 1) // NODES == row
    stacked = []
    for part in parts:
        pair = jnp.concatenate([part, part], axis=1)
        stacked.append(jnp.where(own_lanes, jnp.concatenate([pair, pair, part], axis=1), 0.0))
    pieces = []
    for e in range(ELEMS):
        rows = [part[e * STRIDE : (e + 1) * STRIDE] for part in stacked]
        rows = jnp.concatenate(rows, axis=0) if len(rows) > 1 else rows[0]
        out = dot(rows.astype(jnp.bfloat16), turned_ref[e])
        pieces.append(jnp.broadcast_to(jnp.sum(out, axis=0, keepdims=True), (STRIDE, ROWS)))
    full = jnp.where(own_lanes, jnp.concatenate(pieces, axis=0), 0.0)
    half = full[:, :128] + full[:, 128:256]
    return half[:, :NODES] + half[:, NODES:] + full[:, 256:]


def rounded(values):
    return [values.astype(jnp.bfloat16).astype(F32)]


def two_parts(values):
    high = values.astype(jnp.bfloat16).astype(F32)
    return [high, values - high]


def face_of(grown, face):
    base = 3 * NODES + face * 2 * FACE
    return grown[:, base : base + 2 * FACE]


def pack(grown, face):
    values = face_of(grown, face)
    rows = [values[e * STRIDE : (e + 1) * STRIDE] for e in range(ELEMS)]
    return jnp.concatenate(rows, axis=1)


def copies(tile, slot):
    lane = lax.broadcasted_iota(jnp.int32, tile.shape, 1)
    values = jnp.where(lane // FACE == slot, tile, 0.0)
    for shift in (FACE, 2 * FACE, 4 * FACE):
        values = values + pltpu.roll(values, shift, 1)
    return values


def unpack(tile):
    slot = lax.broadcasted_iota(jnp.int32, tile.shape, 1) // FACE
    level = [tile]
    for bit in (1, 2, 4):
        upper = slot & bit != 0
        without = [jnp.where(upper, pltpu.roll(a, bit * FACE, 1), a) for a in level]
        only = [jnp.where(upper, a, pltpu.roll(a, 128 - bit * FACE, 1)) for a in level]
        level = without + only
    return [level[e * 2 + kind] for kind in range(2) for e in range(ELEMS)]


def write_sends(odd_ref, grown, send_refs):
    p_odd, s_odd, r = (odd_ref[i * STRIDE : (i + 1) * STRIDE, :] > 0.5 for i in range(3))
    faces = [pack(grown, f) for f in range(6)]
    send_refs[0][...] = jnp.where(r, faces[4], faces[5])
    send_refs[1][...] = jnp.where(p_odd, faces[1], faces[0])
    send_refs[2][...] = jnp.where(s_odd, faces[2], faces[3])
    send_refs[3][...] = jnp.where(s_odd, faces[3], faces[2])
    send_refs[4][...] = jnp.where(p_odd, faces[0], faces[1])


def place_terms(groups, omask_ref, lay_ref, first_face):
    laid = []
    for i, terms in enumerate(groups):
        base = (first_face + 2 * i) * RW
        terms = terms * omask_ref[base : base + 2 * RW, :]
        laid += [terms[:RW], terms[RW:]]
    laid = jnp.concatenate(laid, axis=1)
    high, low = halves(laid)
    out = dot(jnp.concatenate([high, low], axis=0), lay_ref[first_face * 8 * FACE : LAID, :])
    return out[:RW] + out[RW:]


def halo_part(recv, rem, omask_ref, lay_ref):
    rad, pass_b, span_a, span_b, pass_a = [unpack(r[...]) for r in recv]
    groups = []
    for pieces, mat in ((pass_a + pass_b, rem[0]), (span_a + span_b, rem[1]), (rad, rem[2])):
        groups.append(dot(mat[...], right_stack(jnp.concatenate(pieces, axis=0))))
    return place_terms(groups, omask_ref, lay_ref, 0)


def start_kernel(rs_ref, table_ref):
    rs = rs_ref[...]
    table_ref[...] = jnp.broadcast_to(scalar_row([total(rs * rs)]), table_ref.shape)


def prepare_kernel(rs_ref, mass_ref, ints_ref, rise_ref, x_ref, massw_ref, member_ref, odd_ref, row_ref):
    x_ref[...] = jnp.zeros_like(x_ref)
    massw_ref[...] = jnp.zeros_like(massw_ref)
    for e in range(ELEMS):
        for v in range(VARS):
            lanes = slice(v * NODES, (v + 1) * NODES)
            row = e * STRIDE + v
            x_ref[row : row + 1, :] = rs_ref[e : e + 1, lanes]
            massw_ref[row : row + 1, :] = mass_ref[e : e + 1, lanes]
    member = member_mask(ints_ref)
    member_ref[...] = member
    row_ref[...] = coarse_row(member, rise_ref, x_ref[...])
    for i in range(3):
        odd = (ints_ref[i, PLACE] % 2).astype(F32)
        odd_ref[i * STRIDE : (i + 1) * STRIDE, :] = jnp.full((STRIDE, 128), odd, F32)


def setup_kernel(
    ints_ref,
    volume_ref,
    flux_ref,
    visc_ref,
    blocks_ref,
    consts_ref,
    cinv_ref,
    rem0_ref,
    rem1_ref,
    rem2_ref,
    loc1_ref,
    loc2_ref,
    omask_ref,
    vmat_ref,
    cinv3_ref,
    turned_ref,
    coef_ref,
    amat_ref,
):
    p_odd, s_odd = ints_ref[0, PLACE] % 2, ints_ref[1, PLACE] % 2
    device = ints_ref[3, PLACE]
    coef_ref[...] = jnp.zeros_like(coef_ref)
    for u in range(VARS):
        here = slice(u * ELEMS, (u + 1) * ELEMS)
        for axis in range(3):
            coef_ref[here, 80 + axis * 8 : 80 + axis * 8 + VARS] = volume_ref[axis, u]
        for v in range(VARS):
            coef_ref[here, v * 8 : v * 8 + 6] = flux_ref[u, v]
            coef_ref[here, 40 + v * 8 : 40 + v * 8 + 6] = visc_ref[u, v]
    tile, codes, wall_signs, vtile, vmask, expand = (
        consts_ref[a : a + n, :lanes] for a, n, lanes in CONSTS
    )
    coef = exact_dot(expand, coef_ref[...])
    vmat_ref[...] = right_factor(exact_dot(coef[:, 80:104], vtile) * vmask)
    turned = cinv_ref[0, 0].T
    high, low = halves(turned)
    cinv3_ref[...] = jnp.concatenate([high, high, low], axis=0)
    for e in range(ELEMS):
        turned_ref[e] = blocks_ref[e].T
    face_lane = lax.broadcasted_iota(jnp.int32, (RW, 80), 1) % 8
    coef = [jnp.where(face_lane == f, coef[:, :80], 0.0) for f in range(6)]
    spread = exact_dot(jnp.concatenate(coef, axis=0), tile)
    lane = lax.broadcasted_iota(jnp.int32, (STRIDE, 8 * FACE), 1)
    for f in range(6):
        colcode = jnp.broadcast_to(codes[f : f + 1], (STRIDE, 256))
        signs = jnp.broadcast_to(wall_signs[f : f + 1], (STRIDE, 256))
        for e in range(ELEMS):
            near = ints_ref[e, NEIGH + f]
            tag = ints_ref[e, TAGS + f]
            spot = near % ELEMS
            crossing = near // ELEMS != device
            if f == 0:
                source = 1 - p_odd
            elif f == 1:
                source = p_odd
            elif f == 2:
                source = 3 - s_odd
            elif f == 3:
                source = 2 + s_odd
            else:
                source = jnp.where(crossing, 4, 8 if f == 4 else 7)
            code = source * ELEMS + spot
            turn_code = ints_ref[e, ORIENT + f]
            if f >= 2:
                wall_code = (5 + f - 2) * ELEMS + e
                code = jnp.where(tag == 0, code, jnp.where(tag == 1, wall_code, -1))
                turn_code = jnp.where(tag == 0, turn_code, 0)
            rows = slice(f * RW + e * STRIDE, f * RW + (e + 1) * STRIDE)
            values = spread[rows]
            values = jnp.where(tag == 1, values * signs, values)
            amat_ref[rows, :] = jnp.where(colcode == code.astype(F32), -values, 0.0)
            omask_ref[rows, :] = jnp.where(lane // FACE == turn_code, 1.0, 0.0)
    one = 2 * RW
    rem0_ref[...] = right_factor(amat_ref[:one, : 2 * one])
    rem1_ref[...] = right_factor(amat_ref[one : 2 * one, : 2 * one])
    loc1_ref[...] = right_factor(amat_ref[one : 2 * one, 2 * one : 4 * one])
    rem2_ref[...] = right_factor(amat_ref[2 * one :, :one])
    loc2_ref[...] = right_factor(amat_ref[2 * one :, one : 3 * one])


def right_factor(values):
    high = values.astype(jnp.bfloat16).astype(F32)
    return jnp.concatenate([high, high, values - high], axis=1).astype(jnp.bfloat16)


def coarse_kernel(r0, r1, r2, r3, cinv, member, lay, coarse_ref):
    coarse = (r0[...] + r1[...]) + (r2[...] + r3[...])
    coarse_ref[...] = coarse_values(coarse, cinv, member, lay)


def blocks_kernel(x, blocks, out_ref):
    out_ref[...] = apply_blocks(blocks, two_parts(x[...]))


def finish_first(odd, first, rise, first_ref, grown_ref, sends):
    first_ref[...] = first
    grown = dot(left_stack(first), rise[:, :GROWN])
    grown_ref[...] = grown
    write_sends(odd, grown, sends)


def first0_kernel(odd, table, x, coarse, blocks, rise, *outs):
    z_ref, coarse_ref, scal_ref, first_ref, grown_ref, *sends = outs
    beta = jnp.sqrt(read_scalars(table, 1)[0])
    z = x[...] / beta
    z_ref[...] = z
    scal_ref[...] = jnp.broadcast_to(beta, scal_ref.shape)
    scaled = coarse[...] / beta
    coarse_ref[...] = scaled
    first = apply_blocks(blocks, rounded(z)) + scaled
    finish_first(odd, first, rise, first_ref, grown_ref, sends)


def first1_kernel(odd, table, x, coarse, b0, coarse0, blocks, rise, *outs):
    z_ref, scal_ref, first_ref, grown_ref, *sends = outs
    h00, square = read_scalars(table, 2)
    h10 = jnp.sqrt(jnp.maximum(square - h00 * h00, 1e-7 * square))
    z = (x[...] - h00 * b0[...]) / h10
    z_ref[...] = z
    row = lax.broadcasted_iota(jnp.int32, scal_ref.shape, 0)
    scal_ref[...] = jnp.where(row == 0, h00, jnp.where(row == 1, h10, square))
    scaled = (coarse[...] - h00 * coarse0[...]) / h10
    first = apply_blocks(blocks, rounded(z)) + scaled
    finish_first(odd, first, rise, first_ref, grown_ref, sends)


def first2_kernel(odd, r0, r1, r2, r3, fine, cinv, member, lay, rise, *outs):
    first_ref, grown_ref, *sends = outs
    coarse = (r0[...] + r1[...]) + (r2[...] + r3[...])
    first = fine[...] + coarse_values(coarse, cinv, member, lay)
    finish_first(odd, first, rise, first_ref, grown_ref, sends)


def local_kernel(x, grown_ref, mass, vmat, loc1, loc2, omask, lay, out_ref):
    grown = grown_ref[...]
    slopes = jnp.concatenate([grown[:, i * NODES : (i + 1) * NODES] for i in range(3)], axis=0)
    result = 1.5 * mass[...] * x[...] + dot(vmat[...], right_stack(slopes))
    groups = []
    for faces, mat in (((2, 3), loc1), ((4, 5), loc2)):
        pieces = []
        for f in faces:
            base = 3 * NODES + f * 2 * FACE
            tile = grown[:, base // 128 * 128 : base // 128 * 128 + 128]
            slot = base % 128 // FACE
            pieces += [copies(tile, slot), copies(tile, slot + 1)]
        groups.append(dot(mat[...], right_stack(jnp.concatenate(pieces, axis=0))))
    out_ref[...] = result + place_terms(groups, omask, lay, 2)


def second_kernel(step, *refs):
    odd, z, first, local = refs[:4]
    recv = refs[4:9]
    rem, omask, lay, blocks, rise = refs[9:12], *refs[12:16]
    search_ref, grown_ref, *sends = refs[16:]
    defect = z[...] - (local[...] + halo_part(recv, rem, omask, lay))
    parts = two_parts(defect) if step == 2 else rounded(defect)
    search = first[...] + apply_blocks(blocks, parts)
    search_ref[...] = search
    grown = dot(left_stack(search), rise[:, :GROWN])
    grown_ref[...] = grown
    write_sends(odd, grown, sends)


def third_kernel(step, *refs):
    local = refs[0]
    recv = refs[1:6]
    rem, omask, lay = refs[6:9], refs[9], refs[10]
    mapped = local[...] + halo_part(recv, rem, omask, lay)
    if step == 0:
        member, rise, b0, w_ref, table_ref, row_ref = refs[11:]
        scalars = [total(mapped * b0[...]), total(mapped * mapped)]
    elif step == 1:
        member, rise, w_ref, row_ref = refs[11:]
    else:
        b0, b1, w1, w_ref, table_ref = refs[11:]
        scalars = [total(w1[...] * b[...]) for b in (b0, b1, w1)]
        scalars += [total(mapped * b[...]) for b in (b0, b1, w1)]
        scalars += [total(mapped * mapped)]
    w_ref[...] = mapped
    if step != 1:
        table_ref[...] = jnp.broadcast_to(scalar_row(scalars), table_ref.shape)
    if step != 2:
        row_ref[...] = coarse_row(member[...], rise, mapped)


def inverse_sqrt(value):
    guess = lax.rsqrt(value)
    return guess * (1.5 - 0.5 * (value * guess) * guess)


def least_squares(matrix, beta):
    iters = len(matrix) - 1
    target = [beta] + [jnp.zeros_like(beta)] * iters
    inverse = []
    for k in range(iters):
        top, low = matrix[k][k], matrix[k + 1][k]
        scale = inverse_sqrt(top * top + low * low)
        inverse.append(scale)
        cosine, sine = top * scale, low * scale
        for later in range(k + 1, iters):
            upper, lower = matrix[k][later], matrix[k + 1][later]
            matrix[k][later] = cosine * upper + sine * lower
            matrix[k + 1][later] = -sine * upper + cosine * lower
        upper, lower = target[k], target[k + 1]
        target[k] = cosine * upper + sine * lower
        target[k + 1] = -sine * upper + cosine * lower
    weights = [None] * iters
    for k in reversed(range(iters)):
        value = target[k]
        for later in range(k + 1, iters):
            value = value - matrix[k][later] * weights[later]
        weights[k] = value * inverse[k]
    return weights


def final_kernel(table, scal0, scal1, x, s0, s1, s2, w0, w1, w2, update_ref, residual_ref):
    sums = jnp.sum(table[...], axis=0, keepdims=True)
    g0, g1, g2, q0, q1, qw, qq = [sums[:, i : i + 1] for i in range(7)]
    beta = scal0[0:1, 0:1]
    h00, h10, square0 = [scal1[i : i + 1, 0:1] for i in range(3)]
    h01, h11 = g0, g1
    squared = jnp.maximum(g2 - h01 * h01 - h11 * h11, 1e-7 * g2)
    inv21 = inverse_sqrt(squared)
    h21 = squared * inv21
    cross = h00 * h01 + h10 * h11
    h02 = (q0 - h01 * h00 - h11 * h01) * inv21
    h12 = (q1 - h01 * h10 - h11 * h11) * inv21
    with_w1 = (qw - h01 * cross - h11 * g2) * inv21
    h22 = (with_w1 - h01 * h02 - h11 * h12) * inv21
    with_w0 = h00 * q0 + h10 * q1
    square = qq + h01 * h01 * square0 + h11 * h11 * g2
    square = square - 2.0 * (h01 * with_w0 + h11 * qw - h01 * h11 * cross)
    square = square * inv21 * inv21
    h32 = jnp.sqrt(jnp.maximum(square - h02 * h02 - h12 * h12 - h22 * h22, 1e-7 * square))
    zero = jnp.zeros_like(beta)
    hess = [[h00, h01, h02], [h10, h11, h12], [zero, h21, h22], [zero, zero, h32]]
    y0, y1, y2 = least_squares(hess, beta)
    y2 = y2 * inv21
    y0 = y0 - y2 * h01
    y1 = y1 - y2 * h11
    update = y0 * s0[...] + y1 * s1[...] + y2 * s2[...]
    residual = x[...] - (y0 * w0[...] + y1 * w1[...] + y2 * w2[...])
    for e in range(ELEMS):
        for v in range(VARS):
            lanes = slice(v * NODES, (v + 1) * NODES)
            row = e * STRIDE + v
            update_ref[e : e + 1, lanes] = update[row : row + 1, :]
            residual_ref[e : e + 1, lanes] = residual[row : row + 1, :]


VMEM = pltpu.VMEM
SMEM = pltpu.SMEM


def shape_of(out):
    return out if isinstance(out, jax.ShapeDtypeStruct) else jax.ShapeDtypeStruct(out, F32)


def call(kernel, name, args, outs, smem=(), scratch=(), raw=()):
    return pl.pallas_call(
        kernel,
        name=name,
        out_shape=[shape_of(out) for out in outs],
        in_specs=[
            pl.BlockSpec()
            if i in raw
            else pl.BlockSpec(memory_space=SMEM if i in smem else VMEM)
            for i in range(len(args))
        ],
        out_specs=[pl.BlockSpec(memory_space=VMEM)] * len(outs),
        scratch_shapes=[VMEM(shape, F32) for shape in scratch],
        compiler_params=pltpu.CompilerParams(vmem_limit_bytes=32 * 1024 * 1024),
    )(*args)


def with_step(kernel, step):
    def run(*refs):
        kernel(step, *refs)

    return run


def body(
    right_side,
    mass,
    volume_jac,
    face_flux,
    face_visc,
    block_inverse,
    coarse_inverse,
    neighbours,
    orientation,
    bc_tags,
    coarse_group,
):
    t = {name: jnp.asarray(value) for name, value in tables().items()}
    n_pass, n_span = lax.axis_size("passage"), lax.axis_size("span")
    n_rad = lax.axis_size("radial")
    devices = n_pass * n_span * n_rad
    p, s, r = (lax.axis_index(a) for a in AXES)
    place = jnp.stack([p, s, r, (p * n_span + s) * n_rad + r]).astype(jnp.int32)
    ints = [neighbours, orientation, bc_tags, coarse_group[:, None], place[:, None]]
    ints = jnp.concatenate(ints, axis=1)
    volume_t = jnp.transpose(volume_jac, (1, 2, 0, 3))
    flux_t, visc_t = (jnp.transpose(a, (2, 3, 0, 1)) for a in (face_flux, face_visc))

    pass_a = [(i, i ^ 1) for i in range(n_pass)]
    pass_b = [(i, (i + 1 if i % 2 else i - 1) % n_pass) for i in range(n_pass)]
    span_a = [(i, i ^ 1) for i in range(n_span)]
    span_b = [(i, (i + 1 if i % 2 else i - 1) % n_span) for i in range(n_span)]
    rad = [(0, 1), (1, 0)]

    def exchange(sends):
        ways = (
            ("radial", rad),
            ("passage", pass_b),
            ("span", span_a),
            ("span", span_b),
            ("passage", pass_a),
        )
        return [lax.ppermute(x, axis, way) for x, (axis, way) in zip(sends, ways)]

    def span_rows(row):
        return [row] + [
            lax.ppermute(row, "span", [(i, i ^ k) for i in range(n_span)]) for k in (2, 3, 1)
        ]

    vec = (RW, NODES)
    grow = (RW, GROWN)
    send = (STRIDE, 128)
    table_shape = (devices, 128)

    def half_floats(*shape):
        return jax.ShapeDtypeStruct(shape, jnp.bfloat16)

    (table,) = call(start_kernel, "start", (right_side,), [table_shape], raw=(0,))
    table = lax.all_to_all(table, AXES, 0, 0, tiled=True)
    x, massw, member, odd, row = call(
        prepare_kernel,
        "prepare",
        (right_side, mass, ints, t["rise"]),
        [vec, vec, (RW, WIDE), (3 * STRIDE, 128), (1, WIDE)],
        smem=(2,),
        raw=(0, 1, 3),
    )
    rows = span_rows(row)
    pair = half_floats(2 * RW, 3 * 4 * RW)
    rem0, rem1, rem2, loc1, loc2, omask, vmat, cinv3, turned = call(
        setup_kernel,
        "setup",
        (
            ints,
            volume_t,
            flux_t,
            visc_t,
            block_inverse,
            t["consts"],
            coarse_inverse,
        ),
        [
            pair,
            pair,
            half_floats(2 * RW, 3 * 2 * RW),
            pair,
            pair,
            (6 * RW, 8 * FACE),
            half_floats(RW, 9 * RW),
            half_floats(3 * KC, KC),
            half_floats(*block_inverse.shape),
        ],
        smem=(0,),
        raw=tuple(range(1, 7)),
        scratch=[(24, 104), (6 * RW, 256)],
    )
    remote = (rem0, rem1, rem2, omask, t["lay"])
    near = (massw, vmat, loc1, loc2, omask, t["lay"])

    def local_part(vector, grown, step):
        return call(local_kernel, "local%d" % step, (vector, grown) + near, [vec])[0]

    coarse_tables = (cinv3, member, t["lay"])
    tail = (turned, t["rise"])
    basis, search, images, scalars = [], [], [], []
    coarse0 = None
    outs = [vec, grow] + [send] * 5
    for step in range(3):
        if step < 2:
            (coarse,) = call(coarse_kernel, "coarse%d" % step, (*rows, *coarse_tables), [vec])
        if step == 0:
            z, coarse0, scal, first, grown, *sends = call(
                first0_kernel,
                "first0",
                (odd, table, x, coarse) + tail,
                [vec, vec, (8, 128)] + outs,
            )
            scalars.append(scal)
        elif step == 1:
            z, scal, first, grown, *sends = call(
                first1_kernel,
                "first1",
                (odd, table, images[0], coarse, basis[0], coarse0) + tail,
                [vec, (8, 128)] + outs,
            )
            scalars.append(scal)
        else:
            z = images[1]
            (fine,) = call(blocks_kernel, "fine", (z, turned), [vec])
            first, grown, *sends = call(
                first2_kernel,
                "first2",
                (odd, *rows, fine, *coarse_tables, t["rise"]),
                outs,
            )
        basis.append(z)
        recv = exchange(sends)
        local = local_part(first, grown, step)
        direction, grown, *sends = call(
            with_step(second_kernel, step),
            "second%d" % step,
            (odd, z, first, local, *recv) + remote + tail,
            outs,
        )
        search.append(direction)
        recv = exchange(sends)
        local = local_part(direction, grown, step)
        kernel = with_step(third_kernel, step)
        args = (local, *recv) + remote
        if step == 0:
            image, table, row = call(
                kernel,
                "third0",
                args + (member, t["rise"], basis[0]),
                [vec, table_shape, (1, WIDE)],
            )
            table = lax.all_to_all(table, AXES, 0, 0, tiled=True)
            rows = span_rows(row)
        elif step == 1:
            image, row = call(kernel, "third1", args + (member, t["rise"]), [vec, (1, WIDE)])
            rows = span_rows(row)
        else:
            image, table = call(kernel, "third2", args + tuple(basis), [vec, table_shape])
            table = lax.all_to_all(table, AXES, 0, 0, tiled=True)
        images.append(image)

    update, residual = call(
        final_kernel,
        "final",
        (table, *scalars, x, *search, *images),
        [right_side.shape] * 2,
    )
    return (update, residual)


def solution(mesh):
    rows = P(AXES, None)
    blocks = P(AXES, None, None)
    jac = P(AXES, None, None, None)
    in_specs = (
        rows,
        rows,
        jac,
        jac,
        jac,
        blocks,
        P("passage", "radial", None, None),
        rows,
        rows,
        rows,
        P(AXES),
    )
    return jax.shard_map(body, mesh=mesh, in_specs=in_specs, out_specs=(rows, rows), check_vma=False)
```

```python
import math

import jax
import jax.numpy as jnp
import numpy as np
from jax import lax
from jax.experimental import pallas as pl
from jax.experimental.pallas import tpu as pltpu
from jax.sharding import PartitionSpec as P

QN = 4
VARS = 5
CG = 4
ELEMS = 4
NODES = QN**3
ROWS = 320
KC = 160
STRIDE = 8
RW = ELEMS * STRIDE
FACE = QN * QN
SOURCES = ((0, 1), (2, 3, 5, 6), (4, 7, 8))
WIDE = 256
AXES = ("passage", "span", "radial")
NEIGH, ORIENT, TAGS, GROUP, PLACE = 0, 6, 12, 18, 19
HIGHEST = lax.Precision.HIGHEST
GROWN = 3 * NODES + 6 * 2 * FACE
LAID = 6 * 8 * FACE
CONSTS = ((0, 80, 256), (80, 8, 256), (88, 8, 256), (96, 24, 96), (120, 32, 96), (152, 32, 24))
F32 = jnp.float32


def lobatto_nodes():
    inner_node = 1.0 / math.sqrt(5.0)
    return np.array([-1.0, -inner_node, inner_node, 1.0])


def derivative_table():
    nodes = lobatto_nodes()
    weights = np.ones(QN)
    for row_id in range(QN):
        for col_id in range(QN):
            if col_id != row_id:
                weights[row_id] = weights[row_id] / (nodes[row_id] - nodes[col_id])
    result = np.zeros((QN, QN))
    for row_id in range(QN):
        for col_id in range(QN):
            if col_id != row_id:
                result[row_id, col_id] = (
                    weights[col_id] / weights[row_id] / (nodes[row_id] - nodes[col_id])
                )
        result[row_id, row_id] = -np.sum(result[row_id])
    return result


def vertex_table():
    nodes = lobatto_nodes()
    shapes = np.stack([(1.0 - nodes) / 2.0, (1.0 + nodes) / 2.0])
    first_part = shapes[:, None, None, :, None, None]
    second_part = shapes[None, :, None, None, :, None]
    third_part = shapes[None, None, :, None, None, :]
    return (first_part * second_part * third_part).reshape(8, NODES)


def coords(node):
    return (node // 16, node // 4 % 4, node % 4)


def others(node, axis):
    picked = [c for i, c in enumerate(coords(node)) if i != axis]
    return picked[0] * QN + picked[1]


def layer_of(face):
    return 0 if face % 2 == 0 else QN - 1


def stacked(values):
    high = values.astype(jnp.bfloat16)
    low = (values - high.astype(np.float32)).astype(jnp.bfloat16)
    return np.concatenate([high, high, low], axis=0)


def tables():
    dmat = derivative_table()
    de = np.zeros((NODES, 3 * NODES + 6 * 2 * FACE), np.float32)
    place = np.zeros((6, 1, FACE, NODES), np.float32)
    for node in range(NODES):
        for axis in range(3):
            for target in range(NODES):
                if others(node, axis) == others(target, axis):
                    de[node, axis * NODES + target] = dmat[
                        coords(target)[axis], coords(node)[axis]
                    ]
        for face in range(6):
            axis = face // 2
            spot = others(node, axis)
            base = 3 * NODES + face * 2 * FACE
            de[node, base + FACE + spot] = dmat[layer_of(face), coords(node)[axis]]
            if coords(node)[axis] == layer_of(face):
                de[node, base + spot] = 1.0
                place[face, :, spot, node] = 1.0
    turn = np.zeros((FACE, 8, FACE), np.float32)
    for code in range(8):
        for i in range(QN):
            for j in range(QN):
                a = QN - 1 - i if code & 2 else i
                b = QN - 1 - j if code & 1 else j
                if code & 4:
                    a, b = b, a
                turn[a * QN + b, code, i * QN + j] = 1.0
    rtab = vertex_table().astype(np.float32)
    restrict = np.zeros((NODES, WIDE), np.float32)
    restrict[:, :KC] = np.tile(rtab.T, (1, CG * VARS))
    lay = np.einsum("aob,fbk->foak", turn, place[:, 0]).reshape(6 * 8 * FACE, NODES)
    tile = np.zeros((80, 256), np.float32)
    for col in range(256):
        kind, v = col // RW % 2, col % STRIDE
        if v < VARS:
            tile[kind * 40 + v * 8 : kind * 40 + v * 8 + 6, col] = 1.0
    code = np.full((8, 256), -100.0, np.float32)
    sign = np.ones((8, 256), np.float32)
    for face in range(6):
        axis = face // 2
        for place_id, source in enumerate(SOURCES[axis]):
            for col in range(2 * RW):
                kind, n, v = col // RW, col // STRIDE % ELEMS, col % STRIDE
                lane = place_id * 2 * RW + col
                code[face, lane] = source * ELEMS + n
                sign[face, lane] = (-1.0 if v == 1 + axis else 1.0) * (-1.0 if kind else 1.0)
    rows = np.zeros((RW, 24), np.float32)
    for e in range(ELEMS):
        for u in range(VARS):
            rows[e * STRIDE + u, u * ELEMS + e] = 1.0
    vtile = np.zeros((24, 3 * RW), np.float32)
    vmask = np.zeros((RW, 3 * RW), np.float32)
    for col in range(3 * RW):
        axis, n, v = col // RW, col // STRIDE % ELEMS, col % STRIDE
        if v < VARS:
            vtile[axis * 8 + v, col] = 1.0
        vmask[n * STRIDE : (n + 1) * STRIDE, col] = 1.0
    consts = np.zeros((184, 256), np.float32)
    for (row, count, lanes), part in zip(CONSTS, (tile, code, sign, vtile, vmask, rows)):
        consts[row : row + count, :lanes] = part
    return dict(
        consts=consts,
        rise=np.concatenate([stacked(de), stacked(restrict)], axis=1),
        lay=np.concatenate(
            [lay.astype(jnp.bfloat16), stacked(np.ascontiguousarray(restrict.T))], axis=0
        ),
    )


def exact_dot(a, b):
    return jnp.dot(a, b, precision=HIGHEST, preferred_element_type=F32)


def halves(values):
    high = values.astype(jnp.bfloat16)
    return high, (values - high.astype(F32)).astype(jnp.bfloat16)


def left_stack(values):
    high = values.astype(jnp.bfloat16).astype(F32)
    return jnp.concatenate([high, values - high, high], axis=1).astype(jnp.bfloat16)


def right_stack(values):
    high, low = halves(values)
    return jnp.concatenate([high, low, high], axis=0)


def dot(a, b):
    return jnp.dot(a, b, preferred_element_type=F32)


def total(values):
    return jnp.sum(values, axis=(0, 1), keepdims=True)


def member_mask(ints_ref):
    row = lax.broadcasted_iota(jnp.int32, (STRIDE, WIDE), 0)
    lane = lax.broadcasted_iota(jnp.int32, (STRIDE, WIDE), 1)
    pieces = []
    for e in range(ELEMS):
        hit = (lane // (VARS * 8) == ints_ref[e, GROUP]) & (lane // 8 % VARS == row)
        pieces.append(jnp.where(hit & (lane < KC), 1.0, 0.0))
    return jnp.concatenate(pieces, axis=0)


def coarse_row(member, rise_ref, vector):
    return jnp.sum(member * dot(left_stack(vector), rise_ref[:, GROWN:]), axis=0, keepdims=True)


def scalar_row(scalars):
    lane = lax.broadcasted_iota(jnp.int32, (1, 128), 1)
    row = jnp.zeros((1, 128), F32)
    for i, value in enumerate(scalars):
        row = jnp.where(lane == i, value, row)
    return row


def read_scalars(table_ref, count):
    sums = jnp.sum(table_ref[...], axis=0, keepdims=True)
    return [jnp.broadcast_to(sums[:, i : i + 1], (1, 128)) for i in range(count)]


def coarse_values(coarse, cinv_ref, member_ref, lay_ref):
    solved = dot(left_stack(coarse[:, :KC]), cinv_ref[...])
    solved = jnp.concatenate([solved, jnp.zeros((1, WIDE - KC), F32)], axis=1)
    return dot(left_stack(member_ref[...] * solved), lay_ref[LAID:, :])


def apply_blocks(turned_ref, parts):
    row = lax.broadcasted_iota(jnp.int32, (RW, ROWS), 0) % STRIDE
    own_lanes = lax.broadcasted_iota(jnp.int32, (RW, ROWS), 1) // NODES == row
    stacked = []
    for part in parts:
        pair = jnp.concatenate([part, part], axis=1)
        stacked.append(jnp.where(own_lanes, jnp.concatenate([pair, pair, part], axis=1), 0.0))
    pieces = []
    for e in range(ELEMS):
        rows = [part[e * STRIDE : (e + 1) * STRIDE] for part in stacked]
        rows = jnp.concatenate(rows, axis=0) if len(rows) > 1 else rows[0]
        out = dot(rows.astype(jnp.bfloat16), turned_ref[e])
        pieces.append(jnp.broadcast_to(jnp.sum(out, axis=0, keepdims=True), (STRIDE, ROWS)))
    full = jnp.where(own_lanes, jnp.concatenate(pieces, axis=0), 0.0)
    half = full[:, :128] + full[:, 128:256]
    return half[:, :NODES] + half[:, NODES:] + full[:, 256:]


def rounded(values):
    return [values.astype(jnp.bfloat16).astype(F32)]


def two_parts(values):
    high = values.astype(jnp.bfloat16).astype(F32)
    return [high, values - high]


def face_of(grown, face):
    base = 3 * NODES + face * 2 * FACE
    return grown[:, base : base + 2 * FACE]


def pack(grown, face):
    values = face_of(grown, face)
    rows = [values[e * STRIDE : (e + 1) * STRIDE] for e in range(ELEMS)]
    return jnp.concatenate(rows, axis=1)


def copies(tile, slot):
    lane = lax.broadcasted_iota(jnp.int32, tile.shape, 1)
    values = jnp.where(lane // FACE == slot, tile, 0.0)
    for shift in (FACE, 2 * FACE, 4 * FACE):
        values = values + pltpu.roll(values, shift, 1)
    return values


def unpack(tile):
    slot = lax.broadcasted_iota(jnp.int32, tile.shape, 1) // FACE
    level = [tile]
    for bit in (1, 2, 4):
        upper = slot & bit != 0
        without = [jnp.where(upper, pltpu.roll(a, bit * FACE, 1), a) for a in level]
        only = [jnp.where(upper, a, pltpu.roll(a, 128 - bit * FACE, 1)) for a in level]
        level = without + only
    return [level[e * 2 + kind] for kind in range(2) for e in range(ELEMS)]


def write_sends(odd_ref, grown, send_refs):
    p_odd, s_odd, r = (odd_ref[i * STRIDE : (i + 1) * STRIDE, :] > 0.5 for i in range(3))
    faces = [pack(grown, f) for f in range(6)]
    send_refs[0][...] = jnp.where(r, faces[4], faces[5])
    send_refs[1][...] = jnp.where(p_odd, faces[1], faces[0])
    send_refs[2][...] = jnp.where(s_odd, faces[2], faces[3])
    send_refs[3][...] = jnp.where(s_odd, faces[3], faces[2])
    send_refs[4][...] = jnp.where(p_odd, faces[0], faces[1])


def place_terms(groups, omask_ref, lay_ref, first_face):
    laid = []
    for i, terms in enumerate(groups):
        base = (first_face + 2 * i) * RW
        terms = terms * omask_ref[base : base + 2 * RW, :]
        laid += [terms[:RW], terms[RW:]]
    laid = jnp.concatenate(laid, axis=1)
    high, low = halves(laid)
    out = dot(jnp.concatenate([high, low], axis=0), lay_ref[first_face * 8 * FACE : LAID, :])
    return out[:RW] + out[RW:]


def halo_part(recv, rem, omask_ref, lay_ref):
    rad, pass_b, span_a, span_b, pass_a = [unpack(r[...]) for r in recv]
    groups = []
    for pieces, mat in ((pass_a + pass_b, rem[0]), (span_a + span_b, rem[1]), (rad, rem[2])):
        groups.append(dot(mat[...], right_stack(jnp.concatenate(pieces, axis=0))))
    return place_terms(groups, omask_ref, lay_ref, 0)


def start_kernel(rs_ref, table_ref):
    rs = rs_ref[...]
    table_ref[...] = jnp.broadcast_to(scalar_row([total(rs * rs)]), table_ref.shape)


def prepare_kernel(rs_ref, mass_ref, ints_ref, rise_ref, x_ref, massw_ref, member_ref, odd_ref, row_ref):
    x_ref[...] = jnp.zeros_like(x_ref)
    massw_ref[...] = jnp.zeros_like(massw_ref)
    for e in range(ELEMS):
        for v in range(VARS):
            lanes = slice(v * NODES, (v + 1) * NODES)
            row = e * STRIDE + v
            x_ref[row : row + 1, :] = rs_ref[e : e + 1, lanes]
            massw_ref[row : row + 1, :] = mass_ref[e : e + 1, lanes]
    member = member_mask(ints_ref)
    member_ref[...] = member
    row_ref[...] = coarse_row(member, rise_ref, x_ref[...])
    for i in range(3):
        odd = (ints_ref[i, PLACE] % 2).astype(F32)
        odd_ref[i * STRIDE : (i + 1) * STRIDE, :] = jnp.full((STRIDE, 128), odd, F32)


def setup_kernel(
    ints_ref,
    volume_ref,
    flux_ref,
    visc_ref,
    blocks_ref,
    consts_ref,
    cinv_ref,
    rem0_ref,
    rem1_ref,
    rem2_ref,
    loc1_ref,
    loc2_ref,
    omask_ref,
    vmat_ref,
    cinv3_ref,
    turned_ref,
    coef_ref,
    amat_ref,
):
    p_odd, s_odd = ints_ref[0, PLACE] % 2, ints_ref[1, PLACE] % 2
    device = ints_ref[3, PLACE]
    coef_ref[...] = jnp.zeros_like(coef_ref)
    for u in range(VARS):
        here = slice(u * ELEMS, (u + 1) * ELEMS)
        for axis in range(3):
            coef_ref[here, 80 + axis * 8 : 80 + axis * 8 + VARS] = volume_ref[axis, u]
        for v in range(VARS):
            coef_ref[here, v * 8 : v * 8 + 6] = flux_ref[u, v]
            coef_ref[here, 40 + v * 8 : 40 + v * 8 + 6] = visc_ref[u, v]
    tile, codes, wall_signs, vtile, vmask, expand = (
        consts_ref[a : a + n, :lanes] for a, n, lanes in CONSTS
    )
    coef = exact_dot(expand, coef_ref[...])
    vmat_ref[...] = right_factor(exact_dot(coef[:, 80:104], vtile) * vmask)
    turned = cinv_ref[0, 0].T
    high, low = halves(turned)
    cinv3_ref[...] = jnp.concatenate([high, high, low], axis=0)
    for e in range(ELEMS):
        turned_ref[e] = blocks_ref[e].T
    face_lane = lax.broadcasted_iota(jnp.int32, (RW, 80), 1) % 8
    coef = [jnp.where(face_lane == f, coef[:, :80], 0.0) for f in range(6)]
    spread = exact_dot(jnp.concatenate(coef, axis=0), tile)
    lane = lax.broadcasted_iota(jnp.int32, (STRIDE, 8 * FACE), 1)
    for f in range(6):
        colcode = jnp.broadcast_to(codes[f : f + 1], (STRIDE, 256))
        signs = jnp.broadcast_to(wall_signs[f : f + 1], (STRIDE, 256))
        for e in range(ELEMS):
            near = ints_ref[e, NEIGH + f]
            tag = ints_ref[e, TAGS + f]
            spot = near % ELEMS
            crossing = near // ELEMS != device
            if f == 0:
                source = 1 - p_odd
            elif f == 1:
                source = p_odd
            elif f == 2:
                source = 3 - s_odd
            elif f == 3:
                source = 2 + s_odd
            else:
                source = jnp.where(crossing, 4, 8 if f == 4 else 7)
            code = source * ELEMS + spot
            turn_code = ints_ref[e, ORIENT + f]
            if f >= 2:
                wall_code = (5 + f - 2) * ELEMS + e
                code = jnp.where(tag == 0, code, jnp.where(tag == 1, wall_code, -1))
                turn_code = jnp.where(tag == 0, turn_code, 0)
            rows = slice(f * RW + e * STRIDE, f * RW + (e + 1) * STRIDE)
            values = spread[rows]
            values = jnp.where(tag == 1, values * signs, values)
            amat_ref[rows, :] = jnp.where(colcode == code.astype(F32), -values, 0.0)
            omask_ref[rows, :] = jnp.where(lane // FACE == turn_code, 1.0, 0.0)
    one = 2 * RW
    rem0_ref[...] = right_factor(amat_ref[:one, : 2 * one])
    rem1_ref[...] = right_factor(amat_ref[one : 2 * one, : 2 * one])
    loc1_ref[...] = right_factor(amat_ref[one : 2 * one, 2 * one : 4 * one])
    rem2_ref[...] = right_factor(amat_ref[2 * one :, :one])
    loc2_ref[...] = right_factor(amat_ref[2 * one :, one : 3 * one])


def right_factor(values):
    high = values.astype(jnp.bfloat16).astype(F32)
    return jnp.concatenate([high, high, values - high], axis=1).astype(jnp.bfloat16)


def coarse_kernel(r0, r1, r2, r3, cinv, member, lay, coarse_ref):
    coarse = (r0[...] + r1[...]) + (r2[...] + r3[...])
    coarse_ref[...] = coarse_values(coarse, cinv, member, lay)


def blocks_kernel(x, blocks, out_ref):
    out_ref[...] = apply_blocks(blocks, two_parts(x[...]))


def finish_first(odd, first, rise, first_ref, grown_ref, sends):
    first_ref[...] = first
    grown = dot(left_stack(first), rise[:, :GROWN])
    grown_ref[...] = grown
    write_sends(odd, grown, sends)


def first0_kernel(odd, table, x, coarse, blocks, rise, *outs):
    z_ref, coarse_ref, scal_ref, first_ref, grown_ref, *sends = outs
    beta = jnp.sqrt(read_scalars(table, 1)[0])
    z = x[...] / beta[:, :NODES]
    z_ref[...] = z
    scal_ref[...] = jnp.broadcast_to(beta, scal_ref.shape)
    scaled = coarse[...] / beta[:, :NODES]
    coarse_ref[...] = scaled
    first = apply_blocks(blocks, rounded(z)) + scaled
    finish_first(odd, first, rise, first_ref, grown_ref, sends)


def first1_kernel(odd, table, x, coarse, b0, coarse0, blocks, rise, *outs):
    z_ref, scal_ref, first_ref, grown_ref, *sends = outs
    h00, square = read_scalars(table, 2)
    h10 = jnp.sqrt(jnp.maximum(square - h00 * h00, 1e-7 * square))
    for i, value in enumerate((h00, h10, square)):
        scal_ref[i * STRIDE : (i + 1) * STRIDE, :] = jnp.broadcast_to(value, (STRIDE, 128))
    h00, h10 = h00[:, :NODES], h10[:, :NODES]
    z = (x[...] - h00 * b0[...]) / h10
    z_ref[...] = z
    scaled = (coarse[...] - h00 * coarse0[...]) / h10
    first = apply_blocks(blocks, rounded(z)) + scaled
    finish_first(odd, first, rise, first_ref, grown_ref, sends)


def first2_kernel(odd, r0, r1, r2, r3, fine, cinv, member, lay, rise, *outs):
    first_ref, grown_ref, *sends = outs
    coarse = (r0[...] + r1[...]) + (r2[...] + r3[...])
    first = fine[...] + coarse_values(coarse, cinv, member, lay)
    finish_first(odd, first, rise, first_ref, grown_ref, sends)


def local_kernel(x, grown_ref, mass, vmat, loc1, loc2, omask, lay, out_ref):
    grown = grown_ref[...]
    slopes = jnp.concatenate([grown[:, i * NODES : (i + 1) * NODES] for i in range(3)], axis=0)
    result = 1.5 * mass[...] * x[...] + dot(vmat[...], right_stack(slopes))
    groups = []
    for faces, mat in (((2, 3), loc1), ((4, 5), loc2)):
        pieces = []
        for f in faces:
            base = 3 * NODES + f * 2 * FACE
            tile = grown[:, base // 128 * 128 : base // 128 * 128 + 128]
            slot = base % 128 // FACE
            pieces += [copies(tile, slot), copies(tile, slot + 1)]
        groups.append(dot(mat[...], right_stack(jnp.concatenate(pieces, axis=0))))
    out_ref[...] = result + place_terms(groups, omask, lay, 2)


def second_kernel(step, *refs):
    odd, z, first, local = refs[:4]
    recv = refs[4:9]
    rem, omask, lay, blocks, rise = refs[9:12], *refs[12:16]
    search_ref, grown_ref, *sends = refs[16:]
    defect = z[...] - (local[...] + halo_part(recv, rem, omask, lay))
    parts = two_parts(defect) if step == 2 else rounded(defect)
    search = first[...] + apply_blocks(blocks, parts)
    search_ref[...] = search
    grown = dot(left_stack(search), rise[:, :GROWN])
    grown_ref[...] = grown
    write_sends(odd, grown, sends)


def third_kernel(step, *refs):
    local = refs[0]
    recv = refs[1:6]
    rem, omask, lay = refs[6:9], refs[9], refs[10]
    mapped = local[...] + halo_part(recv, rem, omask, lay)
    if step == 0:
        member, rise, b0, w_ref, table_ref, row_ref = refs[11:]
        scalars = [total(mapped * b0[...]), total(mapped * mapped)]
    elif step == 1:
        member, rise, w_ref, row_ref = refs[11:]
    else:
        b0, b1, w1, w_ref, table_ref = refs[11:]
        scalars = [total(w1[...] * b[...]) for b in (b0, b1, w1)]
        scalars += [total(mapped * b[...]) for b in (b0, b1, w1)]
        scalars += [total(mapped * mapped)]
    w_ref[...] = mapped
    if step != 1:
        table_ref[...] = jnp.broadcast_to(scalar_row(scalars), table_ref.shape)
    if step != 2:
        row_ref[...] = coarse_row(member[...], rise, mapped)


def inverse_sqrt(value):
    guess = lax.rsqrt(value)
    return guess * (1.5 - 0.5 * (value * guess) * guess)


def least_squares(matrix, beta):
    iters = len(matrix) - 1
    target = [beta] + [jnp.zeros_like(beta)] * iters
    inverse = []
    for k in range(iters):
        top, low = matrix[k][k], matrix[k + 1][k]
        scale = inverse_sqrt(top * top + low * low)
        inverse.append(scale)
        cosine, sine = top * scale, low * scale
        for later in range(k + 1, iters):
            upper, lower = matrix[k][later], matrix[k + 1][later]
            matrix[k][later] = cosine * upper + sine * lower
            matrix[k + 1][later] = -sine * upper + cosine * lower
        upper, lower = target[k], target[k + 1]
        target[k] = cosine * upper + sine * lower
        target[k + 1] = -sine * upper + cosine * lower
    weights = [None] * iters
    for k in reversed(range(iters)):
        value = target[k]
        for later in range(k + 1, iters):
            value = value - matrix[k][later] * weights[later]
        weights[k] = value * inverse[k]
    return weights


def final_kernel(table, scal0, scal1, x, s0, s1, s2, w0, w1, w2, update_ref, residual_ref):
    g0, g1, g2, q0, q1, qw, qq = read_scalars(table, 7)
    beta = scal0[0:1, :]
    h00, h10, square0 = [scal1[i * STRIDE : i * STRIDE + 1, :] for i in range(3)]
    h01, h11 = g0, g1
    squared = jnp.maximum(g2 - h01 * h01 - h11 * h11, 1e-7 * g2)
    inv21 = inverse_sqrt(squared)
    h21 = squared * inv21
    cross = h00 * h01 + h10 * h11
    h02 = (q0 - h01 * h00 - h11 * h01) * inv21
    h12 = (q1 - h01 * h10 - h11 * h11) * inv21
    with_w1 = (qw - h01 * cross - h11 * g2) * inv21
    h22 = (with_w1 - h01 * h02 - h11 * h12) * inv21
    with_w0 = h00 * q0 + h10 * q1
    square = qq + h01 * h01 * square0 + h11 * h11 * g2
    square = square - 2.0 * (h01 * with_w0 + h11 * qw - h01 * h11 * cross)
    square = square * inv21 * inv21
    h32 = jnp.sqrt(jnp.maximum(square - h02 * h02 - h12 * h12 - h22 * h22, 1e-7 * square))
    zero = jnp.zeros_like(beta)
    hess = [[h00, h01, h02], [h10, h11, h12], [zero, h21, h22], [zero, zero, h32]]
    y0, y1, y2 = least_squares(hess, beta)
    y2 = y2 * inv21
    y0 = y0 - y2 * h01
    y1 = y1 - y2 * h11
    y0, y1, y2 = (y[:, :NODES] for y in (y0, y1, y2))
    update = y0 * s0[...] + y1 * s1[...] + y2 * s2[...]
    residual = x[...] - (y0 * w0[...] + y1 * w1[...] + y2 * w2[...])
    for e in range(ELEMS):
        for v in range(VARS):
            lanes = slice(v * NODES, (v + 1) * NODES)
            row = e * STRIDE + v
            update_ref[e : e + 1, lanes] = update[row : row + 1, :]
            residual_ref[e : e + 1, lanes] = residual[row : row + 1, :]


VMEM = pltpu.VMEM
SMEM = pltpu.SMEM


def shape_of(out):
    return out if isinstance(out, jax.ShapeDtypeStruct) else jax.ShapeDtypeStruct(out, F32)


def call(kernel, name, args, outs, smem=(), scratch=(), raw=()):
    return pl.pallas_call(
        kernel,
        name=name,
        out_shape=[shape_of(out) for out in outs],
        in_specs=[
            pl.BlockSpec()
            if i in raw
            else pl.BlockSpec(memory_space=SMEM if i in smem else VMEM)
            for i in range(len(args))
        ],
        out_specs=[pl.BlockSpec(memory_space=VMEM)] * len(outs),
        scratch_shapes=[VMEM(shape, F32) for shape in scratch],
        compiler_params=pltpu.CompilerParams(vmem_limit_bytes=32 * 1024 * 1024),
    )(*args)


def with_step(kernel, step):
    def run(*refs):
        kernel(step, *refs)

    return run


def body(
    right_side,
    mass,
    volume_jac,
    face_flux,
    face_visc,
    block_inverse,
    coarse_inverse,
    neighbours,
    orientation,
    bc_tags,
    coarse_group,
):
    t = {name: jnp.asarray(value) for name, value in tables().items()}
    n_pass, n_span = lax.axis_size("passage"), lax.axis_size("span")
    n_rad = lax.axis_size("radial")
    devices = n_pass * n_span * n_rad
    p, s, r = (lax.axis_index(a) for a in AXES)
    place = jnp.stack([p, s, r, (p * n_span + s) * n_rad + r]).astype(jnp.int32)
    ints = [neighbours, orientation, bc_tags, coarse_group[:, None], place[:, None]]
    ints = jnp.concatenate(ints, axis=1)
    volume_t = jnp.transpose(volume_jac, (1, 2, 0, 3))
    flux_t, visc_t = (jnp.transpose(a, (2, 3, 0, 1)) for a in (face_flux, face_visc))

    pass_a = [(i, i ^ 1) for i in range(n_pass)]
    pass_b = [(i, (i + 1 if i % 2 else i - 1) % n_pass) for i in range(n_pass)]
    span_a = [(i, i ^ 1) for i in range(n_span)]
    span_b = [(i, (i + 1 if i % 2 else i - 1) % n_span) for i in range(n_span)]
    rad = [(0, 1), (1, 0)]

    def exchange(sends):
        ways = (
            ("radial", rad),
            ("passage", pass_b),
            ("span", span_a),
            ("span", span_b),
            ("passage", pass_a),
        )
        return [lax.ppermute(x, axis, way) for x, (axis, way) in zip(sends, ways)]

    def span_rows(row):
        return [row] + [
            lax.ppermute(row, "span", [(i, i ^ k) for i in range(n_span)]) for k in (2, 3, 1)
        ]

    vec = (RW, NODES)
    grow = (RW, GROWN)
    send = (STRIDE, 128)
    table_shape = (devices, 128)

    def half_floats(*shape):
        return jax.ShapeDtypeStruct(shape, jnp.bfloat16)

    (table,) = call(start_kernel, "start", (right_side,), [table_shape], raw=(0,))
    table = lax.all_to_all(table, AXES, 0, 0, tiled=True)
    x, massw, member, odd, row = call(
        prepare_kernel,
        "prepare",
        (right_side, mass, ints, t["rise"]),
        [vec, vec, (RW, WIDE), (3 * STRIDE, 128), (1, WIDE)],
        smem=(2,),
        raw=(0, 1, 3),
    )
    rows = span_rows(row)
    pair = half_floats(2 * RW, 3 * 4 * RW)
    rem0, rem1, rem2, loc1, loc2, omask, vmat, cinv3, turned = call(
        setup_kernel,
        "setup",
        (
            ints,
            volume_t,
            flux_t,
            visc_t,
            block_inverse,
            t["consts"],
            coarse_inverse,
        ),
        [
            pair,
            pair,
            half_floats(2 * RW, 3 * 2 * RW),
            pair,
            pair,
            (6 * RW, 8 * FACE),
            half_floats(RW, 9 * RW),
            half_floats(3 * KC, KC),
            half_floats(*block_inverse.shape),
        ],
        smem=(0,),
        raw=tuple(range(1, 7)),
        scratch=[(24, 104), (6 * RW, 256)],
    )
    remote = (rem0, rem1, rem2, omask, t["lay"])
    near = (massw, vmat, loc1, loc2, omask, t["lay"])

    def local_part(vector, grown, step):
        return call(local_kernel, "local%d" % step, (vector, grown) + near, [vec])[0]

    coarse_tables = (cinv3, member, t["lay"])
    tail = (turned, t["rise"])
    basis, search, images, scalars = [], [], [], []
    coarse0 = None
    outs = [vec, grow] + [send] * 5
    for step in range(3):
        if step < 2:
            (coarse,) = call(coarse_kernel, "coarse%d" % step, (*rows, *coarse_tables), [vec])
        if step == 0:
            z, coarse0, scal, first, grown, *sends = call(
                first0_kernel,
                "first0",
                (odd, table, x, coarse) + tail,
                [vec, vec, (8, 128)] + outs,
            )
            scalars.append(scal)
        elif step == 1:
            z, scal, first, grown, *sends = call(
                first1_kernel,
                "first1",
                (odd, table, images[0], coarse, basis[0], coarse0) + tail,
                [vec, (3 * STRIDE, 128)] + outs,
            )
            scalars.append(scal)
        else:
            z = images[1]
            (fine,) = call(blocks_kernel, "fine", (z, turned), [vec])
            first, grown, *sends = call(
                first2_kernel,
                "first2",
                (odd, *rows, fine, *coarse_tables, t["rise"]),
                outs,
            )
        basis.append(z)
        recv = exchange(sends)
        local = local_part(first, grown, step)
        direction, grown, *sends = call(
            with_step(second_kernel, step),
            "second%d" % step,
            (odd, z, first, local, *recv) + remote + tail,
            outs,
        )
        search.append(direction)
        recv = exchange(sends)
        local = local_part(direction, grown, step)
        kernel = with_step(third_kernel, step)
        args = (local, *recv) + remote
        if step == 0:
            image, table, row = call(
                kernel,
                "third0",
                args + (member, t["rise"], basis[0]),
                [vec, table_shape, (1, WIDE)],
            )
            table = lax.all_to_all(table, AXES, 0, 0, tiled=True)
            rows = span_rows(row)
        elif step == 1:
            image, row = call(kernel, "third1", args + (member, t["rise"]), [vec, (1, WIDE)])
            rows = span_rows(row)
        else:
            image, table = call(kernel, "third2", args + tuple(basis), [vec, table_shape])
            table = lax.all_to_all(table, AXES, 0, 0, tiled=True)
        images.append(image)

    update, residual = call(
        final_kernel,
        "final",
        (table, *scalars, x, *search, *images),
        [right_side.shape] * 2,
    )
    return (update, residual)


def solution(mesh):
    rows = P(AXES, None)
    blocks = P(AXES, None, None)
    jac = P(AXES, None, None, None)
    in_specs = (
        rows,
        rows,
        jac,
        jac,
        jac,
        blocks,
        P("passage", "radial", None, None),
        rows,
        rows,
        rows,
        P(AXES),
    )
    return jax.shard_map(body, mesh=mesh, in_specs=in_specs, out_specs=(rows, rows), check_vma=False)
```

```python
import math

import jax
import jax.numpy as jnp
import numpy as np
from jax import lax
from jax.experimental import pallas as pl
from jax.experimental.pallas import tpu as pltpu
from jax.sharding import PartitionSpec as P

QN = 4
VARS = 5
CG = 4
ELEMS = 4
NODES = QN**3
ROWS = 320
KC = 160
STRIDE = 8
RW = ELEMS * STRIDE
FACE = QN * QN
SOURCES = ((0, 1), (2, 3, 5, 6), (4, 7, 8))
WIDE = 256
AXES = ("passage", "span", "radial")
NEIGH, ORIENT, TAGS, GROUP, PLACE = 0, 6, 12, 18, 19
HIGHEST = lax.Precision.HIGHEST
GROWN = 3 * NODES + 6 * 2 * FACE
LAID = 6 * 8 * FACE
CONSTS = ((0, 80, 256), (80, 8, 256), (88, 8, 256), (96, 24, 96), (120, 32, 96), (152, 32, 24))
F32 = jnp.float32


def lobatto_nodes():
    inner_node = 1.0 / math.sqrt(5.0)
    return np.array([-1.0, -inner_node, inner_node, 1.0])


def derivative_table():
    nodes = lobatto_nodes()
    weights = np.ones(QN)
    for row_id in range(QN):
        for col_id in range(QN):
            if col_id != row_id:
                weights[row_id] = weights[row_id] / (nodes[row_id] - nodes[col_id])
    result = np.zeros((QN, QN))
    for row_id in range(QN):
        for col_id in range(QN):
            if col_id != row_id:
                result[row_id, col_id] = (
                    weights[col_id] / weights[row_id] / (nodes[row_id] - nodes[col_id])
                )
        result[row_id, row_id] = -np.sum(result[row_id])
    return result


def vertex_table():
    nodes = lobatto_nodes()
    shapes = np.stack([(1.0 - nodes) / 2.0, (1.0 + nodes) / 2.0])
    first_part = shapes[:, None, None, :, None, None]
    second_part = shapes[None, :, None, None, :, None]
    third_part = shapes[None, None, :, None, None, :]
    return (first_part * second_part * third_part).reshape(8, NODES)


def coords(node):
    return (node // 16, node // 4 % 4, node % 4)


def others(node, axis):
    picked = [c for i, c in enumerate(coords(node)) if i != axis]
    return picked[0] * QN + picked[1]


def layer_of(face):
    return 0 if face % 2 == 0 else QN - 1


def stacked(values):
    high = values.astype(jnp.bfloat16)
    low = (values - high.astype(np.float32)).astype(jnp.bfloat16)
    return np.concatenate([high, high, low], axis=0)


def tables():
    dmat = derivative_table()
    de = np.zeros((NODES, 3 * NODES + 6 * 2 * FACE), np.float32)
    place = np.zeros((6, 1, FACE, NODES), np.float32)
    for node in range(NODES):
        for axis in range(3):
            for target in range(NODES):
                if others(node, axis) == others(target, axis):
                    de[node, axis * NODES + target] = dmat[
                        coords(target)[axis], coords(node)[axis]
                    ]
        for face in range(6):
            axis = face // 2
            spot = others(node, axis)
            base = 3 * NODES + face * 2 * FACE
            de[node, base + FACE + spot] = dmat[layer_of(face), coords(node)[axis]]
            if coords(node)[axis] == layer_of(face):
                de[node, base + spot] = 1.0
                place[face, :, spot, node] = 1.0
    turn = np.zeros((FACE, 8, FACE), np.float32)
    for code in range(8):
        for i in range(QN):
            for j in range(QN):
                a = QN - 1 - i if code & 2 else i
                b = QN - 1 - j if code & 1 else j
                if code & 4:
                    a, b = b, a
                turn[a * QN + b, code, i * QN + j] = 1.0
    rtab = vertex_table().astype(np.float32)
    restrict = np.zeros((NODES, WIDE), np.float32)
    restrict[:, :KC] = np.tile(rtab.T, (1, CG * VARS))
    lay = np.einsum("aob,fbk->foak", turn, place[:, 0]).reshape(6 * 8 * FACE, NODES)
    tile = np.zeros((80, 256), np.float32)
    for col in range(256):
        kind, v = col // RW % 2, col % STRIDE
        if v < VARS:
            tile[kind * 40 + v * 8 : kind * 40 + v * 8 + 6, col] = 1.0
    code = np.full((8, 256), -100.0, np.float32)
    sign = np.ones((8, 256), np.float32)
    for face in range(6):
        axis = face // 2
        for place_id, source in enumerate(SOURCES[axis]):
            for col in range(2 * RW):
                kind, n, v = col // RW, col // STRIDE % ELEMS, col % STRIDE
                lane = place_id * 2 * RW + col
                code[face, lane] = source * ELEMS + n
                sign[face, lane] = (-1.0 if v == 1 + axis else 1.0) * (-1.0 if kind else 1.0)
    rows = np.zeros((RW, 24), np.float32)
    for e in range(ELEMS):
        for u in range(VARS):
            rows[e * STRIDE + u, u * ELEMS + e] = 1.0
    vtile = np.zeros((24, 3 * RW), np.float32)
    vmask = np.zeros((RW, 3 * RW), np.float32)
    for col in range(3 * RW):
        axis, n, v = col // RW, col // STRIDE % ELEMS, col % STRIDE
        if v < VARS:
            vtile[axis * 8 + v, col] = 1.0
        vmask[n * STRIDE : (n + 1) * STRIDE, col] = 1.0
    consts = np.zeros((184, 256), np.float32)
    for (row, count, lanes), part in zip(CONSTS, (tile, code, sign, vtile, vmask, rows)):
        consts[row : row + count, :lanes] = part
    return dict(
        consts=consts,
        rise=np.concatenate([stacked(de), stacked(restrict)], axis=1),
        lay=np.concatenate(
            [lay.astype(jnp.bfloat16), stacked(np.ascontiguousarray(restrict.T))], axis=0
        ),
    )


def exact_dot(a, b):
    return jnp.dot(a, b, precision=HIGHEST, preferred_element_type=F32)


def halves(values):
    high = values.astype(jnp.bfloat16)
    return high, (values - high.astype(F32)).astype(jnp.bfloat16)


def left_stack(values):
    high = values.astype(jnp.bfloat16).astype(F32)
    return jnp.concatenate([high, values - high, high], axis=1).astype(jnp.bfloat16)


def right_stack(values):
    high, low = halves(values)
    return jnp.concatenate([high, low, high], axis=0)


def dot(a, b):
    return jnp.dot(a, b, preferred_element_type=F32)


def total(values):
    return jnp.sum(values, axis=(0, 1), keepdims=True)


def member_mask(ints_ref):
    row = lax.broadcasted_iota(jnp.int32, (STRIDE, WIDE), 0)
    lane = lax.broadcasted_iota(jnp.int32, (STRIDE, WIDE), 1)
    pieces = []
    for e in range(ELEMS):
        hit = (lane // (VARS * 8) == ints_ref[e, GROUP]) & (lane // 8 % VARS == row)
        pieces.append(jnp.where(hit & (lane < KC), 1.0, 0.0))
    return jnp.concatenate(pieces, axis=0)


def coarse_row(member, rise_ref, vector):
    return jnp.sum(member * dot(left_stack(vector), rise_ref[:, GROWN:]), axis=0, keepdims=True)


def scalar_row(scalars):
    lane = lax.broadcasted_iota(jnp.int32, (1, 128), 1)
    row = jnp.zeros((1, 128), F32)
    for i, value in enumerate(scalars):
        row = jnp.where(lane == i, value, row)
    return row


def read_scalars(table_ref, count):
    sums = jnp.sum(table_ref[...], axis=0, keepdims=True)
    return [jnp.broadcast_to(sums[:, i : i + 1], (1, 128)) for i in range(count)]


def coarse_values(coarse, cinv_ref, member_ref, lay_ref):
    solved = dot(left_stack(coarse[:, :KC]), cinv_ref[...])
    solved = jnp.concatenate([solved, jnp.zeros((1, WIDE - KC), F32)], axis=1)
    return dot(left_stack(member_ref[...] * solved), lay_ref[LAID:, :])


def apply_blocks(turned_ref, parts):
    row = lax.broadcasted_iota(jnp.int32, (RW, ROWS), 0) % STRIDE
    own_lanes = lax.broadcasted_iota(jnp.int32, (RW, ROWS), 1) // NODES == row
    stacked = []
    for part in parts:
        pair = jnp.concatenate([part, part], axis=1)
        stacked.append(jnp.where(own_lanes, jnp.concatenate([pair, pair, part], axis=1), 0.0))
    pieces = []
    for e in range(ELEMS):
        rows = [part[e * STRIDE : (e + 1) * STRIDE] for part in stacked]
        rows = jnp.concatenate(rows, axis=0) if len(rows) > 1 else rows[0]
        out = dot(rows.astype(jnp.bfloat16), turned_ref[e])
        pieces.append(jnp.broadcast_to(jnp.sum(out, axis=0, keepdims=True), (STRIDE, ROWS)))
    full = jnp.where(own_lanes, jnp.concatenate(pieces, axis=0), 0.0)
    half = full[:, :128] + full[:, 128:256]
    return half[:, :NODES] + half[:, NODES:] + full[:, 256:]


def rounded(values):
    return [values.astype(jnp.bfloat16).astype(F32)]


def face_of(grown, face):
    base = 3 * NODES + face * 2 * FACE
    return grown[:, base : base + 2 * FACE]


def pack(grown, face):
    values = face_of(grown, face)
    rows = [values[e * STRIDE : (e + 1) * STRIDE] for e in range(ELEMS)]
    return jnp.concatenate(rows, axis=1)


def copies(tile, slot):
    lane = lax.broadcasted_iota(jnp.int32, tile.shape, 1)
    values = jnp.where(lane // FACE == slot, tile, 0.0)
    for shift in (FACE, 2 * FACE, 4 * FACE):
        values = values + pltpu.roll(values, shift, 1)
    return values


def unpack(tile):
    slot = lax.broadcasted_iota(jnp.int32, tile.shape, 1) // FACE
    level = [tile]
    for bit in (1, 2, 4):
        upper = slot & bit != 0
        without = [jnp.where(upper, pltpu.roll(a, bit * FACE, 1), a) for a in level]
        only = [jnp.where(upper, a, pltpu.roll(a, 128 - bit * FACE, 1)) for a in level]
        level = without + only
    return [level[e * 2 + kind] for kind in range(2) for e in range(ELEMS)]


def write_sends(odd_ref, grown, send_refs):
    p_odd, s_odd, r = (odd_ref[i * STRIDE : (i + 1) * STRIDE, :] > 0.5 for i in range(3))
    faces = [pack(grown, f) for f in range(6)]
    send_refs[0][...] = jnp.where(r, faces[4], faces[5])
    send_refs[1][...] = jnp.where(p_odd, faces[1], faces[0])
    send_refs[2][...] = jnp.where(s_odd, faces[2], faces[3])
    send_refs[3][...] = jnp.where(s_odd, faces[3], faces[2])
    send_refs[4][...] = jnp.where(p_odd, faces[0], faces[1])


def place_terms(groups, omask_ref, lay_ref, first_face):
    laid = []
    for i, terms in enumerate(groups):
        base = (first_face + 2 * i) * RW
        terms = terms * omask_ref[base : base + 2 * RW, :]
        laid += [terms[:RW], terms[RW:]]
    laid = jnp.concatenate(laid, axis=1)
    high, low = halves(laid)
    out = dot(jnp.concatenate([high, low], axis=0), lay_ref[first_face * 8 * FACE : LAID, :])
    return out[:RW] + out[RW:]


def halo_part(recv, rem, omask_ref, lay_ref):
    rad, pass_b, span_a, span_b, pass_a = [unpack(r[...]) for r in recv]
    groups = []
    for pieces, mat in ((pass_a + pass_b, rem[0]), (span_a + span_b, rem[1]), (rad, rem[2])):
        groups.append(dot(mat[...], right_stack(jnp.concatenate(pieces, axis=0))))
    return place_terms(groups, omask_ref, lay_ref, 0)


def start_kernel(rs_ref, table_ref):
    rs = rs_ref[...]
    table_ref[...] = jnp.broadcast_to(scalar_row([total(rs * rs)]), table_ref.shape)


def prepare_kernel(rs_ref, mass_ref, ints_ref, rise_ref, x_ref, massw_ref, member_ref, odd_ref, row_ref):
    x_ref[...] = jnp.zeros_like(x_ref)
    massw_ref[...] = jnp.zeros_like(massw_ref)
    for e in range(ELEMS):
        for v in range(VARS):
            lanes = slice(v * NODES, (v + 1) * NODES)
            row = e * STRIDE + v
            x_ref[row : row + 1, :] = rs_ref[e : e + 1, lanes]
            massw_ref[row : row + 1, :] = mass_ref[e : e + 1, lanes]
    member = member_mask(ints_ref)
    member_ref[...] = member
    row_ref[...] = coarse_row(member, rise_ref, x_ref[...])
    for i in range(3):
        odd = (ints_ref[i, PLACE] % 2).astype(F32)
        odd_ref[i * STRIDE : (i + 1) * STRIDE, :] = jnp.full((STRIDE, 128), odd, F32)


def setup_kernel(
    ints_ref,
    volume_ref,
    flux_ref,
    visc_ref,
    blocks_ref,
    consts_ref,
    cinv_ref,
    rem0_ref,
    rem1_ref,
    rem2_ref,
    loc1_ref,
    loc2_ref,
    omask_ref,
    vmat_ref,
    cinv3_ref,
    turned_ref,
    coef_ref,
    amat_ref,
):
    p_odd, s_odd = ints_ref[0, PLACE] % 2, ints_ref[1, PLACE] % 2
    device = ints_ref[3, PLACE]
    coef_ref[...] = jnp.zeros_like(coef_ref)
    for u in range(VARS):
        here = slice(u * ELEMS, (u + 1) * ELEMS)
        for axis in range(3):
            coef_ref[here, 80 + axis * 8 : 80 + axis * 8 + VARS] = volume_ref[axis, u]
        for v in range(VARS):
            coef_ref[here, v * 8 : v * 8 + 6] = flux_ref[u, v]
            coef_ref[here, 40 + v * 8 : 40 + v * 8 + 6] = visc_ref[u, v]
    tile, codes, wall_signs, vtile, vmask, expand = (
        consts_ref[a : a + n, :lanes] for a, n, lanes in CONSTS
    )
    coef = exact_dot(expand, coef_ref[...])
    vmat_ref[...] = right_factor(exact_dot(coef[:, 80:104], vtile) * vmask)
    turned = cinv_ref[0, 0].T
    high, low = halves(turned)
    cinv3_ref[...] = jnp.concatenate([high, high, low], axis=0)
    for e in range(ELEMS):
        turned_ref[e] = blocks_ref[e].T
    face_lane = lax.broadcasted_iota(jnp.int32, (RW, 80), 1) % 8
    coef = [jnp.where(face_lane == f, coef[:, :80], 0.0) for f in range(6)]
    spread = exact_dot(jnp.concatenate(coef, axis=0), tile)
    lane = lax.broadcasted_iota(jnp.int32, (STRIDE, 8 * FACE), 1)
    for f in range(6):
        colcode = jnp.broadcast_to(codes[f : f + 1], (STRIDE, 256))
        signs = jnp.broadcast_to(wall_signs[f : f + 1], (STRIDE, 256))
        for e in range(ELEMS):
            near = ints_ref[e, NEIGH + f]
            tag = ints_ref[e, TAGS + f]
            spot = near % ELEMS
            crossing = near // ELEMS != device
            if f == 0:
                source = 1 - p_odd
            elif f == 1:
                source = p_odd
            elif f == 2:
                source = 3 - s_odd
            elif f == 3:
                source = 2 + s_odd
            else:
                source = jnp.where(crossing, 4, 8 if f == 4 else 7)
            code = source * ELEMS + spot
            turn_code = ints_ref[e, ORIENT + f]
            if f >= 2:
                wall_code = (5 + f - 2) * ELEMS + e
                code = jnp.where(tag == 0, code, jnp.where(tag == 1, wall_code, -1))
                turn_code = jnp.where(tag == 0, turn_code, 0)
            rows = slice(f * RW + e * STRIDE, f * RW + (e + 1) * STRIDE)
            values = spread[rows]
            values = jnp.where(tag == 1, values * signs, values)
            amat_ref[rows, :] = jnp.where(colcode == code.astype(F32), -values, 0.0)
            omask_ref[rows, :] = jnp.where(lane // FACE == turn_code, 1.0, 0.0)
    one = 2 * RW
    rem0_ref[...] = right_factor(amat_ref[:one, : 2 * one])
    rem1_ref[...] = right_factor(amat_ref[one : 2 * one, : 2 * one])
    loc1_ref[...] = right_factor(amat_ref[one : 2 * one, 2 * one : 4 * one])
    rem2_ref[...] = right_factor(amat_ref[2 * one :, :one])
    loc2_ref[...] = right_factor(amat_ref[2 * one :, one : 3 * one])


def right_factor(values):
    high = values.astype(jnp.bfloat16).astype(F32)
    return jnp.concatenate([high, high, values - high], axis=1).astype(jnp.bfloat16)


def coarse_kernel(r0, r1, r2, r3, cinv, member, lay, coarse_ref):
    coarse = (r0[...] + r1[...]) + (r2[...] + r3[...])
    coarse_ref[...] = coarse_values(coarse, cinv, member, lay)


def finish_first(odd, first, rise, first_ref, grown_ref, sends):
    first_ref[...] = first
    grown = dot(left_stack(first), rise[:, :GROWN])
    grown_ref[...] = grown
    write_sends(odd, grown, sends)


def first0_kernel(odd, table, x, coarse, blocks, rise, *outs):
    z_ref, coarse_ref, scal_ref, first_ref, grown_ref, *sends = outs
    beta = jnp.sqrt(read_scalars(table, 1)[0])
    z = x[...] / beta[:, :NODES]
    z_ref[...] = z
    scal_ref[...] = jnp.broadcast_to(beta, scal_ref.shape)
    scaled = coarse[...] / beta[:, :NODES]
    coarse_ref[...] = scaled
    first = apply_blocks(blocks, rounded(z)) + scaled
    finish_first(odd, first, rise, first_ref, grown_ref, sends)


def next_kernel(step, odd, table, x, coarse, *refs):
    basis, coarses, refs = refs[:step], refs[step : 2 * step], refs[2 * step :]
    blocks, rise, z_ref, coarse_ref, scal_ref, first_ref, grown_ref, *sends = refs
    *coeffs, square = read_scalars(table, step + 1)
    rest = square
    for h in coeffs:
        rest = rest - h * h
    height = jnp.sqrt(jnp.maximum(rest, 1e-7 * square))
    for i, value in enumerate((*coeffs, height)):
        scal_ref[i * STRIDE : (i + 1) * STRIDE, :] = jnp.broadcast_to(value, (STRIDE, 128))
    z, scaled = x[...], coarse[...]
    for h, vector, known in zip(coeffs, basis, coarses):
        z = z - h[:, :NODES] * vector[...]
        scaled = scaled - h[:, :NODES] * known[...]
    z = z / height[:, :NODES]
    scaled = scaled / height[:, :NODES]
    z_ref[...] = z
    coarse_ref[...] = scaled
    first = apply_blocks(blocks, rounded(z)) + scaled
    finish_first(odd, first, rise, first_ref, grown_ref, sends)


def local_kernel(x, grown_ref, mass, vmat, loc1, loc2, omask, lay, out_ref):
    grown = grown_ref[...]
    slopes = jnp.concatenate([grown[:, i * NODES : (i + 1) * NODES] for i in range(3)], axis=0)
    result = 1.5 * mass[...] * x[...] + dot(vmat[...], right_stack(slopes))
    groups = []
    for faces, mat in (((2, 3), loc1), ((4, 5), loc2)):
        pieces = []
        for f in faces:
            base = 3 * NODES + f * 2 * FACE
            tile = grown[:, base // 128 * 128 : base // 128 * 128 + 128]
            slot = base % 128 // FACE
            pieces += [copies(tile, slot), copies(tile, slot + 1)]
        groups.append(dot(mat[...], right_stack(jnp.concatenate(pieces, axis=0))))
    out_ref[...] = result + place_terms(groups, omask, lay, 2)


def second_kernel(*refs):
    odd, z, first, local = refs[:4]
    recv = refs[4:9]
    rem, omask, lay, blocks, rise = refs[9:12], *refs[12:16]
    search_ref, grown_ref, *sends = refs[16:]
    defect = z[...] - (local[...] + halo_part(recv, rem, omask, lay))
    search = first[...] + apply_blocks(blocks, rounded(defect))
    search_ref[...] = search
    grown = dot(left_stack(search), rise[:, :GROWN])
    grown_ref[...] = grown
    write_sends(odd, grown, sends)


def third_kernel(step, *refs):
    local = refs[0]
    recv = refs[1:6]
    rem, omask, lay = refs[6:9], refs[9], refs[10]
    mapped = local[...] + halo_part(recv, rem, omask, lay)
    if step == 2:
        *basis, w_ref, table_ref = refs[11:]
    else:
        member, rise, *basis, w_ref, table_ref, row_ref = refs[11:]
        row_ref[...] = coarse_row(member[...], rise, mapped)
    scalars = [total(mapped * b[...]) for b in basis] + [total(mapped * mapped)]
    w_ref[...] = mapped
    table_ref[...] = jnp.broadcast_to(scalar_row(scalars), table_ref.shape)


def inverse_sqrt(value):
    guess = lax.rsqrt(value)
    return guess * (1.5 - 0.5 * (value * guess) * guess)


def least_squares(matrix, beta):
    iters = len(matrix) - 1
    target = [beta] + [jnp.zeros_like(beta)] * iters
    inverse = []
    for k in range(iters):
        top, low = matrix[k][k], matrix[k + 1][k]
        scale = inverse_sqrt(top * top + low * low)
        inverse.append(scale)
        cosine, sine = top * scale, low * scale
        for later in range(k + 1, iters):
            upper, lower = matrix[k][later], matrix[k + 1][later]
            matrix[k][later] = cosine * upper + sine * lower
            matrix[k + 1][later] = -sine * upper + cosine * lower
        upper, lower = target[k], target[k + 1]
        target[k] = cosine * upper + sine * lower
        target[k + 1] = -sine * upper + cosine * lower
    weights = [None] * iters
    for k in reversed(range(iters)):
        value = target[k]
        for later in range(k + 1, iters):
            value = value - matrix[k][later] * weights[later]
        weights[k] = value * inverse[k]
    return weights


def final_kernel(table, scal0, scal1, scal2, x, s0, s1, s2, w0, w1, w2, update_ref, residual_ref):
    h02, h12, h22, square = read_scalars(table, 4)
    beta = scal0[0:1, :]
    h00, h10 = [scal1[i * STRIDE : i * STRIDE + 1, :] for i in range(2)]
    h01, h11, h21 = [scal2[i * STRIDE : i * STRIDE + 1, :] for i in range(3)]
    h32 = jnp.sqrt(jnp.maximum(square - h02 * h02 - h12 * h12 - h22 * h22, 1e-7 * square))
    zero = jnp.zeros_like(beta)
    hess = [[h00, h01, h02], [h10, h11, h12], [zero, h21, h22], [zero, zero, h32]]
    y0, y1, y2 = (y[:, :NODES] for y in least_squares(hess, beta))
    update = y0 * s0[...] + y1 * s1[...] + y2 * s2[...]
    residual = x[...] - (y0 * w0[...] + y1 * w1[...] + y2 * w2[...])
    for e in range(ELEMS):
        for v in range(VARS):
            lanes = slice(v * NODES, (v + 1) * NODES)
            row = e * STRIDE + v
            update_ref[e : e + 1, lanes] = update[row : row + 1, :]
            residual_ref[e : e + 1, lanes] = residual[row : row + 1, :]


VMEM = pltpu.VMEM
SMEM = pltpu.SMEM


def shape_of(out):
    return out if isinstance(out, jax.ShapeDtypeStruct) else jax.ShapeDtypeStruct(out, F32)


def call(kernel, name, args, outs, smem=(), scratch=(), raw=()):
    return pl.pallas_call(
        kernel,
        name=name,
        out_shape=[shape_of(out) for out in outs],
        in_specs=[
            pl.BlockSpec()
            if i in raw
            else pl.BlockSpec(memory_space=SMEM if i in smem else VMEM)
            for i in range(len(args))
        ],
        out_specs=[pl.BlockSpec(memory_space=VMEM)] * len(outs),
        scratch_shapes=[VMEM(shape, F32) for shape in scratch],
        compiler_params=pltpu.CompilerParams(vmem_limit_bytes=32 * 1024 * 1024),
    )(*args)


def with_step(kernel, step):
    def run(*refs):
        kernel(step, *refs)

    return run


def body(
    right_side,
    mass,
    volume_jac,
    face_flux,
    face_visc,
    block_inverse,
    coarse_inverse,
    neighbours,
    orientation,
    bc_tags,
    coarse_group,
):
    t = {name: jnp.asarray(value) for name, value in tables().items()}
    n_pass, n_span = lax.axis_size("passage"), lax.axis_size("span")
    n_rad = lax.axis_size("radial")
    devices = n_pass * n_span * n_rad
    p, s, r = (lax.axis_index(a) for a in AXES)
    place = jnp.stack([p, s, r, (p * n_span + s) * n_rad + r]).astype(jnp.int32)
    ints = [neighbours, orientation, bc_tags, coarse_group[:, None], place[:, None]]
    ints = jnp.concatenate(ints, axis=1)
    volume_t = jnp.transpose(volume_jac, (1, 2, 0, 3))
    flux_t, visc_t = (jnp.transpose(a, (2, 3, 0, 1)) for a in (face_flux, face_visc))

    pass_a = [(i, i ^ 1) for i in range(n_pass)]
    pass_b = [(i, (i + 1 if i % 2 else i - 1) % n_pass) for i in range(n_pass)]
    span_a = [(i, i ^ 1) for i in range(n_span)]
    span_b = [(i, (i + 1 if i % 2 else i - 1) % n_span) for i in range(n_span)]
    rad = [(0, 1), (1, 0)]

    def exchange(sends):
        ways = (
            ("radial", rad),
            ("passage", pass_b),
            ("span", span_a),
            ("span", span_b),
            ("passage", pass_a),
        )
        return [lax.ppermute(x, axis, way) for x, (axis, way) in zip(sends, ways)]

    def span_rows(row):
        return [row] + [
            lax.ppermute(row, "span", [(i, i ^ k) for i in range(n_span)]) for k in (2, 3, 1)
        ]

    vec = (RW, NODES)
    grow = (RW, GROWN)
    send = (STRIDE, 128)
    table_shape = (devices, 128)

    def half_floats(*shape):
        return jax.ShapeDtypeStruct(shape, jnp.bfloat16)

    (table,) = call(start_kernel, "start", (right_side,), [table_shape], raw=(0,))
    table = lax.all_to_all(table, AXES, 0, 0, tiled=True)
    x, massw, member, odd, row = call(
        prepare_kernel,
        "prepare",
        (right_side, mass, ints, t["rise"]),
        [vec, vec, (RW, WIDE), (3 * STRIDE, 128), (1, WIDE)],
        smem=(2,),
        raw=(0, 1, 3),
    )
    rows = span_rows(row)
    pair = half_floats(2 * RW, 3 * 4 * RW)
    rem0, rem1, rem2, loc1, loc2, omask, vmat, cinv3, turned = call(
        setup_kernel,
        "setup",
        (
            ints,
            volume_t,
            flux_t,
            visc_t,
            block_inverse,
            t["consts"],
            coarse_inverse,
        ),
        [
            pair,
            pair,
            half_floats(2 * RW, 3 * 2 * RW),
            pair,
            pair,
            (6 * RW, 8 * FACE),
            half_floats(RW, 9 * RW),
            half_floats(3 * KC, KC),
            half_floats(*block_inverse.shape),
        ],
        smem=(0,),
        raw=tuple(range(1, 7)),
        scratch=[(24, 104), (6 * RW, 256)],
    )
    remote = (rem0, rem1, rem2, omask, t["lay"])
    near = (massw, vmat, loc1, loc2, omask, t["lay"])

    def local_part(vector, grown, step):
        return call(local_kernel, "local%d" % step, (vector, grown) + near, [vec])[0]

    coarse_tables = (cinv3, member, t["lay"])
    tail = (turned, t["rise"])
    basis, search, images, scalars, coarses = [], [], [], [], []
    outs = [vec, grow] + [send] * 5
    for step in range(3):
        (coarse,) = call(coarse_kernel, "coarse%d" % step, (*rows, *coarse_tables), [vec])
        if step == 0:
            kernel, args = first0_kernel, (odd, table, x, coarse)
        else:
            kernel, args = with_step(next_kernel, step), (odd, table, images[-1], coarse)
        z, scaled, scal, first, grown, *sends = call(
            kernel,
            "first%d" % step,
            (*args, *basis, *coarses, *tail),
            [vec, vec, ((8, 16, 24)[step], 128)] + outs,
        )
        basis.append(z)
        coarses.append(scaled)
        scalars.append(scal)
        recv = exchange(sends)
        local = local_part(first, grown, step)
        direction, grown, *sends = call(
            second_kernel,
            "second%d" % step,
            (odd, z, first, local, *recv) + remote + tail,
            outs,
        )
        search.append(direction)
        recv = exchange(sends)
        local = local_part(direction, grown, step)
        kernel = with_step(third_kernel, step)
        args = (local, *recv) + remote
        if step < 2:
            image, table, row = call(
                kernel,
                "third%d" % step,
                args + (member, t["rise"], *basis),
                [vec, table_shape, (1, WIDE)],
            )
            rows = span_rows(row)
        else:
            image, table = call(kernel, "third2", args + tuple(basis), [vec, table_shape])
        table = lax.all_to_all(table, AXES, 0, 0, tiled=True)
        images.append(image)

    update, residual = call(
        final_kernel,
        "final",
        (table, *scalars, x, *search, *images),
        [right_side.shape] * 2,
    )
    return (update, residual)


def solution(mesh):
    rows = P(AXES, None)
    blocks = P(AXES, None, None)
    jac = P(AXES, None, None, None)
    in_specs = (
        rows,
        rows,
        jac,
        jac,
        jac,
        blocks,
        P("passage", "radial", None, None),
        rows,
        rows,
        rows,
        P(AXES),
    )
    return jax.shard_map(body, mesh=mesh, in_specs=in_specs, out_specs=(rows, rows), check_vma=False)
```

```python
import math

import jax
import jax.numpy as jnp
import numpy as np
from jax import lax
from jax.experimental import pallas as pl
from jax.experimental.pallas import tpu as pltpu
from jax.sharding import PartitionSpec as P

QN = 4
VARS = 5
CG = 4
ELEMS = 4
NODES = QN**3
ROWS = 320
KC = 160
STRIDE = 8
RW = ELEMS * STRIDE
FACE = QN * QN
SOURCES = ((0, 1), (2, 3, 5, 6), (4, 7, 8))
WIDE = 256
AXES = ("passage", "span", "radial")
NEIGH, ORIENT, TAGS, GROUP, PLACE = 0, 6, 12, 18, 19
HIGHEST = lax.Precision.HIGHEST
GROWN = 3 * NODES + 6 * 2 * FACE
LAID = 6 * 8 * FACE
CONSTS = ((0, 80, 256), (80, 8, 256), (88, 8, 256), (96, 24, 96), (120, 32, 96), (152, 32, 24))
F32 = jnp.float32


def lobatto_nodes():
    inner_node = 1.0 / math.sqrt(5.0)
    return np.array([-1.0, -inner_node, inner_node, 1.0])


def derivative_table():
    nodes = lobatto_nodes()
    weights = np.ones(QN)
    for row_id in range(QN):
        for col_id in range(QN):
            if col_id != row_id:
                weights[row_id] = weights[row_id] / (nodes[row_id] - nodes[col_id])
    result = np.zeros((QN, QN))
    for row_id in range(QN):
        for col_id in range(QN):
            if col_id != row_id:
                result[row_id, col_id] = (
                    weights[col_id] / weights[row_id] / (nodes[row_id] - nodes[col_id])
                )
        result[row_id, row_id] = -np.sum(result[row_id])
    return result


def vertex_table():
    nodes = lobatto_nodes()
    shapes = np.stack([(1.0 - nodes) / 2.0, (1.0 + nodes) / 2.0])
    first_part = shapes[:, None, None, :, None, None]
    second_part = shapes[None, :, None, None, :, None]
    third_part = shapes[None, None, :, None, None, :]
    return (first_part * second_part * third_part).reshape(8, NODES)


def coords(node):
    return (node // 16, node // 4 % 4, node % 4)


def others(node, axis):
    picked = [c for i, c in enumerate(coords(node)) if i != axis]
    return picked[0] * QN + picked[1]


def layer_of(face):
    return 0 if face % 2 == 0 else QN - 1


def stacked(values):
    high = values.astype(jnp.bfloat16)
    rest = values - high.astype(np.float32)
    mid = rest.astype(jnp.bfloat16)
    low = (rest - mid.astype(np.float32)).astype(jnp.bfloat16)
    return np.concatenate([high, high, high, mid, mid, low], axis=0)


def short_stacked(values):
    high = values.astype(jnp.bfloat16)
    low = (values - high.astype(np.float32)).astype(jnp.bfloat16)
    return np.concatenate([high, high, low], axis=0)


def tables():
    dmat = derivative_table()
    de = np.zeros((NODES, 3 * NODES + 6 * 2 * FACE), np.float32)
    place = np.zeros((6, 1, FACE, NODES), np.float32)
    for node in range(NODES):
        for axis in range(3):
            for target in range(NODES):
                if others(node, axis) == others(target, axis):
                    de[node, axis * NODES + target] = dmat[
                        coords(target)[axis], coords(node)[axis]
                    ]
        for face in range(6):
            axis = face // 2
            spot = others(node, axis)
            base = 3 * NODES + face * 2 * FACE
            de[node, base + FACE + spot] = dmat[layer_of(face), coords(node)[axis]]
            if coords(node)[axis] == layer_of(face):
                de[node, base + spot] = 1.0
                place[face, :, spot, node] = 1.0
    turn = np.zeros((FACE, 8, FACE), np.float32)
    for code in range(8):
        for i in range(QN):
            for j in range(QN):
                a = QN - 1 - i if code & 2 else i
                b = QN - 1 - j if code & 1 else j
                if code & 4:
                    a, b = b, a
                turn[a * QN + b, code, i * QN + j] = 1.0
    rtab = vertex_table().astype(np.float32)
    restrict = np.zeros((NODES, WIDE), np.float32)
    restrict[:, :KC] = np.tile(rtab.T, (1, CG * VARS))
    lay = np.einsum("aob,fbk->foak", turn, place[:, 0]).reshape(6 * 8 * FACE, NODES)
    tile = np.zeros((80, 256), np.float32)
    for col in range(256):
        kind, v = col // RW % 2, col % STRIDE
        if v < VARS:
            tile[kind * 40 + v * 8 : kind * 40 + v * 8 + 6, col] = 1.0
    code = np.full((8, 256), -100.0, np.float32)
    sign = np.ones((8, 256), np.float32)
    for face in range(6):
        axis = face // 2
        for place_id, source in enumerate(SOURCES[axis]):
            for col in range(2 * RW):
                kind, n, v = col // RW, col // STRIDE % ELEMS, col % STRIDE
                lane = place_id * 2 * RW + col
                code[face, lane] = source * ELEMS + n
                sign[face, lane] = (-1.0 if v == 1 + axis else 1.0) * (-1.0 if kind else 1.0)
    rows = np.zeros((RW, 24), np.float32)
    for e in range(ELEMS):
        for u in range(VARS):
            rows[e * STRIDE + u, u * ELEMS + e] = 1.0
    vtile = np.zeros((24, 3 * RW), np.float32)
    vmask = np.zeros((RW, 3 * RW), np.float32)
    for col in range(3 * RW):
        axis, n, v = col // RW, col // STRIDE % ELEMS, col % STRIDE
        if v < VARS:
            vtile[axis * 8 + v, col] = 1.0
        vmask[n * STRIDE : (n + 1) * STRIDE, col] = 1.0
    consts = np.zeros((184, 256), np.float32)
    for (row, count, lanes), part in zip(CONSTS, (tile, code, sign, vtile, vmask, rows)):
        consts[row : row + count, :lanes] = part
    return dict(
        consts=consts,
        rise=stacked(de),
        restrict=short_stacked(restrict),
        lay=np.concatenate(
            [lay.astype(jnp.bfloat16), short_stacked(np.ascontiguousarray(restrict.T))], axis=0
        ),
    )


def exact_dot(a, b):
    return jnp.dot(a, b, precision=HIGHEST, preferred_element_type=F32)


def thirds(values):
    high = values.astype(jnp.bfloat16).astype(F32)
    rest = values - high
    mid = rest.astype(jnp.bfloat16).astype(F32)
    return high, mid, rest - mid


def left_stack(values):
    high, mid, low = thirds(values)
    return jnp.concatenate([high, mid, low, high, mid, high], axis=1).astype(jnp.bfloat16)


def short_stack(values):
    high = values.astype(jnp.bfloat16).astype(F32)
    return jnp.concatenate([high, values - high, high], axis=1).astype(jnp.bfloat16)


def right_stack(values):
    high, mid, low = (part.astype(jnp.bfloat16) for part in thirds(values))
    return jnp.concatenate([high, mid, low, high, mid, high], axis=0)


def right_factor(values):
    high, mid, low = thirds(values)
    return jnp.concatenate([high, high, high, mid, mid, low], axis=1).astype(jnp.bfloat16)


def dot(a, b):
    return jnp.dot(a, b, preferred_element_type=F32)


def total(values):
    return jnp.sum(values, axis=(0, 1), keepdims=True)


def member_mask(ints_ref):
    row = lax.broadcasted_iota(jnp.int32, (STRIDE, WIDE), 0)
    lane = lax.broadcasted_iota(jnp.int32, (STRIDE, WIDE), 1)
    pieces = []
    for e in range(ELEMS):
        hit = (lane // (VARS * 8) == ints_ref[e, GROUP]) & (lane // 8 % VARS == row)
        pieces.append(jnp.where(hit & (lane < KC), 1.0, 0.0))
    return jnp.concatenate(pieces, axis=0)


def coarse_row(member, restrict_ref, vector):
    return jnp.sum(member * dot(short_stack(vector), restrict_ref[...]), axis=0, keepdims=True)


def scalar_row(scalars):
    lane = lax.broadcasted_iota(jnp.int32, (1, 128), 1)
    row = jnp.zeros((1, 128), F32)
    for i, value in enumerate(scalars):
        row = jnp.where(lane == i, value, row)
    return row


def read_scalars(table_ref, count):
    sums = jnp.sum(table_ref[...], axis=0, keepdims=True)
    return [jnp.broadcast_to(sums[:, i : i + 1], (1, 128)) for i in range(count)]


def coarse_values(coarse, cinv_ref, member_ref, lay_ref):
    solved = dot(short_stack(coarse[:, :KC]), cinv_ref[...])
    solved = jnp.concatenate([solved, jnp.zeros((1, WIDE - KC), F32)], axis=1)
    return dot(short_stack(member_ref[...] * solved), lay_ref[LAID:, :])


def apply_blocks(turned_ref, parts):
    row = lax.broadcasted_iota(jnp.int32, (RW, ROWS), 0) % STRIDE
    own_lanes = lax.broadcasted_iota(jnp.int32, (RW, ROWS), 1) // NODES == row
    stacked = []
    for part in parts:
        pair = jnp.concatenate([part, part], axis=1)
        stacked.append(jnp.where(own_lanes, jnp.concatenate([pair, pair, part], axis=1), 0.0))
    pieces = []
    for e in range(ELEMS):
        rows = [part[e * STRIDE : (e + 1) * STRIDE] for part in stacked]
        rows = jnp.concatenate(rows, axis=0) if len(rows) > 1 else rows[0]
        out = dot(rows.astype(jnp.bfloat16), turned_ref[e])
        pieces.append(jnp.broadcast_to(jnp.sum(out, axis=0, keepdims=True), (STRIDE, ROWS)))
    full = jnp.where(own_lanes, jnp.concatenate(pieces, axis=0), 0.0)
    half = full[:, :128] + full[:, 128:256]
    return half[:, :NODES] + half[:, NODES:] + full[:, 256:]


def rounded(values):
    return [values.astype(jnp.bfloat16).astype(F32)]


def two_parts(values):
    high = values.astype(jnp.bfloat16).astype(F32)
    return [high, values - high]


def face_of(grown, face):
    base = 3 * NODES + face * 2 * FACE
    return grown[:, base : base + 2 * FACE]


def pack(grown, face):
    values = face_of(grown, face)
    rows = [values[e * STRIDE : (e + 1) * STRIDE] for e in range(ELEMS)]
    return jnp.concatenate(rows, axis=1)


def copies(tile, slot):
    lane = lax.broadcasted_iota(jnp.int32, tile.shape, 1)
    values = jnp.where(lane // FACE == slot, tile, 0.0)
    for shift in (FACE, 2 * FACE, 4 * FACE):
        values = values + pltpu.roll(values, shift, 1)
    return values


def unpack(tile):
    slot = lax.broadcasted_iota(jnp.int32, tile.shape, 1) // FACE
    level = [tile]
    for bit in (1, 2, 4):
        upper = slot & bit != 0
        without = [jnp.where(upper, pltpu.roll(a, bit * FACE, 1), a) for a in level]
        only = [jnp.where(upper, a, pltpu.roll(a, 128 - bit * FACE, 1)) for a in level]
        level = without + only
    return [level[e * 2 + kind] for kind in range(2) for e in range(ELEMS)]


def write_sends(odd_ref, grown, send_refs):
    p_odd, s_odd, r = (odd_ref[i * STRIDE : (i + 1) * STRIDE, :] > 0.5 for i in range(3))
    faces = [pack(grown, f) for f in range(6)]
    send_refs[0][...] = jnp.where(r, faces[4], faces[5])
    send_refs[1][...] = jnp.where(p_odd, faces[1], faces[0])
    send_refs[2][...] = jnp.where(s_odd, faces[2], faces[3])
    send_refs[3][...] = jnp.where(s_odd, faces[3], faces[2])
    send_refs[4][...] = jnp.where(p_odd, faces[0], faces[1])


def place_terms(groups, omask_ref, lay_ref, first_face):
    laid = []
    for i, terms in enumerate(groups):
        base = (first_face + 2 * i) * RW
        terms = terms * omask_ref[base : base + 2 * RW, :]
        laid += [terms[:RW], terms[RW:]]
    laid = jnp.concatenate(laid, axis=1)
    out = dot(jnp.concatenate(thirds(laid), axis=0).astype(jnp.bfloat16), lay_ref[first_face * 8 * FACE : LAID, :])
    return out[:RW] + (out[RW : 2 * RW] + out[2 * RW :])


def halo_part(recv, rem, omask_ref, lay_ref):
    rad, pass_b, span_a, span_b, pass_a = [unpack(r[...]) for r in recv]
    groups = []
    for pieces, mat in ((pass_a + pass_b, rem[0]), (span_a + span_b, rem[1]), (rad, rem[2])):
        groups.append(dot(mat[...], right_stack(jnp.concatenate(pieces, axis=0))))
    return place_terms(groups, omask_ref, lay_ref, 0)


def start_kernel(rs_ref, table_ref):
    rs = rs_ref[...]
    table_ref[...] = jnp.broadcast_to(scalar_row([total(rs * rs)]), table_ref.shape)


def prepare_kernel(rs_ref, mass_ref, ints_ref, restrict_ref, x_ref, massw_ref, member_ref, odd_ref, row_ref):
    x_ref[...] = jnp.zeros_like(x_ref)
    massw_ref[...] = jnp.zeros_like(massw_ref)
    for e in range(ELEMS):
        for v in range(VARS):
            lanes = slice(v * NODES, (v + 1) * NODES)
            row = e * STRIDE + v
            x_ref[row : row + 1, :] = rs_ref[e : e + 1, lanes]
            massw_ref[row : row + 1, :] = mass_ref[e : e + 1, lanes]
    member = member_mask(ints_ref)
    member_ref[...] = member
    row_ref[...] = coarse_row(member, restrict_ref, x_ref[...])
    for i in range(3):
        odd = (ints_ref[i, PLACE] % 2).astype(F32)
        odd_ref[i * STRIDE : (i + 1) * STRIDE, :] = jnp.full((STRIDE, 128), odd, F32)


def setup_kernel(
    ints_ref,
    volume_ref,
    flux_ref,
    visc_ref,
    blocks_ref,
    consts_ref,
    cinv_ref,
    rem0_ref,
    rem1_ref,
    rem2_ref,
    loc1_ref,
    loc2_ref,
    omask_ref,
    vmat_ref,
    cinv3_ref,
    turned_ref,
    coef_ref,
    amat_ref,
):
    p_odd, s_odd = ints_ref[0, PLACE] % 2, ints_ref[1, PLACE] % 2
    device = ints_ref[3, PLACE]
    coef_ref[...] = jnp.zeros_like(coef_ref)
    for u in range(VARS):
        here = slice(u * ELEMS, (u + 1) * ELEMS)
        for axis in range(3):
            coef_ref[here, 80 + axis * 8 : 80 + axis * 8 + VARS] = volume_ref[axis, u]
        for v in range(VARS):
            coef_ref[here, v * 8 : v * 8 + 6] = flux_ref[u, v]
            coef_ref[here, 40 + v * 8 : 40 + v * 8 + 6] = visc_ref[u, v]
    tile, codes, wall_signs, vtile, vmask, expand = (
        consts_ref[a : a + n, :lanes] for a, n, lanes in CONSTS
    )
    coef = exact_dot(expand, coef_ref[...])
    vmat_ref[...] = right_factor(exact_dot(coef[:, 80:104], vtile) * vmask)
    turned = cinv_ref[0, 0].T
    high = turned.astype(jnp.bfloat16)
    low = (turned - high.astype(F32)).astype(jnp.bfloat16)
    cinv3_ref[...] = jnp.concatenate([high, high, low], axis=0)
    for e in range(ELEMS):
        turned_ref[e] = blocks_ref[e].T
    face_lane = lax.broadcasted_iota(jnp.int32, (RW, 80), 1) % 8
    coef = [jnp.where(face_lane == f, coef[:, :80], 0.0) for f in range(6)]
    spread = exact_dot(jnp.concatenate(coef, axis=0), tile)
    lane = lax.broadcasted_iota(jnp.int32, (STRIDE, 8 * FACE), 1)
    for f in range(6):
        colcode = jnp.broadcast_to(codes[f : f + 1], (STRIDE, 256))
        signs = jnp.broadcast_to(wall_signs[f : f + 1], (STRIDE, 256))
        for e in range(ELEMS):
            near = ints_ref[e, NEIGH + f]
            tag = ints_ref[e, TAGS + f]
            spot = near % ELEMS
            crossing = near // ELEMS != device
            if f == 0:
                source = 1 - p_odd
            elif f == 1:
                source = p_odd
            elif f == 2:
                source = 3 - s_odd
            elif f == 3:
                source = 2 + s_odd
            else:
                source = jnp.where(crossing, 4, 8 if f == 4 else 7)
            code = source * ELEMS + spot
            turn_code = ints_ref[e, ORIENT + f]
            if f >= 2:
                wall_code = (5 + f - 2) * ELEMS + e
                code = jnp.where(tag == 0, code, jnp.where(tag == 1, wall_code, -1))
                turn_code = jnp.where(tag == 0, turn_code, 0)
            rows = slice(f * RW + e * STRIDE, f * RW + (e + 1) * STRIDE)
            values = spread[rows]
            values = jnp.where(tag == 1, values * signs, values)
            amat_ref[rows, :] = jnp.where(colcode == code.astype(F32), -values, 0.0)
            omask_ref[rows, :] = jnp.where(lane // FACE == turn_code, 1.0, 0.0)
    one = 2 * RW
    rem0_ref[...] = right_factor(amat_ref[:one, : 2 * one])
    rem1_ref[...] = right_factor(amat_ref[one : 2 * one, : 2 * one])
    loc1_ref[...] = right_factor(amat_ref[one : 2 * one, 2 * one : 4 * one])
    rem2_ref[...] = right_factor(amat_ref[2 * one :, :one])
    loc2_ref[...] = right_factor(amat_ref[2 * one :, one : 3 * one])


def coarse_kernel(r0, r1, r2, r3, cinv, member, lay, coarse_ref):
    coarse = (r0[...] + r1[...]) + (r2[...] + r3[...])
    coarse_ref[...] = coarse_values(coarse, cinv, member, lay)


def blocks_kernel(x, blocks, out_ref):
    out_ref[...] = apply_blocks(blocks, two_parts(x[...]))


def finish_first(odd, first, rise, first_ref, grown_ref, sends):
    first_ref[...] = first
    grown = dot(left_stack(first), rise[...])
    grown_ref[...] = grown
    write_sends(odd, grown, sends)


def first0_kernel(odd, table, x, coarse, blocks, rise, *outs):
    z_ref, coarse_ref, scal_ref, first_ref, grown_ref, *sends = outs
    beta = jnp.sqrt(read_scalars(table, 1)[0])
    z = x[...] / beta[:, :NODES]
    z_ref[...] = z
    scal_ref[...] = jnp.broadcast_to(beta, scal_ref.shape)
    scaled = coarse[...] / beta[:, :NODES]
    coarse_ref[...] = scaled
    first = apply_blocks(blocks, rounded(z)) + scaled
    finish_first(odd, first, rise, first_ref, grown_ref, sends)


def first1_kernel(odd, table, x, coarse, b0, coarse0, blocks, rise, *outs):
    z_ref, scal_ref, first_ref, grown_ref, *sends = outs
    h00, square = read_scalars(table, 2)
    h10 = jnp.sqrt(jnp.maximum(square - h00 * h00, 1e-7 * square))
    for i, value in enumerate((h00, h10, square)):
        scal_ref[i * STRIDE : (i + 1) * STRIDE, :] = jnp.broadcast_to(value, (STRIDE, 128))
    h00, h10 = h00[:, :NODES], h10[:, :NODES]
    z = (x[...] - h00 * b0[...]) / h10
    z_ref[...] = z
    scaled = (coarse[...] - h00 * coarse0[...]) / h10
    first = apply_blocks(blocks, rounded(z)) + scaled
    finish_first(odd, first, rise, first_ref, grown_ref, sends)


def first2_kernel(odd, r0, r1, r2, r3, fine, cinv, member, lay, rise, *outs):
    first_ref, grown_ref, *sends = outs
    coarse = (r0[...] + r1[...]) + (r2[...] + r3[...])
    first = fine[...] + coarse_values(coarse, cinv, member, lay)
    finish_first(odd, first, rise, first_ref, grown_ref, sends)


def local_kernel(x, grown_ref, mass, vmat, loc1, loc2, omask, lay, out_ref):
    grown = grown_ref[...]
    slopes = jnp.concatenate([grown[:, i * NODES : (i + 1) * NODES] for i in range(3)], axis=0)
    result = 1.5 * mass[...] * x[...] + dot(vmat[...], right_stack(slopes))
    groups = []
    for faces, mat in (((2, 3), loc1), ((4, 5), loc2)):
        pieces = []
        for f in faces:
            base = 3 * NODES + f * 2 * FACE
            tile = grown[:, base // 128 * 128 : base // 128 * 128 + 128]
            slot = base % 128 // FACE
            pieces += [copies(tile, slot), copies(tile, slot + 1)]
        groups.append(dot(mat[...], right_stack(jnp.concatenate(pieces, axis=0))))
    out_ref[...] = result + place_terms(groups, omask, lay, 2)


def second_kernel(step, *refs):
    odd, z, first, local = refs[:4]
    recv = refs[4:9]
    rem, omask, lay, blocks, rise = refs[9:12], *refs[12:16]
    search_ref, grown_ref, *sends = refs[16:]
    defect = z[...] - (local[...] + halo_part(recv, rem, omask, lay))
    parts = two_parts(defect) if step == 2 else rounded(defect)
    search = first[...] + apply_blocks(blocks, parts)
    search_ref[...] = search
    grown = dot(left_stack(search), rise[...])
    grown_ref[...] = grown
    write_sends(odd, grown, sends)


def third_kernel(step, *refs):
    local = refs[0]
    recv = refs[1:6]
    rem, omask, lay = refs[6:9], refs[9], refs[10]
    mapped = local[...] + halo_part(recv, rem, omask, lay)
    if step == 0:
        member, restrict, b0, w_ref, table_ref, row_ref = refs[11:]
        scalars = [total(mapped * b0[...]), total(mapped * mapped)]
    elif step == 1:
        member, restrict, w_ref, row_ref = refs[11:]
    else:
        b0, b1, w1, w_ref, table_ref = refs[11:]
        scalars = [total(w1[...] * b[...]) for b in (b0, b1, w1)]
        scalars += [total(mapped * b[...]) for b in (b0, b1, w1)]
        scalars += [total(mapped * mapped)]
    w_ref[...] = mapped
    if step != 1:
        table_ref[...] = jnp.broadcast_to(scalar_row(scalars), table_ref.shape)
    if step != 2:
        row_ref[...] = coarse_row(member[...], restrict, mapped)


def inverse_sqrt(value):
    guess = lax.rsqrt(value)
    return guess * (1.5 - 0.5 * (value * guess) * guess)


def least_squares(matrix, beta):
    iters = len(matrix) - 1
    target = [beta] + [jnp.zeros_like(beta)] * iters
    inverse = []
    for k in range(iters):
        top, low = matrix[k][k], matrix[k + 1][k]
        scale = inverse_sqrt(top * top + low * low)
        inverse.append(scale)
        cosine, sine = top * scale, low * scale
        for later in range(k + 1, iters):
            upper, lower = matrix[k][later], matrix[k + 1][later]
            matrix[k][later] = cosine * upper + sine * lower
            matrix[k + 1][later] = -sine * upper + cosine * lower
        upper, lower = target[k], target[k + 1]
        target[k] = cosine * upper + sine * lower
        target[k + 1] = -sine * upper + cosine * lower
    weights = [None] * iters
    for k in reversed(range(iters)):
        value = target[k]
        for later in range(k + 1, iters):
            value = value - matrix[k][later] * weights[later]
        weights[k] = value * inverse[k]
    return weights


def final_kernel(table, scal0, scal1, x, s0, s1, s2, w0, w1, w2, update_ref, residual_ref):
    g0, g1, g2, q0, q1, qw, qq = read_scalars(table, 7)
    beta = scal0[0:1, :]
    h00, h10, square0 = [scal1[i * STRIDE : i * STRIDE + 1, :] for i in range(3)]
    h01, h11 = g0, g1
    squared = jnp.maximum(g2 - h01 * h01 - h11 * h11, 1e-7 * g2)
    inv21 = inverse_sqrt(squared)
    h21 = squared * inv21
    cross = h00 * h01 + h10 * h11
    h02 = (q0 - h01 * h00 - h11 * h01) * inv21
    h12 = (q1 - h01 * h10 - h11 * h11) * inv21
    with_w1 = (qw - h01 * cross - h11 * g2) * inv21
    h22 = (with_w1 - h01 * h02 - h11 * h12) * inv21
    with_w0 = h00 * q0 + h10 * q1
    square = qq + h01 * h01 * square0 + h11 * h11 * g2
    square = square - 2.0 * (h01 * with_w0 + h11 * qw - h01 * h11 * cross)
    square = square * inv21 * inv21
    h32 = jnp.sqrt(jnp.maximum(square - h02 * h02 - h12 * h12 - h22 * h22, 1e-7 * square))
    zero = jnp.zeros_like(beta)
    hess = [[h00, h01, h02], [h10, h11, h12], [zero, h21, h22], [zero, zero, h32]]
    y0, y1, y2 = least_squares(hess, beta)
    y2 = y2 * inv21
    y0 = y0 - y2 * h01
    y1 = y1 - y2 * h11
    y0, y1, y2 = (y[:, :NODES] for y in (y0, y1, y2))
    update = y0 * s0[...] + y1 * s1[...] + y2 * s2[...]
    residual = x[...] - (y0 * w0[...] + y1 * w1[...] + y2 * w2[...])
    for e in range(ELEMS):
        for v in range(VARS):
            lanes = slice(v * NODES, (v + 1) * NODES)
            row = e * STRIDE + v
            update_ref[e : e + 1, lanes] = update[row : row + 1, :]
            residual_ref[e : e + 1, lanes] = residual[row : row + 1, :]


VMEM = pltpu.VMEM
SMEM = pltpu.SMEM


def shape_of(out):
    return out if isinstance(out, jax.ShapeDtypeStruct) else jax.ShapeDtypeStruct(out, F32)


def call(kernel, name, args, outs, smem=(), scratch=(), raw=()):
    return pl.pallas_call(
        kernel,
        name=name,
        out_shape=[shape_of(out) for out in outs],
        in_specs=[
            pl.BlockSpec()
            if i in raw
            else pl.BlockSpec(memory_space=SMEM if i in smem else VMEM)
            for i in range(len(args))
        ],
        out_specs=[pl.BlockSpec(memory_space=VMEM)] * len(outs),
        scratch_shapes=[VMEM(shape, F32) for shape in scratch],
        compiler_params=pltpu.CompilerParams(vmem_limit_bytes=32 * 1024 * 1024),
    )(*args)


def with_step(kernel, step):
    def run(*refs):
        kernel(step, *refs)

    return run


def body(
    right_side,
    mass,
    volume_jac,
    face_flux,
    face_visc,
    block_inverse,
    coarse_inverse,
    neighbours,
    orientation,
    bc_tags,
    coarse_group,
):
    t = {name: jnp.asarray(value) for name, value in tables().items()}
    n_pass, n_span = lax.axis_size("passage"), lax.axis_size("span")
    n_rad = lax.axis_size("radial")
    devices = n_pass * n_span * n_rad
    p, s, r = (lax.axis_index(a) for a in AXES)
    place = jnp.stack([p, s, r, (p * n_span + s) * n_rad + r]).astype(jnp.int32)
    ints = [neighbours, orientation, bc_tags, coarse_group[:, None], place[:, None]]
    ints = jnp.concatenate(ints, axis=1)
    volume_t = jnp.transpose(volume_jac, (1, 2, 0, 3))
    flux_t, visc_t = (jnp.transpose(a, (2, 3, 0, 1)) for a in (face_flux, face_visc))

    pass_a = [(i, i ^ 1) for i in range(n_pass)]
    pass_b = [(i, (i + 1 if i % 2 else i - 1) % n_pass) for i in range(n_pass)]
    span_a = [(i, i ^ 1) for i in range(n_span)]
    span_b = [(i, (i + 1 if i % 2 else i - 1) % n_span) for i in range(n_span)]
    rad = [(0, 1), (1, 0)]

    def exchange(sends):
        ways = (
            ("radial", rad),
            ("passage", pass_b),
            ("span", span_a),
            ("span", span_b),
            ("passage", pass_a),
        )
        return [lax.ppermute(x, axis, way) for x, (axis, way) in zip(sends, ways)]

    def span_rows(row):
        return [row] + [
            lax.ppermute(row, "span", [(i, i ^ k) for i in range(n_span)]) for k in (2, 3, 1)
        ]

    vec = (RW, NODES)
    grow = (RW, GROWN)
    send = (STRIDE, 128)
    table_shape = (devices, 128)

    def half_floats(*shape):
        return jax.ShapeDtypeStruct(shape, jnp.bfloat16)

    (table,) = call(start_kernel, "start", (right_side,), [table_shape], raw=(0,))
    table = lax.all_to_all(table, AXES, 0, 0, tiled=True)
    x, massw, member, odd, row = call(
        prepare_kernel,
        "prepare",
        (right_side, mass, ints, t["restrict"]),
        [vec, vec, (RW, WIDE), (3 * STRIDE, 128), (1, WIDE)],
        smem=(2,),
        raw=(0, 1, 3),
    )
    rows = span_rows(row)
    pair = half_floats(2 * RW, 6 * 4 * RW)
    rem0, rem1, rem2, loc1, loc2, omask, vmat, cinv3, turned = call(
        setup_kernel,
        "setup",
        (
            ints,
            volume_t,
            flux_t,
            visc_t,
            block_inverse,
            t["consts"],
            coarse_inverse,
        ),
        [
            pair,
            pair,
            half_floats(2 * RW, 6 * 2 * RW),
            pair,
            pair,
            (6 * RW, 8 * FACE),
            half_floats(RW, 18 * RW),
            half_floats(3 * KC, KC),
            half_floats(*block_inverse.shape),
        ],
        smem=(0,),
        raw=tuple(range(1, 7)),
        scratch=[(24, 104), (6 * RW, 256)],
    )
    remote = (rem0, rem1, rem2, omask, t["lay"])
    near = (massw, vmat, loc1, loc2, omask, t["lay"])

    def local_part(vector, grown, step):
        return call(local_kernel, "local%d" % step, (vector, grown) + near, [vec])[0]

    coarse_tables = (cinv3, member, t["lay"])
    tail = (turned, t["rise"])
    basis, search, images, scalars = [], [], [], []
    coarse0 = None
    outs = [vec, grow] + [send] * 5
    for step in range(3):
        if step < 2:
            (coarse,) = call(coarse_kernel, "coarse%d" % step, (*rows, *coarse_tables), [vec])
        if step == 0:
            z, coarse0, scal, first, grown, *sends = call(
                first0_kernel,
                "first0",
                (odd, table, x, coarse) + tail,
                [vec, vec, (8, 128)] + outs,
            )
            scalars.append(scal)
        elif step == 1:
            z, scal, first, grown, *sends = call(
                first1_kernel,
                "first1",
                (odd, table, images[0], coarse, basis[0], coarse0) + tail,
                [vec, (3 * STRIDE, 128)] + outs,
            )
            scalars.append(scal)
        else:
            z = images[1]
            (fine,) = call(blocks_kernel, "fine", (z, turned), [vec])
            first, grown, *sends = call(
                first2_kernel,
                "first2",
                (odd, *rows, fine, *coarse_tables, t["rise"]),
                outs,
            )
        basis.append(z)
        recv = exchange(sends)
        local = local_part(first, grown, step)
        direction, grown, *sends = call(
            with_step(second_kernel, step),
            "second%d" % step,
            (odd, z, first, local, *recv) + remote + tail,
            outs,
        )
        search.append(direction)
        recv = exchange(sends)
        local = local_part(direction, grown, step)
        kernel = with_step(third_kernel, step)
        args = (local, *recv) + remote
        if step == 0:
            image, table, row = call(
                kernel,
                "third0",
                args + (member, t["restrict"], basis[0]),
                [vec, table_shape, (1, WIDE)],
            )
            table = lax.all_to_all(table, AXES, 0, 0, tiled=True)
            rows = span_rows(row)
        elif step == 1:
            image, row = call(kernel, "third1", args + (member, t["restrict"]), [vec, (1, WIDE)])
            rows = span_rows(row)
        else:
            image, table = call(kernel, "third2", args + tuple(basis), [vec, table_shape])
            table = lax.all_to_all(table, AXES, 0, 0, tiled=True)
        images.append(image)

    update, residual = call(
        final_kernel,
        "final",
        (table, *scalars, x, *search, *images),
        [right_side.shape] * 2,
    )
    return (update, residual)


def solution(mesh):
    rows = P(AXES, None)
    blocks = P(AXES, None, None)
    jac = P(AXES, None, None, None)
    in_specs = (
        rows,
        rows,
        jac,
        jac,
        jac,
        blocks,
        P("passage", "radial", None, None),
        rows,
        rows,
        rows,
        P(AXES),
    )
    return jax.shard_map(body, mesh=mesh, in_specs=in_specs, out_specs=(rows, rows), check_vma=False)
```

```python
import math

import jax
import jax.numpy as jnp
import numpy as np
from jax import lax
from jax.experimental import pallas as pl
from jax.experimental.pallas import tpu as pltpu
from jax.sharding import PartitionSpec as P

QN = 4
VARS = 5
CG = 4
ELEMS = 4
NODES = QN**3
ROWS = 320
KC = 160
STRIDE = 8
RW = ELEMS * STRIDE
FACE = QN * QN
SOURCES = ((0, 1), (2, 3, 5, 6), (4, 7, 8))
WIDE = 256
AXES = ("passage", "span", "radial")
NEIGH, ORIENT, TAGS, GROUP, PLACE = 0, 6, 12, 18, 19
HIGHEST = lax.Precision.HIGHEST
GROWN = 6 * 2 * FACE
LAID = 6 * 8 * FACE
CONSTS = ((0, 80, 256), (80, 8, 256), (88, 8, 256), (96, 24, 96), (120, 32, 96), (152, 32, 24))
F32 = jnp.float32


def lobatto_nodes():
    inner_node = 1.0 / math.sqrt(5.0)
    return np.array([-1.0, -inner_node, inner_node, 1.0])


def derivative_table():
    nodes = lobatto_nodes()
    weights = np.ones(QN)
    for row_id in range(QN):
        for col_id in range(QN):
            if col_id != row_id:
                weights[row_id] = weights[row_id] / (nodes[row_id] - nodes[col_id])
    result = np.zeros((QN, QN))
    for row_id in range(QN):
        for col_id in range(QN):
            if col_id != row_id:
                result[row_id, col_id] = (
                    weights[col_id] / weights[row_id] / (nodes[row_id] - nodes[col_id])
                )
        result[row_id, row_id] = -np.sum(result[row_id])
    return result


def vertex_table():
    nodes = lobatto_nodes()
    shapes = np.stack([(1.0 - nodes) / 2.0, (1.0 + nodes) / 2.0])
    first_part = shapes[:, None, None, :, None, None]
    second_part = shapes[None, :, None, None, :, None]
    third_part = shapes[None, None, :, None, None, :]
    return (first_part * second_part * third_part).reshape(8, NODES)


def coords(node):
    return (node // 16, node // 4 % 4, node % 4)


def others(node, axis):
    picked = [c for i, c in enumerate(coords(node)) if i != axis]
    return picked[0] * QN + picked[1]


def layer_of(face):
    return 0 if face % 2 == 0 else QN - 1


def stacked(values):
    high = values.astype(jnp.bfloat16)
    rest = values - high.astype(np.float32)
    mid = rest.astype(jnp.bfloat16)
    low = (rest - mid.astype(np.float32)).astype(jnp.bfloat16)
    return np.concatenate([high, high, high, mid, mid, low], axis=0)


def short_stacked(values):
    high = values.astype(jnp.bfloat16)
    low = (values - high.astype(np.float32)).astype(jnp.bfloat16)
    return np.concatenate([high, high, low], axis=0)


def tables():
    dmat = derivative_table()
    de = np.zeros((NODES, 3 * NODES + 6 * 2 * FACE), np.float32)
    place = np.zeros((6, 1, FACE, NODES), np.float32)
    for node in range(NODES):
        for axis in range(3):
            for target in range(NODES):
                if others(node, axis) == others(target, axis):
                    de[node, axis * NODES + target] = dmat[
                        coords(target)[axis], coords(node)[axis]
                    ]
        for face in range(6):
            axis = face // 2
            spot = others(node, axis)
            base = 3 * NODES + (face - 2) % 6 * 2 * FACE
            de[node, base + FACE + spot] = dmat[layer_of(face), coords(node)[axis]]
            if coords(node)[axis] == layer_of(face):
                de[node, base + spot] = 1.0
                place[face, :, spot, node] = 1.0
    turn = np.zeros((FACE, 8, FACE), np.float32)
    for code in range(8):
        for i in range(QN):
            for j in range(QN):
                a = QN - 1 - i if code & 2 else i
                b = QN - 1 - j if code & 1 else j
                if code & 4:
                    a, b = b, a
                turn[a * QN + b, code, i * QN + j] = 1.0
    rtab = vertex_table().astype(np.float32)
    restrict = np.zeros((NODES, WIDE), np.float32)
    restrict[:, :KC] = np.tile(rtab.T, (1, CG * VARS))
    lay = np.einsum("aob,fbk->foak", turn, place[:, 0]).reshape(6 * 8 * FACE, NODES)
    tile = np.zeros((80, 256), np.float32)
    for col in range(256):
        kind, v = col // RW % 2, col % STRIDE
        if v < VARS:
            tile[kind * 40 + v * 8 : kind * 40 + v * 8 + 6, col] = 1.0
    code = np.full((8, 256), -100.0, np.float32)
    sign = np.ones((8, 256), np.float32)
    for face in range(6):
        axis = face // 2
        for place_id, source in enumerate(SOURCES[axis]):
            for col in range(2 * RW):
                kind, n, v = col // RW, col // STRIDE % ELEMS, col % STRIDE
                lane = place_id * 2 * RW + col
                code[face, lane] = source * ELEMS + n
                sign[face, lane] = (-1.0 if v == 1 + axis else 1.0) * (-1.0 if kind else 1.0)
    rows = np.zeros((RW, 24), np.float32)
    for e in range(ELEMS):
        for u in range(VARS):
            rows[e * STRIDE + u, u * ELEMS + e] = 1.0
    vtile = np.zeros((24, 3 * RW), np.float32)
    vmask = np.zeros((RW, 3 * RW), np.float32)
    for col in range(3 * RW):
        axis, n, v = col // RW, col // STRIDE % ELEMS, col % STRIDE
        if v < VARS:
            vtile[axis * 8 + v, col] = 1.0
        vmask[n * STRIDE : (n + 1) * STRIDE, col] = 1.0
    consts = np.zeros((184, 256), np.float32)
    for (row, count, lanes), part in zip(CONSTS, (tile, code, sign, vtile, vmask, rows)):
        consts[row : row + count, :lanes] = part
    return dict(
        consts=consts,
        rise=stacked(de[:, 3 * NODES :]),
        slope=stacked(de[:, : 3 * NODES]),
        restrict=short_stacked(restrict),
        lay=np.concatenate(
            [lay.astype(jnp.bfloat16), short_stacked(np.ascontiguousarray(restrict.T))], axis=0
        ),
    )


def exact_dot(a, b):
    return jnp.dot(a, b, precision=HIGHEST, preferred_element_type=F32)


def thirds(values):
    high = values.astype(jnp.bfloat16).astype(F32)
    rest = values - high
    mid = rest.astype(jnp.bfloat16).astype(F32)
    return high, mid, rest - mid


def left_stack(values):
    high, mid, low = thirds(values)
    return jnp.concatenate([high, mid, low, high, mid, high], axis=1).astype(jnp.bfloat16)


def short_stack(values):
    high = values.astype(jnp.bfloat16).astype(F32)
    return jnp.concatenate([high, values - high, high], axis=1).astype(jnp.bfloat16)


def right_stack(values):
    high, mid, low = (part.astype(jnp.bfloat16) for part in thirds(values))
    return jnp.concatenate([high, mid, low, high, mid, high], axis=0)


def right_factor(values):
    high, mid, low = thirds(values)
    return jnp.concatenate([high, high, high, mid, mid, low], axis=1).astype(jnp.bfloat16)


def dot(a, b):
    return jnp.dot(a, b, preferred_element_type=F32)


def total(values):
    return jnp.sum(values, axis=(0, 1), keepdims=True)


def member_mask(ints_ref):
    row = lax.broadcasted_iota(jnp.int32, (STRIDE, WIDE), 0)
    lane = lax.broadcasted_iota(jnp.int32, (STRIDE, WIDE), 1)
    pieces = []
    for e in range(ELEMS):
        hit = (lane // (VARS * 8) == ints_ref[e, GROUP]) & (lane // 8 % VARS == row)
        pieces.append(jnp.where(hit & (lane < KC), 1.0, 0.0))
    return jnp.concatenate(pieces, axis=0)


def coarse_row(member, restrict_ref, vector):
    return jnp.sum(member * dot(short_stack(vector), restrict_ref[...]), axis=0, keepdims=True)


def scalar_row(scalars):
    lane = lax.broadcasted_iota(jnp.int32, (1, 128), 1)
    row = jnp.zeros((1, 128), F32)
    for i, value in enumerate(scalars):
        row = jnp.where(lane == i, value, row)
    return row


def read_scalars(table_ref, count):
    sums = jnp.sum(table_ref[...], axis=0, keepdims=True)
    return [jnp.broadcast_to(sums[:, i : i + 1], (1, 128)) for i in range(count)]


def coarse_values(coarse, cinv_ref, member_ref, lay_ref):
    solved = dot(short_stack(coarse[:, :KC]), cinv_ref[...])
    solved = jnp.concatenate([solved, jnp.zeros((1, WIDE - KC), F32)], axis=1)
    return dot(short_stack(member_ref[...] * solved), lay_ref[LAID:, :])


def apply_blocks(turned_ref, parts):
    row = lax.broadcasted_iota(jnp.int32, (RW, ROWS), 0) % STRIDE
    own_lanes = lax.broadcasted_iota(jnp.int32, (RW, ROWS), 1) // NODES == row
    stacked = []
    for part in parts:
        pair = jnp.concatenate([part, part], axis=1)
        stacked.append(jnp.where(own_lanes, jnp.concatenate([pair, pair, part], axis=1), 0.0))
    pieces = []
    for e in range(ELEMS):
        rows = [part[e * STRIDE : (e + 1) * STRIDE] for part in stacked]
        rows = jnp.concatenate(rows, axis=0) if len(rows) > 1 else rows[0]
        out = dot(rows.astype(jnp.bfloat16), turned_ref[e])
        pieces.append(jnp.broadcast_to(jnp.sum(out, axis=0, keepdims=True), (STRIDE, ROWS)))
    full = jnp.where(own_lanes, jnp.concatenate(pieces, axis=0), 0.0)
    half = full[:, :128] + full[:, 128:256]
    return half[:, :NODES] + half[:, NODES:] + full[:, 256:]


def rounded(values):
    return [values.astype(jnp.bfloat16).astype(F32)]


def two_parts(values):
    high = values.astype(jnp.bfloat16).astype(F32)
    return [high, values - high]


def face_of(grown, face):
    base = (face - 2) % 6 * 2 * FACE
    return grown[:, base : base + 2 * FACE]


def pack(grown, face):
    values = face_of(grown, face)
    rows = [values[e * STRIDE : (e + 1) * STRIDE] for e in range(ELEMS)]
    return jnp.concatenate(rows, axis=1)


def copies(tile, slot):
    lane = lax.broadcasted_iota(jnp.int32, tile.shape, 1)
    values = jnp.where(lane // FACE == slot, tile, 0.0)
    for shift in (FACE, 2 * FACE, 4 * FACE):
        values = values + pltpu.roll(values, shift, 1)
    return values


def unpack(tile):
    slot = lax.broadcasted_iota(jnp.int32, tile.shape, 1) // FACE
    level = [tile]
    for bit in (1, 2, 4):
        upper = slot & bit != 0
        without = [jnp.where(upper, pltpu.roll(a, bit * FACE, 1), a) for a in level]
        only = [jnp.where(upper, a, pltpu.roll(a, 128 - bit * FACE, 1)) for a in level]
        level = without + only
    return [level[e * 2 + kind] for kind in range(2) for e in range(ELEMS)]


def write_sends(odd_ref, grown, send_refs):
    p_odd, s_odd, r = (odd_ref[i * STRIDE : (i + 1) * STRIDE, :] > 0.5 for i in range(3))
    faces = [pack(grown, f) for f in range(6)]
    send_refs[0][...] = jnp.where(r, faces[4], faces[5])
    send_refs[1][...] = jnp.where(p_odd, faces[1], faces[0])
    send_refs[2][...] = jnp.where(s_odd, faces[2], faces[3])
    send_refs[3][...] = jnp.where(s_odd, faces[3], faces[2])
    send_refs[4][...] = jnp.where(p_odd, faces[0], faces[1])


def place_terms(groups, omask_ref, lay_ref, first_face):
    laid = []
    for i, terms in enumerate(groups):
        base = (first_face + 2 * i) * RW
        terms = terms * omask_ref[base : base + 2 * RW, :]
        laid += [terms[:RW], terms[RW:]]
    laid = jnp.concatenate(laid, axis=1)
    out = dot(jnp.concatenate(thirds(laid), axis=0).astype(jnp.bfloat16), lay_ref[first_face * 8 * FACE : LAID, :])
    return out[:RW] + (out[RW : 2 * RW] + out[2 * RW :])


def halo_part(recv, rem, omask_ref, lay_ref):
    rad, pass_b, span_a, span_b, pass_a = [unpack(r[...]) for r in recv]
    groups = []
    for pieces, mat in ((pass_a + pass_b, rem[0]), (span_a + span_b, rem[1]), (rad, rem[2])):
        groups.append(dot(mat[...], right_stack(jnp.concatenate(pieces, axis=0))))
    return place_terms(groups, omask_ref, lay_ref, 0)


def start_kernel(rs_ref, table_ref):
    rs = rs_ref[...]
    table_ref[...] = jnp.broadcast_to(scalar_row([total(rs * rs)]), table_ref.shape)


def prepare_kernel(rs_ref, mass_ref, ints_ref, restrict_ref, x_ref, massw_ref, member_ref, odd_ref, row_ref):
    x_ref[...] = jnp.zeros_like(x_ref)
    massw_ref[...] = jnp.zeros_like(massw_ref)
    for e in range(ELEMS):
        for v in range(VARS):
            lanes = slice(v * NODES, (v + 1) * NODES)
            row = e * STRIDE + v
            x_ref[row : row + 1, :] = rs_ref[e : e + 1, lanes]
            massw_ref[row : row + 1, :] = mass_ref[e : e + 1, lanes]
    member = member_mask(ints_ref)
    member_ref[...] = member
    row_ref[...] = coarse_row(member, restrict_ref, x_ref[...])
    for i in range(3):
        odd = (ints_ref[i, PLACE] % 2).astype(F32)
        odd_ref[i * STRIDE : (i + 1) * STRIDE, :] = jnp.full((STRIDE, 128), odd, F32)


def setup_kernel(
    ints_ref,
    volume_ref,
    flux_ref,
    visc_ref,
    blocks_ref,
    consts_ref,
    cinv_ref,
    rem0_ref,
    rem1_ref,
    rem2_ref,
    loc1_ref,
    loc2_ref,
    omask_ref,
    vmat_ref,
    cinv3_ref,
    turned_ref,
    coef_ref,
    amat_ref,
):
    p_odd, s_odd = ints_ref[0, PLACE] % 2, ints_ref[1, PLACE] % 2
    device = ints_ref[3, PLACE]
    coef_ref[...] = jnp.zeros_like(coef_ref)
    for u in range(VARS):
        here = slice(u * ELEMS, (u + 1) * ELEMS)
        for axis in range(3):
            coef_ref[here, 80 + axis * 8 : 80 + axis * 8 + VARS] = volume_ref[axis, u]
        for v in range(VARS):
            coef_ref[here, v * 8 : v * 8 + 6] = flux_ref[u, v]
            coef_ref[here, 40 + v * 8 : 40 + v * 8 + 6] = visc_ref[u, v]
    tile, codes, wall_signs, vtile, vmask, expand = (
        consts_ref[a : a + n, :lanes] for a, n, lanes in CONSTS
    )
    coef = exact_dot(expand, coef_ref[...])
    vmat_ref[...] = right_factor(exact_dot(coef[:, 80:104], vtile) * vmask)
    turned = cinv_ref[0, 0].T
    high = turned.astype(jnp.bfloat16)
    low = (turned - high.astype(F32)).astype(jnp.bfloat16)
    cinv3_ref[...] = jnp.concatenate([high, high, low], axis=0)
    for e in range(ELEMS):
        turned_ref[e] = blocks_ref[e].T
    face_lane = lax.broadcasted_iota(jnp.int32, (RW, 80), 1) % 8
    coef = [jnp.where(face_lane == f, coef[:, :80], 0.0) for f in range(6)]
    spread = exact_dot(jnp.concatenate(coef, axis=0), tile)
    lane = lax.broadcasted_iota(jnp.int32, (STRIDE, 8 * FACE), 1)
    for f in range(6):
        colcode = jnp.broadcast_to(codes[f : f + 1], (STRIDE, 256))
        signs = jnp.broadcast_to(wall_signs[f : f + 1], (STRIDE, 256))
        for e in range(ELEMS):
            near = ints_ref[e, NEIGH + f]
            tag = ints_ref[e, TAGS + f]
            spot = near % ELEMS
            crossing = near // ELEMS != device
            if f == 0:
                source = 1 - p_odd
            elif f == 1:
                source = p_odd
            elif f == 2:
                source = 3 - s_odd
            elif f == 3:
                source = 2 + s_odd
            else:
                source = jnp.where(crossing, 4, 8 if f == 4 else 7)
            code = source * ELEMS + spot
            turn_code = ints_ref[e, ORIENT + f]
            if f >= 2:
                wall_code = (5 + f - 2) * ELEMS + e
                code = jnp.where(tag == 0, code, jnp.where(tag == 1, wall_code, -1))
                turn_code = jnp.where(tag == 0, turn_code, 0)
            rows = slice(f * RW + e * STRIDE, f * RW + (e + 1) * STRIDE)
            values = spread[rows]
            values = jnp.where(tag == 1, values * signs, values)
            amat_ref[rows, :] = jnp.where(colcode == code.astype(F32), -values, 0.0)
            omask_ref[rows, :] = jnp.where(lane // FACE == turn_code, 1.0, 0.0)
    one = 2 * RW
    rem0_ref[...] = right_factor(amat_ref[:one, : 2 * one])
    rem1_ref[...] = right_factor(amat_ref[one : 2 * one, : 2 * one])
    loc1_ref[...] = right_factor(amat_ref[one : 2 * one, 2 * one : 4 * one])
    rem2_ref[...] = right_factor(amat_ref[2 * one :, :one])
    loc2_ref[...] = right_factor(amat_ref[2 * one :, one : 3 * one])


def coarse_kernel(r0, r1, r2, r3, cinv, member, lay, coarse_ref):
    coarse = (r0[...] + r1[...]) + (r2[...] + r3[...])
    coarse_ref[...] = coarse_values(coarse, cinv, member, lay)


def blocks_kernel(x, blocks, out_ref):
    out_ref[...] = apply_blocks(blocks, two_parts(x[...]))


def finish_first(odd, first, rise, first_ref, grown_ref, sends):
    first_ref[...] = first
    grown = dot(left_stack(first), rise[...])
    grown_ref[...] = grown
    write_sends(odd, grown, sends)


def first0_kernel(odd, table, x, coarse, blocks, rise, *outs):
    z_ref, coarse_ref, scal_ref, first_ref, grown_ref, *sends = outs
    beta = jnp.sqrt(read_scalars(table, 1)[0])
    z = x[...] / beta[:, :NODES]
    z_ref[...] = z
    scal_ref[...] = jnp.broadcast_to(beta, scal_ref.shape)
    scaled = coarse[...] / beta[:, :NODES]
    coarse_ref[...] = scaled
    first = apply_blocks(blocks, rounded(z)) + scaled
    finish_first(odd, first, rise, first_ref, grown_ref, sends)


def first1_kernel(odd, table, x, coarse, b0, coarse0, blocks, rise, *outs):
    z_ref, scal_ref, first_ref, grown_ref, *sends = outs
    h00, square = read_scalars(table, 2)
    h10 = jnp.sqrt(jnp.maximum(square - h00 * h00, 1e-7 * square))
    for i, value in enumerate((h00, h10, square)):
        scal_ref[i * STRIDE : (i + 1) * STRIDE, :] = jnp.broadcast_to(value, (STRIDE, 128))
    h00, h10 = h00[:, :NODES], h10[:, :NODES]
    z = (x[...] - h00 * b0[...]) / h10
    z_ref[...] = z
    scaled = (coarse[...] - h00 * coarse0[...]) / h10
    first = apply_blocks(blocks, rounded(z)) + scaled
    finish_first(odd, first, rise, first_ref, grown_ref, sends)


def first2_kernel(odd, r0, r1, r2, r3, fine, cinv, member, lay, rise, *outs):
    first_ref, grown_ref, *sends = outs
    coarse = (r0[...] + r1[...]) + (r2[...] + r3[...])
    first = fine[...] + coarse_values(coarse, cinv, member, lay)
    finish_first(odd, first, rise, first_ref, grown_ref, sends)


def local_kernel(x, grown_ref, mass, vmat, loc1, loc2, omask, lay, slope, out_ref):
    tile = grown_ref[:, :128]
    slopes = dot(left_stack(x[...]), slope[...])
    slopes = jnp.concatenate([slopes[:, i * NODES : (i + 1) * NODES] for i in range(3)], axis=0)
    result = 1.5 * mass[...] * x[...] + dot(vmat[...], right_stack(slopes))
    groups = []
    for faces, mat in (((2, 3), loc1), ((4, 5), loc2)):
        pieces = []
        for f in faces:
            slot = (f - 2) * 2
            pieces += [copies(tile, slot), copies(tile, slot + 1)]
        groups.append(dot(mat[...], right_stack(jnp.concatenate(pieces, axis=0))))
    out_ref[...] = result + place_terms(groups, omask, lay, 2)


def row_kernel(x, member, restrict, row_ref):
    row_ref[...] = coarse_row(member[...], restrict, x[...])


def second_kernel(step, *refs):
    odd, z, first, local = refs[:4]
    recv = refs[4:9]
    rem, omask, lay, blocks, rise = refs[9:12], *refs[12:16]
    search_ref, grown_ref, *sends = refs[16:]
    defect = z[...] - (local[...] + halo_part(recv, rem, omask, lay))
    parts = two_parts(defect) if step == 2 else rounded(defect)
    search = first[...] + apply_blocks(blocks, parts)
    search_ref[...] = search
    grown = dot(left_stack(search), rise[...])
    grown_ref[...] = grown
    write_sends(odd, grown, sends)


def third_kernel(step, *refs):
    local = refs[0]
    recv = refs[1:6]
    rem, omask, lay = refs[6:9], refs[9], refs[10]
    mapped = local[...] + halo_part(recv, rem, omask, lay)
    if step == 0:
        b0, w_ref, table_ref = refs[11:]
        scalars = [total(mapped * b0[...]), total(mapped * mapped)]
    elif step == 1:
        member, restrict, w_ref, row_ref = refs[11:]
    else:
        b0, b1, w1, w_ref, table_ref = refs[11:]
        scalars = [total(w1[...] * b[...]) for b in (b0, b1, w1)]
        scalars += [total(mapped * b[...]) for b in (b0, b1, w1)]
        scalars += [total(mapped * mapped)]
    w_ref[...] = mapped
    if step != 1:
        table_ref[...] = jnp.broadcast_to(scalar_row(scalars), table_ref.shape)
    if step == 1:
        row_ref[...] = coarse_row(member[...], restrict, mapped)


def inverse_sqrt(value):
    guess = lax.rsqrt(value)
    return guess * (1.5 - 0.5 * (value * guess) * guess)


def least_squares(matrix, beta):
    iters = len(matrix) - 1
    target = [beta] + [jnp.zeros_like(beta)] * iters
    inverse = []
    for k in range(iters):
        top, low = matrix[k][k], matrix[k + 1][k]
        scale = inverse_sqrt(top * top + low * low)
        inverse.append(scale)
        cosine, sine = top * scale, low * scale
        for later in range(k + 1, iters):
            upper, lower = matrix[k][later], matrix[k + 1][later]
            matrix[k][later] = cosine * upper + sine * lower
            matrix[k + 1][later] = -sine * upper + cosine * lower
        upper, lower = target[k], target[k + 1]
        target[k] = cosine * upper + sine * lower
        target[k + 1] = -sine * upper + cosine * lower
    weights = [None] * iters
    for k in reversed(range(iters)):
        value = target[k]
        for later in range(k + 1, iters):
            value = value - matrix[k][later] * weights[later]
        weights[k] = value * inverse[k]
    return weights


def final_kernel(table, scal0, scal1, x, s0, s1, s2, w0, w1, w2, update_ref, residual_ref):
    g0, g1, g2, q0, q1, qw, qq = read_scalars(table, 7)
    beta = scal0[0:1, :]
    h00, h10, square0 = [scal1[i * STRIDE : i * STRIDE + 1, :] for i in range(3)]
    h01, h11 = g0, g1
    squared = jnp.maximum(g2 - h01 * h01 - h11 * h11, 1e-7 * g2)
    inv21 = inverse_sqrt(squared)
    h21 = squared * inv21
    cross = h00 * h01 + h10 * h11
    h02 = (q0 - h01 * h00 - h11 * h01) * inv21
    h12 = (q1 - h01 * h10 - h11 * h11) * inv21
    with_w1 = (qw - h01 * cross - h11 * g2) * inv21
    h22 = (with_w1 - h01 * h02 - h11 * h12) * inv21
    with_w0 = h00 * q0 + h10 * q1
    square = qq + h01 * h01 * square0 + h11 * h11 * g2
    square = square - 2.0 * (h01 * with_w0 + h11 * qw - h01 * h11 * cross)
    square = square * inv21 * inv21
    h32 = jnp.sqrt(jnp.maximum(square - h02 * h02 - h12 * h12 - h22 * h22, 1e-7 * square))
    zero = jnp.zeros_like(beta)
    hess = [[h00, h01, h02], [h10, h11, h12], [zero, h21, h22], [zero, zero, h32]]
    y0, y1, y2 = least_squares(hess, beta)
    y2 = y2 * inv21
    y0 = y0 - y2 * h01
    y1 = y1 - y2 * h11
    y0, y1, y2 = (y[:, :NODES] for y in (y0, y1, y2))
    update = y0 * s0[...] + y1 * s1[...] + y2 * s2[...]
    residual = x[...] - (y0 * w0[...] + y1 * w1[...] + y2 * w2[...])
    for e in range(ELEMS):
        for v in range(VARS):
            lanes = slice(v * NODES, (v + 1) * NODES)
            row = e * STRIDE + v
            update_ref[e : e + 1, lanes] = update[row : row + 1, :]
            residual_ref[e : e + 1, lanes] = residual[row : row + 1, :]


VMEM = pltpu.VMEM
SMEM = pltpu.SMEM


def shape_of(out):
    return out if isinstance(out, jax.ShapeDtypeStruct) else jax.ShapeDtypeStruct(out, F32)


def call(kernel, name, args, outs, smem=(), scratch=(), raw=()):
    return pl.pallas_call(
        kernel,
        name=name,
        out_shape=[shape_of(out) for out in outs],
        in_specs=[
            pl.BlockSpec()
            if i in raw
            else pl.BlockSpec(memory_space=SMEM if i in smem else VMEM)
            for i in range(len(args))
        ],
        out_specs=[pl.BlockSpec(memory_space=VMEM)] * len(outs),
        scratch_shapes=[VMEM(shape, F32) for shape in scratch],
        compiler_params=pltpu.CompilerParams(vmem_limit_bytes=32 * 1024 * 1024),
    )(*args)


def with_step(kernel, step):
    def run(*refs):
        kernel(step, *refs)

    return run


def body(
    right_side,
    mass,
    volume_jac,
    face_flux,
    face_visc,
    block_inverse,
    coarse_inverse,
    neighbours,
    orientation,
    bc_tags,
    coarse_group,
):
    t = {name: jnp.asarray(value) for name, value in tables().items()}
    n_pass, n_span = lax.axis_size("passage"), lax.axis_size("span")
    n_rad = lax.axis_size("radial")
    devices = n_pass * n_span * n_rad
    p, s, r = (lax.axis_index(a) for a in AXES)
    place = jnp.stack([p, s, r, (p * n_span + s) * n_rad + r]).astype(jnp.int32)
    ints = [neighbours, orientation, bc_tags, coarse_group[:, None], place[:, None]]
    ints = jnp.concatenate(ints, axis=1)
    volume_t = jnp.transpose(volume_jac, (1, 2, 0, 3))
    flux_t, visc_t = (jnp.transpose(a, (2, 3, 0, 1)) for a in (face_flux, face_visc))

    pass_a = [(i, i ^ 1) for i in range(n_pass)]
    pass_b = [(i, (i + 1 if i % 2 else i - 1) % n_pass) for i in range(n_pass)]
    span_a = [(i, i ^ 1) for i in range(n_span)]
    span_b = [(i, (i + 1 if i % 2 else i - 1) % n_span) for i in range(n_span)]
    rad = [(0, 1), (1, 0)]

    def exchange(sends):
        ways = (
            ("radial", rad),
            ("passage", pass_b),
            ("span", span_a),
            ("span", span_b),
            ("passage", pass_a),
        )
        return [lax.ppermute(x, axis, way) for x, (axis, way) in zip(sends, ways)]

    def span_rows(row):
        return [row] + [
            lax.ppermute(row, "span", [(i, i ^ k) for i in range(n_span)]) for k in (2, 3, 1)
        ]

    vec = (RW, NODES)
    grow = (RW, GROWN)
    send = (STRIDE, 128)
    table_shape = (devices, 128)

    def half_floats(*shape):
        return jax.ShapeDtypeStruct(shape, jnp.bfloat16)

    (table,) = call(start_kernel, "start", (right_side,), [table_shape], raw=(0,))
    table = lax.all_to_all(table, AXES, 0, 0, tiled=True)
    x, massw, member, odd, row = call(
        prepare_kernel,
        "prepare",
        (right_side, mass, ints, t["restrict"]),
        [vec, vec, (RW, WIDE), (3 * STRIDE, 128), (1, WIDE)],
        smem=(2,),
        raw=(0, 1, 3),
    )
    rows = span_rows(row)
    pair = half_floats(2 * RW, 6 * 4 * RW)
    rem0, rem1, rem2, loc1, loc2, omask, vmat, cinv3, turned = call(
        setup_kernel,
        "setup",
        (
            ints,
            volume_t,
            flux_t,
            visc_t,
            block_inverse,
            t["consts"],
            coarse_inverse,
        ),
        [
            pair,
            pair,
            half_floats(2 * RW, 6 * 2 * RW),
            pair,
            pair,
            (6 * RW, 8 * FACE),
            half_floats(RW, 18 * RW),
            half_floats(3 * KC, KC),
            half_floats(*block_inverse.shape),
        ],
        smem=(0,),
        raw=tuple(range(1, 7)),
        scratch=[(24, 104), (6 * RW, 256)],
    )
    remote = (rem0, rem1, rem2, omask, t["lay"])
    near = (massw, vmat, loc1, loc2, omask, t["lay"], t["slope"])

    def local_part(vector, grown, step):
        return call(local_kernel, "local%d" % step, (vector, grown) + near, [vec])[0]

    coarse_tables = (cinv3, member, t["lay"])
    tail = (turned, t["rise"])
    basis, search, images, scalars = [], [], [], []
    coarse0 = None
    outs = [vec, grow] + [send] * 5
    for step in range(3):
        if step < 2:
            (coarse,) = call(coarse_kernel, "coarse%d" % step, (*rows, *coarse_tables), [vec])
        if step == 0:
            z, coarse0, scal, first, grown, *sends = call(
                first0_kernel,
                "first0",
                (odd, table, x, coarse) + tail,
                [vec, vec, (8, 128)] + outs,
            )
            scalars.append(scal)
        elif step == 1:
            z, scal, first, grown, *sends = call(
                first1_kernel,
                "first1",
                (odd, table, images[0], coarse, basis[0], coarse0) + tail,
                [vec, (3 * STRIDE, 128)] + outs,
            )
            scalars.append(scal)
        else:
            z = images[1]
            (fine,) = call(blocks_kernel, "fine", (z, turned), [vec])
            first, grown, *sends = call(
                first2_kernel,
                "first2",
                (odd, *rows, fine, *coarse_tables, t["rise"]),
                outs,
            )
        basis.append(z)
        recv = exchange(sends)
        local = local_part(first, grown, step)
        direction, grown, *sends = call(
            with_step(second_kernel, step),
            "second%d" % step,
            (odd, z, first, local, *recv) + remote + tail,
            outs,
        )
        search.append(direction)
        recv = exchange(sends)
        local = local_part(direction, grown, step)
        kernel = with_step(third_kernel, step)
        args = (local, *recv) + remote
        if step == 0:
            image, table = call(kernel, "third0", args + (basis[0],), [vec, table_shape])
            table = lax.all_to_all(table, AXES, 0, 0, tiled=True)
            (row,) = call(row_kernel, "row0", (image, member, t["restrict"]), [(1, WIDE)])
            rows = span_rows(row)
        elif step == 1:
            image, row = call(kernel, "third1", args + (member, t["restrict"]), [vec, (1, WIDE)])
            rows = span_rows(row)
        else:
            image, table = call(kernel, "third2", args + tuple(basis), [vec, table_shape])
            table = lax.all_to_all(table, AXES, 0, 0, tiled=True)
        images.append(image)

    update, residual = call(
        final_kernel,
        "final",
        (table, *scalars, x, *search, *images),
        [right_side.shape] * 2,
    )
    return (update, residual)


def solution(mesh):
    rows = P(AXES, None)
    blocks = P(AXES, None, None)
    jac = P(AXES, None, None, None)
    in_specs = (
        rows,
        rows,
        jac,
        jac,
        jac,
        blocks,
        P("passage", "radial", None, None),
        rows,
        rows,
        rows,
        P(AXES),
    )
    return jax.shard_map(body, mesh=mesh, in_specs=in_specs, out_specs=(rows, rows), check_vma=False)
```

```python
import math

import jax
import jax.numpy as jnp
import numpy as np
from jax import lax
from jax.experimental import pallas as pl
from jax.experimental.pallas import tpu as pltpu
from jax.sharding import PartitionSpec as P

QN = 4
VARS = 5
CG = 4
ELEMS = 4
NODES = QN**3
ROWS = 320
KC = 160
STRIDE = 8
RW = ELEMS * STRIDE
FACE = QN * QN
SOURCES = ((0, 1), (2, 3, 5, 6), (4, 7, 8))
WIDE = 256
AXES = ("passage", "span", "radial")
NEIGH, ORIENT, TAGS, GROUP, PLACE = 0, 6, 12, 18, 19
HIGHEST = lax.Precision.HIGHEST
GROWN = 6 * 2 * FACE
LAID = 6 * 8 * FACE
CONSTS = ((0, 80, 256), (80, 8, 256), (88, 8, 256), (96, 24, 96), (120, 32, 96), (152, 32, 24))
F32 = jnp.float32


def lobatto_nodes():
    inner_node = 1.0 / math.sqrt(5.0)
    return np.array([-1.0, -inner_node, inner_node, 1.0])


def derivative_table():
    nodes = lobatto_nodes()
    weights = np.ones(QN)
    for row_id in range(QN):
        for col_id in range(QN):
            if col_id != row_id:
                weights[row_id] = weights[row_id] / (nodes[row_id] - nodes[col_id])
    result = np.zeros((QN, QN))
    for row_id in range(QN):
        for col_id in range(QN):
            if col_id != row_id:
                result[row_id, col_id] = (
                    weights[col_id] / weights[row_id] / (nodes[row_id] - nodes[col_id])
                )
        result[row_id, row_id] = -np.sum(result[row_id])
    return result


def vertex_table():
    nodes = lobatto_nodes()
    shapes = np.stack([(1.0 - nodes) / 2.0, (1.0 + nodes) / 2.0])
    first_part = shapes[:, None, None, :, None, None]
    second_part = shapes[None, :, None, None, :, None]
    third_part = shapes[None, None, :, None, None, :]
    return (first_part * second_part * third_part).reshape(8, NODES)


def coords(node):
    return (node // 16, node // 4 % 4, node % 4)


def others(node, axis):
    picked = [c for i, c in enumerate(coords(node)) if i != axis]
    return picked[0] * QN + picked[1]


def layer_of(face):
    return 0 if face % 2 == 0 else QN - 1


def stacked(values):
    high = values.astype(jnp.bfloat16)
    rest = values - high.astype(np.float32)
    mid = rest.astype(jnp.bfloat16)
    low = (rest - mid.astype(np.float32)).astype(jnp.bfloat16)
    return np.concatenate([high, high, high, mid, mid, low], axis=0)


def short_stacked(values):
    high = values.astype(jnp.bfloat16)
    low = (values - high.astype(np.float32)).astype(jnp.bfloat16)
    return np.concatenate([high, high, low], axis=0)


def tables():
    dmat = derivative_table()
    de = np.zeros((NODES, 3 * NODES + 6 * 2 * FACE), np.float32)
    place = np.zeros((6, 1, FACE, NODES), np.float32)
    for node in range(NODES):
        for axis in range(3):
            for target in range(NODES):
                if others(node, axis) == others(target, axis):
                    de[node, axis * NODES + target] = dmat[
                        coords(target)[axis], coords(node)[axis]
                    ]
        for face in range(6):
            axis = face // 2
            spot = others(node, axis)
            base = 3 * NODES + (face - 2) % 6 * 2 * FACE
            de[node, base + FACE + spot] = dmat[layer_of(face), coords(node)[axis]]
            if coords(node)[axis] == layer_of(face):
                de[node, base + spot] = 1.0
                place[face, :, spot, node] = 1.0
    turn = np.zeros((FACE, 8, FACE), np.float32)
    for code in range(8):
        for i in range(QN):
            for j in range(QN):
                a = QN - 1 - i if code & 2 else i
                b = QN - 1 - j if code & 1 else j
                if code & 4:
                    a, b = b, a
                turn[a * QN + b, code, i * QN + j] = 1.0
    rtab = vertex_table().astype(np.float32)
    restrict = np.zeros((NODES, WIDE), np.float32)
    restrict[:, :KC] = np.tile(rtab.T, (1, CG * VARS))
    lay = np.einsum("aob,fbk->foak", turn, place[:, 0]).reshape(6 * 8 * FACE, NODES)
    tile = np.zeros((80, 256), np.float32)
    for col in range(256):
        kind, v = col // RW % 2, col % STRIDE
        if v < VARS:
            tile[kind * 40 + v * 8 : kind * 40 + v * 8 + 6, col] = 1.0
    code = np.full((8, 256), -100.0, np.float32)
    sign = np.ones((8, 256), np.float32)
    for face in range(6):
        axis = face // 2
        for place_id, source in enumerate(SOURCES[axis]):
            for col in range(2 * RW):
                kind, n, v = col // RW, col // STRIDE % ELEMS, col % STRIDE
                lane = place_id * 2 * RW + col
                code[face, lane] = source * ELEMS + n
                sign[face, lane] = (-1.0 if v == 1 + axis else 1.0) * (-1.0 if kind else 1.0)
    rows = np.zeros((RW, 24), np.float32)
    for e in range(ELEMS):
        for u in range(VARS):
            rows[e * STRIDE + u, u * ELEMS + e] = 1.0
    vtile = np.zeros((24, 3 * RW), np.float32)
    vmask = np.zeros((RW, 3 * RW), np.float32)
    for col in range(3 * RW):
        axis, n, v = col // RW, col // STRIDE % ELEMS, col % STRIDE
        if v < VARS:
            vtile[axis * 8 + v, col] = 1.0
        vmask[n * STRIDE : (n + 1) * STRIDE, col] = 1.0
    consts = np.zeros((184, 256), np.float32)
    for (row, count, lanes), part in zip(CONSTS, (tile, code, sign, vtile, vmask, rows)):
        consts[row : row + count, :lanes] = part
    return dict(
        consts=consts,
        rise=stacked(de[:, 3 * NODES :]),
        slope=stacked(de[:, : 3 * NODES]),
        restrict=short_stacked(restrict),
        lay=np.concatenate(
            [lay.astype(jnp.bfloat16), short_stacked(np.ascontiguousarray(restrict.T))], axis=0
        ),
    )


def exact_dot(a, b):
    return jnp.dot(a, b, precision=HIGHEST, preferred_element_type=F32)


def thirds(values):
    high = values.astype(jnp.bfloat16).astype(F32)
    rest = values - high
    mid = rest.astype(jnp.bfloat16).astype(F32)
    return high, mid, rest - mid


def left_stack(values):
    high, mid, low = thirds(values)
    return jnp.concatenate([high, mid, low, high, mid, high], axis=1).astype(jnp.bfloat16)


def short_stack(values):
    high = values.astype(jnp.bfloat16).astype(F32)
    return jnp.concatenate([high, values - high, high], axis=1).astype(jnp.bfloat16)


def right_stack(values):
    high, mid, low = (part.astype(jnp.bfloat16) for part in thirds(values))
    return jnp.concatenate([high, mid, low, high, mid, high], axis=0)


def right_factor(values):
    high, mid, low = thirds(values)
    return jnp.concatenate([high, high, high, mid, mid, low], axis=1).astype(jnp.bfloat16)


def dot(a, b):
    return jnp.dot(a, b, preferred_element_type=F32)


def total(values):
    return jnp.sum(values, axis=(0, 1), keepdims=True)


def member_mask(ints_ref):
    row = lax.broadcasted_iota(jnp.int32, (STRIDE, WIDE), 0)
    lane = lax.broadcasted_iota(jnp.int32, (STRIDE, WIDE), 1)
    pieces = []
    for e in range(ELEMS):
        hit = (lane // (VARS * 8) == ints_ref[e, GROUP]) & (lane // 8 % VARS == row)
        pieces.append(jnp.where(hit & (lane < KC), 1.0, 0.0))
    return jnp.concatenate(pieces, axis=0)


def coarse_row(member, restrict_ref, vector):
    return jnp.sum(member * dot(short_stack(vector), restrict_ref[...]), axis=0, keepdims=True)


def scalar_row(scalars):
    lane = lax.broadcasted_iota(jnp.int32, (1, 128), 1)
    row = jnp.zeros((1, 128), F32)
    for i, value in enumerate(scalars):
        row = jnp.where(lane == i, value, row)
    return row


def read_scalars(table_ref, count):
    sums = jnp.sum(table_ref[...], axis=0, keepdims=True)
    return [jnp.broadcast_to(sums[:, i : i + 1], (1, 128)) for i in range(count)]


def coarse_values(coarse, cinv_ref, member_ref, lay_ref):
    solved = dot(short_stack(coarse[:, :KC]), cinv_ref[...])
    solved = jnp.concatenate([solved, jnp.zeros((1, WIDE - KC), F32)], axis=1)
    return dot(short_stack(member_ref[...] * solved), lay_ref[LAID:, :])


def apply_blocks(turned_ref, parts):
    row = lax.broadcasted_iota(jnp.int32, (RW, ROWS), 0) % STRIDE
    own_lanes = lax.broadcasted_iota(jnp.int32, (RW, ROWS), 1) // NODES == row
    stacked = []
    for part in parts:
        pair = jnp.concatenate([part, part], axis=1)
        stacked.append(jnp.where(own_lanes, jnp.concatenate([pair, pair, part], axis=1), 0.0))
    pieces = []
    for e in range(ELEMS):
        rows = [part[e * STRIDE : (e + 1) * STRIDE] for part in stacked]
        rows = jnp.concatenate(rows, axis=0) if len(rows) > 1 else rows[0]
        out = dot(rows.astype(jnp.bfloat16), turned_ref[e])
        pieces.append(jnp.broadcast_to(jnp.sum(out, axis=0, keepdims=True), (STRIDE, ROWS)))
    full = jnp.where(own_lanes, jnp.concatenate(pieces, axis=0), 0.0)
    half = full[:, :128] + full[:, 128:256]
    return half[:, :NODES] + half[:, NODES:] + full[:, 256:]


def rounded(values):
    return [values.astype(jnp.bfloat16).astype(F32)]


def two_parts(values):
    high = values.astype(jnp.bfloat16).astype(F32)
    return [high, values - high]


def face_of(grown, face):
    base = (face - 2) % 6 * 2 * FACE
    return grown[:, base : base + 2 * FACE]


def pack(grown, face):
    values = face_of(grown, face)
    rows = [values[e * STRIDE : (e + 1) * STRIDE] for e in range(ELEMS)]
    return jnp.concatenate(rows, axis=1)


def copies(tile, slot):
    lane = lax.broadcasted_iota(jnp.int32, tile.shape, 1)
    values = jnp.where(lane // FACE == slot, tile, 0.0)
    for shift in (FACE, 2 * FACE, 4 * FACE):
        values = values + pltpu.roll(values, shift, 1)
    return values


def unpack(tile):
    slot = lax.broadcasted_iota(jnp.int32, tile.shape, 1) // FACE
    level = [tile]
    for bit in (1, 2, 4):
        upper = slot & bit != 0
        without = [jnp.where(upper, pltpu.roll(a, bit * FACE, 1), a) for a in level]
        only = [jnp.where(upper, a, pltpu.roll(a, 128 - bit * FACE, 1)) for a in level]
        level = without + only
    return [level[e * 2 + kind] for kind in range(2) for e in range(ELEMS)]


def write_sends(odd_ref, grown, send_refs):
    p_odd, s_odd, r = (odd_ref[i * STRIDE : (i + 1) * STRIDE, :] > 0.5 for i in range(3))
    faces = [pack(grown, f) for f in range(6)]
    send_refs[0][...] = jnp.where(r, faces[4], faces[5])
    send_refs[1][...] = jnp.where(p_odd, faces[1], faces[0])
    send_refs[2][...] = jnp.where(s_odd, faces[2], faces[3])
    send_refs[3][...] = jnp.where(s_odd, faces[3], faces[2])
    send_refs[4][...] = jnp.where(p_odd, faces[0], faces[1])


def place_terms(groups, omask_ref, lay_ref, first_face):
    laid = []
    for i, terms in enumerate(groups):
        base = (first_face + 2 * i) * RW
        terms = terms * omask_ref[base : base + 2 * RW, :]
        laid += [terms[:RW], terms[RW:]]
    laid = jnp.concatenate(laid, axis=1)
    out = dot(jnp.concatenate(thirds(laid), axis=0).astype(jnp.bfloat16), lay_ref[first_face * 8 * FACE : LAID, :])
    return out[:RW] + (out[RW : 2 * RW] + out[2 * RW :])


def halo_part(recv, rem, omask_ref, lay_ref):
    rad, pass_b, span_a, span_b, pass_a = [unpack(r[...]) for r in recv]
    groups = []
    for pieces, mat in ((pass_a + pass_b, rem[0]), (span_a + span_b, rem[1]), (rad, rem[2])):
        groups.append(dot(mat[...], right_stack(jnp.concatenate(pieces, axis=0))))
    return place_terms(groups, omask_ref, lay_ref, 0)


def start_kernel(rs_hbm, table_ref, rs_ref, sem):
    copy = pltpu.make_async_copy(rs_hbm, rs_ref, sem)
    copy.start()
    copy.wait()
    rs = rs_ref[...]
    table_ref[...] = jnp.broadcast_to(scalar_row([total(rs * rs)]), table_ref.shape)


def prepare_kernel(rs_ref, mass_ref, ints_ref, restrict_ref, x_ref, massw_ref, member_ref, odd_ref, row_ref):
    x_ref[...] = jnp.zeros_like(x_ref)
    massw_ref[...] = jnp.zeros_like(massw_ref)
    for e in range(ELEMS):
        for v in range(VARS):
            lanes = slice(v * NODES, (v + 1) * NODES)
            row = e * STRIDE + v
            x_ref[row : row + 1, :] = rs_ref[e : e + 1, lanes]
            massw_ref[row : row + 1, :] = mass_ref[e : e + 1, lanes]
    member = member_mask(ints_ref)
    member_ref[...] = member
    row_ref[...] = coarse_row(member, restrict_ref, x_ref[...])
    for i in range(3):
        odd = (ints_ref[i, PLACE] % 2).astype(F32)
        odd_ref[i * STRIDE : (i + 1) * STRIDE, :] = jnp.full((STRIDE, 128), odd, F32)


def setup_kernel(
    ints_ref,
    volume_ref,
    flux_ref,
    visc_ref,
    blocks_ref,
    consts_ref,
    cinv_ref,
    rem0_ref,
    rem1_ref,
    rem2_ref,
    loc1_ref,
    loc2_ref,
    omask_ref,
    vmat_ref,
    cinv3_ref,
    turned_ref,
    coef_ref,
    amat_ref,
):
    p_odd, s_odd = ints_ref[0, PLACE] % 2, ints_ref[1, PLACE] % 2
    device = ints_ref[3, PLACE]
    coef_ref[...] = jnp.zeros_like(coef_ref)
    for u in range(VARS):
        here = slice(u * ELEMS, (u + 1) * ELEMS)
        for axis in range(3):
            coef_ref[here, 80 + axis * 8 : 80 + axis * 8 + VARS] = volume_ref[axis, u]
        for v in range(VARS):
            coef_ref[here, v * 8 : v * 8 + 6] = flux_ref[u, v]
            coef_ref[here, 40 + v * 8 : 40 + v * 8 + 6] = visc_ref[u, v]
    tile, codes, wall_signs, vtile, vmask, expand = (
        consts_ref[a : a + n, :lanes] for a, n, lanes in CONSTS
    )
    coef = exact_dot(expand, coef_ref[...])
    vmat_ref[...] = right_factor(exact_dot(coef[:, 80:104], vtile) * vmask)
    turned = cinv_ref[0, 0].T
    high = turned.astype(jnp.bfloat16)
    low = (turned - high.astype(F32)).astype(jnp.bfloat16)
    cinv3_ref[...] = jnp.concatenate([high, high, low], axis=0)
    for e in range(ELEMS):
        turned_ref[e] = blocks_ref[e].T
    face_lane = lax.broadcasted_iota(jnp.int32, (RW, 80), 1) % 8
    coef = [jnp.where(face_lane == f, coef[:, :80], 0.0) for f in range(6)]
    spread = exact_dot(jnp.concatenate(coef, axis=0), tile)
    lane = lax.broadcasted_iota(jnp.int32, (STRIDE, 8 * FACE), 1)
    for f in range(6):
        colcode = jnp.broadcast_to(codes[f : f + 1], (STRIDE, 256))
        signs = jnp.broadcast_to(wall_signs[f : f + 1], (STRIDE, 256))
        for e in range(ELEMS):
            near = ints_ref[e, NEIGH + f]
            tag = ints_ref[e, TAGS + f]
            spot = near % ELEMS
            crossing = near // ELEMS != device
            if f == 0:
                source = 1 - p_odd
            elif f == 1:
                source = p_odd
            elif f == 2:
                source = 3 - s_odd
            elif f == 3:
                source = 2 + s_odd
            else:
                source = jnp.where(crossing, 4, 8 if f == 4 else 7)
            code = source * ELEMS + spot
            turn_code = ints_ref[e, ORIENT + f]
            if f >= 2:
                wall_code = (5 + f - 2) * ELEMS + e
                code = jnp.where(tag == 0, code, jnp.where(tag == 1, wall_code, -1))
                turn_code = jnp.where(tag == 0, turn_code, 0)
            rows = slice(f * RW + e * STRIDE, f * RW + (e + 1) * STRIDE)
            values = spread[rows]
            values = jnp.where(tag == 1, values * signs, values)
            amat_ref[rows, :] = jnp.where(colcode == code.astype(F32), -values, 0.0)
            omask_ref[rows, :] = jnp.where(lane // FACE == turn_code, 1.0, 0.0)
    one = 2 * RW
    rem0_ref[...] = right_factor(amat_ref[:one, : 2 * one])
    rem1_ref[...] = right_factor(amat_ref[one : 2 * one, : 2 * one])
    loc1_ref[...] = right_factor(amat_ref[one : 2 * one, 2 * one : 4 * one])
    rem2_ref[...] = right_factor(amat_ref[2 * one :, :one])
    loc2_ref[...] = right_factor(amat_ref[2 * one :, one : 3 * one])


def coarse_kernel(r0, r1, r2, r3, cinv, member, lay, coarse_ref):
    coarse = (r0[...] + r1[...]) + (r2[...] + r3[...])
    coarse_ref[...] = coarse_values(coarse, cinv, member, lay)


def blocks_kernel(x, blocks, out_ref):
    out_ref[...] = apply_blocks(blocks, two_parts(x[...]))


def finish_first(odd, first, rise, first_ref, grown_ref, sends):
    first_ref[...] = first
    grown = dot(left_stack(first), rise[...])
    grown_ref[...] = grown
    write_sends(odd, grown, sends)


def first0_kernel(odd, table, x, coarse, blocks, rise, *outs):
    z_ref, coarse_ref, scal_ref, first_ref, grown_ref, *sends = outs
    beta = jnp.sqrt(read_scalars(table, 1)[0])
    z = x[...] / beta[:, :NODES]
    z_ref[...] = z
    scal_ref[...] = jnp.broadcast_to(beta, scal_ref.shape)
    scaled = coarse[...] / beta[:, :NODES]
    coarse_ref[...] = scaled
    first = apply_blocks(blocks, rounded(z)) + scaled
    finish_first(odd, first, rise, first_ref, grown_ref, sends)


def first1_kernel(odd, table, x, coarse, b0, coarse0, blocks, rise, *outs):
    z_ref, scal_ref, first_ref, grown_ref, *sends = outs
    h00, square = read_scalars(table, 2)
    h10 = jnp.sqrt(jnp.maximum(square - h00 * h00, 1e-7 * square))
    for i, value in enumerate((h00, h10, square)):
        scal_ref[i * STRIDE : (i + 1) * STRIDE, :] = jnp.broadcast_to(value, (STRIDE, 128))
    h00, h10 = h00[:, :NODES], h10[:, :NODES]
    z = (x[...] - h00 * b0[...]) / h10
    z_ref[...] = z
    scaled = (coarse[...] - h00 * coarse0[...]) / h10
    first = apply_blocks(blocks, rounded(z)) + scaled
    finish_first(odd, first, rise, first_ref, grown_ref, sends)


def first2_kernel(odd, r0, r1, r2, r3, fine, cinv, member, lay, rise, *outs):
    first_ref, grown_ref, *sends = outs
    coarse = (r0[...] + r1[...]) + (r2[...] + r3[...])
    first = fine[...] + coarse_values(coarse, cinv, member, lay)
    finish_first(odd, first, rise, first_ref, grown_ref, sends)


def local_kernel(x, grown_ref, mass, vmat, loc1, loc2, omask, lay, slope, out_ref):
    tile = grown_ref[:, :128]
    slopes = dot(left_stack(x[...]), slope[...])
    slopes = jnp.concatenate([slopes[:, i * NODES : (i + 1) * NODES] for i in range(3)], axis=0)
    result = 1.5 * mass[...] * x[...] + dot(vmat[...], right_stack(slopes))
    groups = []
    for faces, mat in (((2, 3), loc1), ((4, 5), loc2)):
        pieces = []
        for f in faces:
            slot = (f - 2) * 2
            pieces += [copies(tile, slot), copies(tile, slot + 1)]
        groups.append(dot(mat[...], right_stack(jnp.concatenate(pieces, axis=0))))
    out_ref[...] = result + place_terms(groups, omask, lay, 2)


def row_kernel(x, member, restrict, row_ref):
    row_ref[...] = coarse_row(member[...], restrict, x[...])


def second_kernel(step, *refs):
    odd, z, first, local = refs[:4]
    recv = refs[4:9]
    rem, omask, lay, blocks, rise = refs[9:12], *refs[12:16]
    search_ref, grown_ref, *sends = refs[16:]
    defect = z[...] - (local[...] + halo_part(recv, rem, omask, lay))
    parts = two_parts(defect) if step == 2 else rounded(defect)
    search = first[...] + apply_blocks(blocks, parts)
    search_ref[...] = search
    grown = dot(left_stack(search), rise[...])
    grown_ref[...] = grown
    write_sends(odd, grown, sends)


def third_kernel(step, *refs):
    local = refs[0]
    recv = refs[1:6]
    rem, omask, lay = refs[6:9], refs[9], refs[10]
    mapped = local[...] + halo_part(recv, rem, omask, lay)
    if step == 0:
        b0, w_ref, table_ref = refs[11:]
        scalars = [total(mapped * b0[...]), total(mapped * mapped)]
    elif step == 1:
        member, restrict, w_ref, row_ref = refs[11:]
    else:
        b0, b1, w1, w_ref, table_ref = refs[11:]
        scalars = [total(w1[...] * b[...]) for b in (b0, b1, w1)]
        scalars += [total(mapped * b[...]) for b in (b0, b1, w1)]
        scalars += [total(mapped * mapped)]
    w_ref[...] = mapped
    if step != 1:
        table_ref[...] = jnp.broadcast_to(scalar_row(scalars), table_ref.shape)
    if step == 1:
        row_ref[...] = coarse_row(member[...], restrict, mapped)


def inverse_sqrt(value):
    guess = lax.rsqrt(value)
    return guess * (1.5 - 0.5 * (value * guess) * guess)


def least_squares(matrix, beta):
    iters = len(matrix) - 1
    target = [beta] + [jnp.zeros_like(beta)] * iters
    inverse = []
    for k in range(iters):
        top, low = matrix[k][k], matrix[k + 1][k]
        scale = inverse_sqrt(top * top + low * low)
        inverse.append(scale)
        cosine, sine = top * scale, low * scale
        for later in range(k + 1, iters):
            upper, lower = matrix[k][later], matrix[k + 1][later]
            matrix[k][later] = cosine * upper + sine * lower
            matrix[k + 1][later] = -sine * upper + cosine * lower
        upper, lower = target[k], target[k + 1]
        target[k] = cosine * upper + sine * lower
        target[k + 1] = -sine * upper + cosine * lower
    weights = [None] * iters
    for k in reversed(range(iters)):
        value = target[k]
        for later in range(k + 1, iters):
            value = value - matrix[k][later] * weights[later]
        weights[k] = value * inverse[k]
    return weights


def final_kernel(table, scal0, scal1, x, s0, s1, s2, w0, w1, w2, update_ref, residual_ref):
    g0, g1, g2, q0, q1, qw, qq = read_scalars(table, 7)
    beta = scal0[0:1, :]
    h00, h10, square0 = [scal1[i * STRIDE : i * STRIDE + 1, :] for i in range(3)]
    h01, h11 = g0, g1
    squared = jnp.maximum(g2 - h01 * h01 - h11 * h11, 1e-7 * g2)
    inv21 = inverse_sqrt(squared)
    h21 = squared * inv21
    cross = h00 * h01 + h10 * h11
    h02 = (q0 - h01 * h00 - h11 * h01) * inv21
    h12 = (q1 - h01 * h10 - h11 * h11) * inv21
    with_w1 = (qw - h01 * cross - h11 * g2) * inv21
    h22 = (with_w1 - h01 * h02 - h11 * h12) * inv21
    with_w0 = h00 * q0 + h10 * q1
    square = qq + h01 * h01 * square0 + h11 * h11 * g2
    square = square - 2.0 * (h01 * with_w0 + h11 * qw - h01 * h11 * cross)
    square = square * inv21 * inv21
    h32 = jnp.sqrt(jnp.maximum(square - h02 * h02 - h12 * h12 - h22 * h22, 1e-7 * square))
    zero = jnp.zeros_like(beta)
    hess = [[h00, h01, h02], [h10, h11, h12], [zero, h21, h22], [zero, zero, h32]]
    y0, y1, y2 = least_squares(hess, beta)
    y2 = y2 * inv21
    y0 = y0 - y2 * h01
    y1 = y1 - y2 * h11
    y0, y1, y2 = (y[:, :NODES] for y in (y0, y1, y2))
    update = y0 * s0[...] + y1 * s1[...] + y2 * s2[...]
    residual = x[...] - (y0 * w0[...] + y1 * w1[...] + y2 * w2[...])
    for e in range(ELEMS):
        for v in range(VARS):
            lanes = slice(v * NODES, (v + 1) * NODES)
            row = e * STRIDE + v
            update_ref[e : e + 1, lanes] = update[row : row + 1, :]
            residual_ref[e : e + 1, lanes] = residual[row : row + 1, :]


VMEM = pltpu.VMEM
SMEM = pltpu.SMEM


def shape_of(out):
    return out if isinstance(out, jax.ShapeDtypeStruct) else jax.ShapeDtypeStruct(out, F32)


def call(kernel, name, args, outs, smem=(), scratch=(), raw=()):
    return pl.pallas_call(
        kernel,
        name=name,
        out_shape=[shape_of(out) for out in outs],
        in_specs=[
            pl.BlockSpec()
            if i in raw
            else pl.BlockSpec(memory_space=SMEM if i in smem else VMEM)
            for i in range(len(args))
        ],
        out_specs=[pl.BlockSpec(memory_space=VMEM)] * len(outs),
        scratch_shapes=[VMEM(shape, F32) for shape in scratch],
        compiler_params=pltpu.CompilerParams(vmem_limit_bytes=32 * 1024 * 1024),
    )(*args)


def with_step(kernel, step):
    def run(*refs):
        kernel(step, *refs)

    return run


def body(
    right_side,
    mass,
    volume_jac,
    face_flux,
    face_visc,
    block_inverse,
    coarse_inverse,
    neighbours,
    orientation,
    bc_tags,
    coarse_group,
):
    t = {name: jnp.asarray(value) for name, value in tables().items()}
    n_pass, n_span = lax.axis_size("passage"), lax.axis_size("span")
    n_rad = lax.axis_size("radial")
    devices = n_pass * n_span * n_rad
    p, s, r = (lax.axis_index(a) for a in AXES)
    place = jnp.stack([p, s, r, (p * n_span + s) * n_rad + r]).astype(jnp.int32)
    ints = [neighbours, orientation, bc_tags, coarse_group[:, None], place[:, None]]
    ints = jnp.concatenate(ints, axis=1)
    volume_t = jnp.transpose(volume_jac, (1, 2, 0, 3))
    flux_t, visc_t = (jnp.transpose(a, (2, 3, 0, 1)) for a in (face_flux, face_visc))

    pass_a = [(i, i ^ 1) for i in range(n_pass)]
    pass_b = [(i, (i + 1 if i % 2 else i - 1) % n_pass) for i in range(n_pass)]
    span_a = [(i, i ^ 1) for i in range(n_span)]
    span_b = [(i, (i + 1 if i % 2 else i - 1) % n_span) for i in range(n_span)]
    rad = [(0, 1), (1, 0)]

    def exchange(sends):
        ways = (
            ("radial", rad),
            ("passage", pass_b),
            ("span", span_a),
            ("span", span_b),
            ("passage", pass_a),
        )
        return [lax.ppermute(x, axis, way) for x, (axis, way) in zip(sends, ways)]

    def span_rows(row):
        return [row] + [
            lax.ppermute(row, "span", [(i, i ^ k) for i in range(n_span)]) for k in (2, 3, 1)
        ]

    vec = (RW, NODES)
    grow = (RW, GROWN)
    send = (STRIDE, 128)
    table_shape = (devices, 128)

    def half_floats(*shape):
        return jax.ShapeDtypeStruct(shape, jnp.bfloat16)

    table = pl.pallas_call(
        start_kernel,
        name="start",
        out_shape=jax.ShapeDtypeStruct(table_shape, F32),
        in_specs=[pl.BlockSpec(memory_space=pl.ANY)],
        out_specs=pl.BlockSpec(memory_space=VMEM),
        scratch_shapes=[VMEM(right_side.shape, F32), pltpu.SemaphoreType.DMA],
    )(right_side)
    table = lax.all_to_all(table, AXES, 0, 0, tiled=True)
    x, massw, member, odd, row = call(
        prepare_kernel,
        "prepare",
        (right_side, mass, ints, t["restrict"]),
        [vec, vec, (RW, WIDE), (3 * STRIDE, 128), (1, WIDE)],
        smem=(2,),
        raw=(0, 1, 3),
    )
    rows = span_rows(row)
    pair = half_floats(2 * RW, 6 * 4 * RW)
    rem0, rem1, rem2, loc1, loc2, omask, vmat, cinv3, turned = call(
        setup_kernel,
        "setup",
        (
            ints,
            volume_t,
            flux_t,
            visc_t,
            block_inverse,
            t["consts"],
            coarse_inverse,
        ),
        [
            pair,
            pair,
            half_floats(2 * RW, 6 * 2 * RW),
            pair,
            pair,
            (6 * RW, 8 * FACE),
            half_floats(RW, 18 * RW),
            half_floats(3 * KC, KC),
            half_floats(*block_inverse.shape),
        ],
        smem=(0,),
        raw=tuple(range(1, 7)),
        scratch=[(24, 104), (6 * RW, 256)],
    )
    remote = (rem0, rem1, rem2, omask, t["lay"])
    near = (massw, vmat, loc1, loc2, omask, t["lay"], t["slope"])

    def local_part(vector, grown, step):
        return call(local_kernel, "local%d" % step, (vector, grown) + near, [vec])[0]

    coarse_tables = (cinv3, member, t["lay"])
    tail = (turned, t["rise"])
    basis, search, images, scalars = [], [], [], []
    coarse0 = None
    outs = [vec, grow] + [send] * 5
    for step in range(3):
        if step < 2:
            (coarse,) = call(coarse_kernel, "coarse%d" % step, (*rows, *coarse_tables), [vec])
        if step == 0:
            z, coarse0, scal, first, grown, *sends = call(
                first0_kernel,
                "first0",
                (odd, table, x, coarse) + tail,
                [vec, vec, (8, 128)] + outs,
            )
            scalars.append(scal)
        elif step == 1:
            z, scal, first, grown, *sends = call(
                first1_kernel,
                "first1",
                (odd, table, images[0], coarse, basis[0], coarse0) + tail,
                [vec, (3 * STRIDE, 128)] + outs,
            )
            scalars.append(scal)
        else:
            z = images[1]
            (fine,) = call(blocks_kernel, "fine", (z, turned), [vec])
            first, grown, *sends = call(
                first2_kernel,
                "first2",
                (odd, *rows, fine, *coarse_tables, t["rise"]),
                outs,
            )
        basis.append(z)
        recv = exchange(sends)
        local = local_part(first, grown, step)
        direction, grown, *sends = call(
            with_step(second_kernel, step),
            "second%d" % step,
            (odd, z, first, local, *recv) + remote + tail,
            outs,
        )
        search.append(direction)
        recv = exchange(sends)
        local = local_part(direction, grown, step)
        kernel = with_step(third_kernel, step)
        args = (local, *recv) + remote
        if step == 0:
            image, table = call(kernel, "third0", args + (basis[0],), [vec, table_shape])
            table = lax.all_to_all(table, AXES, 0, 0, tiled=True)
            (row,) = call(row_kernel, "row0", (image, member, t["restrict"]), [(1, WIDE)])
            rows = span_rows(row)
        elif step == 1:
            image, row = call(kernel, "third1", args + (member, t["restrict"]), [vec, (1, WIDE)])
            rows = span_rows(row)
        else:
            image, table = call(kernel, "third2", args + tuple(basis), [vec, table_shape])
            table = lax.all_to_all(table, AXES, 0, 0, tiled=True)
        images.append(image)

    update, residual = call(
        final_kernel,
        "final",
        (table, *scalars, x, *search, *images),
        [right_side.shape] * 2,
    )
    return (update, residual)


def solution(mesh):
    rows = P(AXES, None)
    blocks = P(AXES, None, None)
    jac = P(AXES, None, None, None)
    in_specs = (
        rows,
        rows,
        jac,
        jac,
        jac,
        blocks,
        P("passage", "radial", None, None),
        rows,
        rows,
        rows,
        P(AXES),
    )
    return jax.shard_map(body, mesh=mesh, in_specs=in_specs, out_specs=(rows, rows), check_vma=False)
```
